256 devices in a mesh: dp: 16 (over x, y_lo, core), atom: 16 (over y_hi, z).
Axes of the slice: x: 4, y: 4 (y_hi: 2, y_lo: 2; y = y_hi * 2 + y_lo), z: 8, core: 2. Of those that a mesh axis runs over, the one named last changes fastest.
Arguments:
- node_feats: bfloat16 [16, 128, 2048], P('dp', None, 'atom'), may hold values from -6 to 6
- frac: float32 [16, 3, 2048], P('dp', None, 'atom'), may hold values from 0 to 1
- neighbours: int32 [16, 32, 2048], P('dp', None, 'atom'), may hold values from 0 to 2047, as said below
- images: int32 [16, 32, 2048], P('dp', None, 'atom'), may hold values from 0 to 26
- neighbour_count: int32 [16, 2048], P('dp', 'atom'), may hold values from 16 to 32, as said below
- atom_count: int32 [16], P('dp'), may hold values from 512 to 2048, as said below
- miller: int32 [3, 2048], replicated, may hold values from -6 to 6
- in_weight: bfloat16 [128, 128], replicated, may hold values from -0.5 to 0.5
- radial_weight: float32 [3, 8, 128], replicated, may hold values from -6 to 6
- out_weight: bfloat16 [384, 128], replicated, may hold values from -0.3125 to 0.3125
- filter_weight: float32 [2048, 128], replicated, may hold values from -6 to 6
- cotangent: bfloat16 [16, 128, 2048], P('dp', None, 'atom'), may hold values from -6 to 6
Outputs:
- updated: bfloat16 [16, 128, 2048], P('dp', None, 'atom')
- grad_filter: float32 [2048, 128], P('atom')
- grad_in: float32 [128, 128], replicated
- grad_out: float32 [384, 128], replicated
The draws below stay inside these ranges and needn't reach their ends.
Inputs may be any that keep to these rules, and one draw needn't show every extreme that they name: `neighbours`: the neighbour in any slot of atom g is (g + o) mod 2048 with 1 <= |o| <= 32. `neighbour_count`: atom 0 of every structure uses all 32 slots. Atoms 0 to atom_count - 1 are real, the rest are padding; some structure is full.
All inputs are finite; a program needn't handle non-finite values.
Results may differ from the reference program's by a relative error of at most 0.02.
Values may be sent and summed in bfloat16 or wider, within the bound.
No kernel may reach another device: no remote copies, remote signals or barrier semaphores. Data moves between devices by JAX's collectives and lax.ppermute only.
A program may use at most 128 MiB of HBM per device.

```python
import math
import jax
import jax.numpy as jnp
from jax import lax

C = 128
K = 2048
NB = 8
NEI = 32
GHOST = 32
ATOMS = 2048
STRUCTS = 16


def draw_neighbours(key, part):
    key = jax.random.fold_in(key, 11)
    key_mag, key_sign = jax.random.split(key)
    magnitude = jax.random.randint(key_mag, (STRUCTS, NEI, ATOMS), 1, GHOST + 1)
    direction = 2 * jax.random.randint(key_sign, (STRUCTS, NEI, ATOMS), 0, 2) - 1
    position = jnp.arange(ATOMS, dtype=jnp.int32)[None, None, :]
    return ((position + direction * magnitude) % ATOMS).astype(jnp.int32)


def draw_neighbour_count(key, part):
    key = jax.random.fold_in(key, 12)
    counts = jax.random.randint(key, (STRUCTS, ATOMS), NEI // 2, NEI + 1)
    return counts.at[:, 0].set(NEI).astype(jnp.int32)


def draw_atom_count(key, part):
    key = jax.random.fold_in(key, 13)
    key_count, key_full = jax.random.split(key)
    counts = jax.random.randint(key_count, (STRUCTS,), ATOMS // 4, ATOMS + 1)
    fullest = jax.random.randint(key_full, (), 0, STRUCTS)
    return counts.at[fullest].set(ATOMS).astype(jnp.int32)


def set_ends(drawn, own_key, low, largest):
    longest = drawn.shape.index(max(drawn.shape))
    spots = []
    for shift in (0, 1):
        where = [jax.random.randint(jax.random.fold_in(own_key, axis), (), 0, length) for axis, length in enumerate(drawn.shape)]
        where[longest] = (where[longest] + shift) % drawn.shape[longest]
        spots.append(tuple(where))
    return drawn.at[spots[0]].set(low).at[spots[1]].set(largest)


def block_scale(rng, extent, cuts, least, largest):
    def one(dim, parts):
        heights = jax.random.uniform(jax.random.fold_in(jax.random.fold_in(rng, 6), dim), (parts,), jnp.float32, least / len(cuts), largest / len(cuts))
        return jnp.repeat(jnp.exp(heights), extent[dim] // parts).reshape((-1,) + (1,) * (len(extent) - dim - 1))

    level = one(*cuts[0])
    for cut in cuts[1:]:
        level = level * one(*cut)
    return level


def noise(key, dims, spread, reach, cuts=(), kind=jnp.bfloat16):
    drawn = spread * jax.random.normal(key, dims, jnp.float32)
    if cuts:
        drawn = drawn * block_scale(key, dims, cuts, -0.22, 0.18)
    return jnp.clip(drawn, -reach, reach).astype(kind)


def setup_inputs(seed: int = 0) -> dict:
    seeds = jax.random.split(jax.random.key(seed), 13)
    node_feats = noise(seeds[0], (STRUCTS, C, ATOMS), 1.0, 6.0, ((0, 16), (2, 16)))
    frac = jnp.clip(1.0 * jax.random.uniform(seeds[1], (STRUCTS, 3, ATOMS), jnp.float32) ** block_scale(seeds[1], (STRUCTS, 3, ATOMS), ((0, 16), (2, 16)), -0.2, 0.2), 0.0, 1.0)
    neighbours = draw_neighbours(jax.random.fold_in(seeds[12], 71), 0)
    images = set_ends(jax.random.randint(seeds[3], (STRUCTS, NEI, ATOMS), 0, 27), jax.random.fold_in(seeds[3], 1), 0, 26).astype(jnp.int32)
    neighbour_count = draw_neighbour_count(jax.random.fold_in(seeds[12], 71), 0)
    atom_count = draw_atom_count(jax.random.fold_in(seeds[12], 71), 0)
    miller = set_ends(jax.random.randint(seeds[6], (3, K), -6, 7), jax.random.fold_in(seeds[6], 1), -6, 6).astype(jnp.int32)
    in_weight = noise(seeds[7], (C, C), C ** -0.5, 0.5)
    radial_weight = noise(seeds[8], (3, NB, C), 1.0, 6.0, (), jnp.float32)
    out_weight = noise(seeds[9], (3 * C, C), (3 * C) ** -0.5, 0.3125)
    filter_weight = noise(seeds[10], (K, C), 1.0, 6.0, (), jnp.float32)
    cotangent = noise(seeds[11], (STRUCTS, C, ATOMS), 1.0, 6.0, ((0, 16), (2, 16)))
    return dict(node_feats=node_feats, frac=frac, neighbours=neighbours, images=images, neighbour_count=neighbour_count, atom_count=atom_count, miller=miller, in_weight=in_weight, radial_weight=radial_weight, out_weight=out_weight, filter_weight=filter_weight, cotangent=cotangent)


two_pi = 2.0 * math.pi
maximum_degree = lax.Precision.HIGHEST
contract_last = (((1,), (1,)), ((), ()))
contract_first = (((0,), (0,)), ((), ()))

def harmonics(vector_feature):
    along_x, along_y, along_z = (vector_feature[0], vector_feature[1], vector_feature[2])
    square = along_x * along_x + along_y * along_y + along_z * along_z
    root_three = math.sqrt(3.0)
    root_fifteen = math.sqrt(15.0)
    root_five = math.sqrt(5.0)
    spherical_harmonic = jnp.stack([jnp.ones_like(along_x), root_three * along_x, root_three * along_y, root_three * along_z, root_fifteen * along_x * along_y, root_fifteen * along_y * along_z, 0.5 * root_five * (3.0 * along_z * along_z - square), root_fifteen * along_x * along_z, 0.5 * root_fifteen * (along_x * along_x - along_y * along_y)])
    return (spherical_harmonic, square)

def edge_terms(frac_own, frac_ext, slot_index, image_codes, radial_weight):
    others = jnp.take(frac_ext, slot_index, axis=1)
    shifts = jnp.stack([image_codes // 9, image_codes // 3 % 3, image_codes % 3]).astype(jnp.float32) - 1.0
    vector_feature = 0.5 * (others - frac_own[:, None, :] + shifts)
    spherical_harmonic, square = harmonics(vector_feature)
    length = jnp.sqrt(square)
    basis_count = radial_weight.shape[1]
    spacing = 1.75 / (basis_count - 1)
    centres = jnp.arange(basis_count, dtype=jnp.float32) * spacing
    gauss_basis = jnp.exp(-jnp.square((length[None] - centres[:, None, None]) / spacing))
    radial = jnp.einsum('lnc,nea->lcea', radial_weight, gauss_basis, precision=maximum_degree)
    return (spherical_harmonic, radial)

def edge_sum(spherical_harmonic, radial, weighted):
    edge_message = radial * weighted[None]
    scalar_part = jnp.einsum('ea,cea->ca', spherical_harmonic[0], edge_message[0], precision=maximum_degree)
    vector_component = jnp.einsum('osf,xsf->oxf', spherical_harmonic[1:4], edge_message[1], precision=maximum_degree)
    tensor_component = jnp.einsum('osf,xsf->oxf', spherical_harmonic[4:9], edge_message[2], precision=maximum_degree)
    return jnp.concatenate([scalar_part[None], vector_component, tensor_component], axis=0)

def spread_back(spherical_harmonic, radial, incoming_gradient):
    scalar_part = jnp.einsum('ea,ca->cea', spherical_harmonic[0], incoming_gradient[0], precision=maximum_degree)
    vector_component = jnp.einsum('ftl,fjl->jtl', spherical_harmonic[1:4], incoming_gradient[1:4], precision=maximum_degree)
    tensor_component = jnp.einsum('ftl,fjl->jtl', spherical_harmonic[4:9], incoming_gradient[4:9], precision=maximum_degree)
    return radial[0] * scalar_part + radial[1] * vector_component + radial[2] * tensor_component

def invariants(features):
    squared = features * features
    return jnp.concatenate([squared[0], squared[1] + squared[2] + squared[3], squared[4] + squared[5] + squared[6] + squared[7] + squared[8]], axis=0)

def widen_grad(inv_grad, features):
    channels = features.shape[1]
    repeated = jnp.concatenate([inv_grad[:channels][None]] + [inv_grad[channels:2 * channels][None]] * 3 + [inv_grad[2 * channels:][None]] * 5, axis=0)
    return 2.0 * features * repeated

def phases(miller, frac):
    factor = miller.astype(jnp.float32)
    argument = factor[0][:, None] * frac[0][None] + factor[1][:, None] * frac[1][None] + factor[2][:, None] * frac[2][None]
    angles = two_pi * argument
    return (jnp.cos(angles), jnp.sin(angles))

def spectrum(values, cos_table, sin_table):
    wide_values = values.astype(jnp.float32)
    real_part = lax.dot_general(wide_values, cos_table, contract_last, precision=maximum_degree)
    imag_part = lax.dot_general(wide_values, sin_table, contract_last, precision=maximum_degree)
    return (real_part, imag_part)

def project(real_coef, imag_coef, cos_table, sin_table):
    return jnp.dot(real_coef, cos_table, precision=maximum_degree) + jnp.dot(imag_coef, sin_table, precision=maximum_degree)

def one_structure(node_feats, frac, neighbours, images, neighbour_count, atom_count, cotangent, miller, in_weight, radial_weight, out_weight, filter_weight):
    channels, atom_slots = node_feats.shape
    kcount = miller.shape[1]
    slot_total = neighbours.shape[0]
    live = (jnp.arange(atom_slots, dtype=jnp.int32) < atom_count).astype(jnp.float32)
    hidden = (lax.dot_general(in_weight, node_feats, contract_first, preferred_element_type=jnp.float32) * live[None]).astype(jnp.bfloat16)
    hidden_float = hidden.astype(jnp.float32)
    slot_ids = jnp.arange(slot_total, dtype=jnp.int32)[:, None]
    edge_weight = (slot_ids < neighbour_count[None]).astype(jnp.float32) * live[None] * slot_total ** (-0.5)
    features = jnp.zeros((9, channels, atom_slots), jnp.float32)
    for offset in range(0, slot_total, 8):
        block_slots = neighbours[offset:offset + 8]
        spherical_harmonic, radial = edge_terms(frac, frac, block_slots, images[offset:offset + 8], radial_weight)
        weighted = jnp.take(hidden_float, block_slots, axis=1) * edge_weight[offset:offset + 8][None]
        features = features + edge_sum(spherical_harmonic, radial, weighted)
    inv_round = invariants(features).astype(jnp.bfloat16)
    local_out = lax.dot_general(out_weight, inv_round, contract_first, preferred_element_type=jnp.float32)
    cos_table, sin_table = phases(miller, frac)
    s_real, s_imag = spectrum(hidden, cos_table, sin_table)
    masked = cotangent * live.astype(jnp.bfloat16)[None]
    g_real, g_imag = spectrum(masked, cos_table, sin_table)
    scale = 1.0 / math.sqrt(kcount * atom_slots)
    filt_t = filter_weight.T
    ewald = project(scale * filt_t * s_real, scale * filt_t * s_imag, cos_table, sin_table)
    updated = ((node_feats.astype(jnp.float32) + local_out + ewald) * live[None]).astype(jnp.bfloat16)
    grad_filter = (scale * (s_real * g_real + s_imag * g_imag)).T
    inv_grad = jnp.dot(out_weight, masked, preferred_element_type=jnp.float32)
    incoming_gradient = widen_grad(inv_grad, features)
    grad_hidden = jnp.zeros((channels, atom_slots), jnp.float32)
    for offset in range(0, slot_total, 8):
        block_slots = neighbours[offset:offset + 8]
        spherical_harmonic, radial = edge_terms(frac, frac, block_slots, images[offset:offset + 8], radial_weight)
        pulled = spread_back(spherical_harmonic, radial, incoming_gradient) * edge_weight[offset:offset + 8][None]
        grad_hidden = grad_hidden.at[:, block_slots.reshape(-1)].add(pulled.reshape(channels, -1))
    grad_hidden = grad_hidden + project(scale * filt_t * g_real, scale * filt_t * g_imag, cos_table, sin_table)
    grad_hidden = grad_hidden * live[None]
    grad_in = lax.dot_general(node_feats.astype(jnp.float32), grad_hidden, contract_last, precision=maximum_degree)
    grad_out = lax.dot_general(inv_round, masked, contract_last, preferred_element_type=jnp.float32)
    return (updated, grad_filter, grad_in, grad_out)

def reference(node_feats, frac, neighbours, images, neighbour_count, atom_count, miller, in_weight, radial_weight, out_weight, filter_weight, cotangent):
    channels = node_feats.shape[1]
    kcount = miller.shape[1]

    def visit(carry, inputs):
        result = one_structure(*inputs, miller, in_weight, radial_weight, out_weight, filter_weight)
        return ((carry[0] + result[1], carry[1] + result[2], carry[2] + result[3]), result[0])
    start_sums = (jnp.zeros((kcount, channels), jnp.float32), jnp.zeros((channels, channels), jnp.float32), jnp.zeros((3 * channels, channels), jnp.float32))
    totals, updated = lax.scan(visit, start_sums, (node_feats, frac, neighbours, images, neighbour_count, atom_count, cotangent))
    return (updated, totals[0], totals[1], totals[2])
```

```python
import math

import jax
import jax.numpy as jnp
from jax import lax
from jax.experimental import pallas as pl
from jax.experimental.pallas import tpu as pltpu
from jax.sharding import PartitionSpec as P

F32 = jnp.float32
BF16 = jnp.bfloat16
I32 = jnp.int32

CH = 128
ROWS = 128
SLABS = 16
STRUCTS = 16
ATOMS = ROWS * SLABS
SLOTS = 32
EDGES = SLOTS * ROWS
GHOST = 32
KVEC = 2048
KSHARE = KVEC // SLABS
NB = 8
TOP = 6
SIDE = 2 * TOP + 1
PLANE = 176
HALF = (TOP + 1) * PLANE
FRAC_AT = CH
COT_AT = CH + 16
PAY = 2 * CH + 16

VMEM = pl.BlockSpec(memory_space=pltpu.VMEM)
SMEM = pl.BlockSpec(memory_space=pltpu.SMEM)

NN = (((1,), (0,)), ((), ()))
NT = (((1,), (1,)), ((), ()))
TN = (((0,), (0,)), ((), ()))


def dot(a, b, dims):
    return lax.dot_general(a, b, dims, preferred_element_type=F32)


def split(x):
    hi = x.astype(BF16)
    return hi, (x - hi.astype(F32)).astype(BF16)


def call(kernel, out, scratch, mib, flops, *args):
    smem = sum(1 for a in args if a.ndim == 1)
    specs = [SMEM if a.ndim == 1 else VMEM for a in args]
    del smem
    return pl.pallas_call(
        kernel,
        out_shape=out,
        in_specs=specs,
        out_specs=jax.tree.map(lambda _: VMEM, out),
        scratch_shapes=scratch,
        compiler_params=pltpu.CompilerParams(vmem_limit_bytes=mib * 2**20),
        cost_estimate=pl.CostEstimate(
            flops=flops, bytes_accessed=2**20, transcendentals=0
        ),
    )(*args)


def pack_kernel(place, feats, cot, frac, pay, pad):
    live = lax.broadcasted_iota(I32, (CH, ROWS), 1) < place[1]
    pay[0:CH] = jnp.where(live, feats[0].astype(F32), 0.0).astype(BF16)
    pay[COT_AT:PAY] = jnp.where(live, cot[0].astype(F32), 0.0).astype(BF16)
    pad[...] = jnp.zeros((8, ROWS), F32)
    pad[0:3, :] = frac[0]
    hi, lo = split(pad[...])
    pay[FRAC_AT:COT_AT] = jnp.concatenate(
        [hi.astype(F32), lo.astype(F32)], axis=0
    ).astype(BF16)


def joined_frac(block):
    wide = block.astype(F32)
    return wide[0:8] + wide[8:16]


ROOT3, ROOT5, ROOT15 = math.sqrt(3.0), math.sqrt(5.0), math.sqrt(15.0)
STEP = 1.75 / (NB - 1)
BAND = 16


def edge_kernel(
    place,
    own,
    left,
    right,
    neighbours,
    images,
    count,
    in_weight,
    radial_weight,
    out_weight,
    early,
    local,
    ext,
    hot,
    weights,
    basis,
    radial,
    moved,
    shape_w,
    length,
    feats9,
    up9,
    pulled,
    inv,
):
    first, live_here = place[0], place[1]
    lane = lax.broadcasted_iota(I32, (CH, ROWS), 1)
    ext[:, 0:ROWS] = own[0:CH]
    ext[:, ROWS : 2 * ROWS] = jnp.where(
        lane < GHOST, right[0:CH].astype(F32), left[0:CH].astype(F32)
    ).astype(BF16)
    hidden = dot(in_weight[...], ext[...], TN).astype(BF16)

    offset = (neighbours[0] - first) & (ATOMS - 1)
    column = jnp.where(offset < ROWS + GHOST, offset, offset - (ATOMS - 2 * ROWS))
    at = column & (ROWS - 1)
    in_slab = column < ROWS
    frac_own = joined_frac(own[FRAC_AT:COT_AT])
    frac_left = joined_frac(left[FRAC_AT:COT_AT])
    frac_right = joined_frac(right[FRAC_AT:COT_AT])
    lane8 = lax.broadcasted_iota(I32, (8, ROWS), 1)
    frac_far = jnp.where(lane8 < GHOST, frac_right, frac_left)

    code = images[0]
    ninth = (code * 57) >> 9
    third = (code * 171) >> 9
    shifts = (ninth, third - 3 * ninth, code - 3 * third)
    vector = []
    for d in range(3):
        near = jnp.broadcast_to(frac_own[d : d + 1], (SLOTS, ROWS))
        far = jnp.broadcast_to(frac_far[d : d + 1], (SLOTS, ROWS))
        other = jnp.where(
            in_slab,
            jnp.take_along_axis(near, at, axis=1),
            jnp.take_along_axis(far, at, axis=1),
        )
        vector.append(0.5 * (other - near + (shifts[d].astype(F32) - 1.0)))
    x, y, z = vector
    square = x * x + y * y + z * z
    slot = lax.broadcasted_iota(I32, (SLOTS, ROWS), 0)
    lane32 = lax.broadcasted_iota(I32, (SLOTS, ROWS), 1)
    used = (slot < count[...]) & (lane32 < live_here)
    weight = jnp.where(used, SLOTS**-0.5, 0.0)
    harmonics = (
        weight,
        weight * (ROOT3 * x),
        weight * (ROOT3 * y),
        weight * (ROOT3 * z),
        weight * (ROOT15 * x * y),
        weight * (ROOT15 * y * z),
        weight * (0.5 * ROOT5 * (3.0 * z * z - square)),
        weight * (ROOT15 * x * z),
        weight * (0.5 * ROOT15 * (x * x - y * y)),
    )
    for m in range(9):
        shape_w[m] = harmonics[m]
    length[...] = jnp.sqrt(square)

    rows256 = lax.broadcasted_iota(I32, (2 * ROWS, ROWS), 0)
    centre = lax.broadcasted_iota(I32, (NB, ROWS), 0).astype(F32) * STEP
    basis[24:32, :] = jnp.zeros((8, EDGES), F32)
    for e in range(SLOTS):
        here = slice(e * ROWS, (e + 1) * ROWS)
        hot[:, here] = jnp.where(rows256 == column[e : e + 1], 1.0, 0.0).astype(BF16)
        gap = (length[e : e + 1, :] - centre) * (1.0 / STEP)
        gauss = jnp.exp(-(gap * gap))
        hi, lo = split(gauss)
        basis[0:8, here] = hi.astype(F32)
        basis[8:16, here] = lo.astype(F32)
        basis[16:24, here] = hi.astype(F32)
    weights[...] = jnp.zeros((32, 3 * CH), F32)
    for l in range(3):
        hi, lo = split(radial_weight[l])
        part = slice(l * CH, (l + 1) * CH)
        weights[0:8, part] = hi.astype(F32)
        weights[8:16, part] = hi.astype(F32)
        weights[16:24, part] = lo.astype(F32)
    radial[...] = dot(weights[...].astype(BF16), basis[...].astype(BF16), TN)
    moved[...] = dot(hidden, hot[...], NN)

    def forward(step, carry):
        top = pl.multiple_of(step * BAND, BAND)
        total = [jnp.zeros((BAND, ROWS), F32) for _ in range(9)]
        for e in range(SLOTS):
            here = slice(e * ROWS, (e + 1) * ROWS)
            value = moved[pl.ds(top, BAND), here]
            parts = [
                radial[pl.ds(pl.multiple_of(l * CH + top, BAND), BAND), here] * value
                for l in range(3)
            ]
            for m in range(9):
                l = 0 if m == 0 else (1 if m < 4 else 2)
                total[m] = total[m] + shape_w[m, e : e + 1, :] * parts[l]
        for m in range(9):
            feats9[m, pl.ds(top, BAND), :] = total[m]
        squares = [t * t for t in total]
        inv[pl.ds(top, BAND), :] = squares[0].astype(BF16)
        inv[pl.ds(pl.multiple_of(CH + top, BAND), BAND), :] = (
            squares[1] + squares[2] + squares[3]
        ).astype(BF16)
        inv[pl.ds(pl.multiple_of(2 * CH + top, BAND), BAND), :] = (
            squares[4] + squares[5] + squares[6] + squares[7] + squares[8]
        ).astype(BF16)
        return carry

    lax.fori_loop(0, CH // BAND, forward, 0)

    masked = own[COT_AT:PAY]
    local[...] = dot(out_weight[...], inv[...], TN)
    up9[...] = 2.0 * dot(out_weight[...], masked, NN)
    early[CH : 4 * CH, :] = dot(inv[...], masked, NT)

    def backward(step, carry):
        top = pl.multiple_of(step * BAND, BAND)
        up = [
            up9[pl.ds(pl.multiple_of(l * CH + top, BAND), BAND), :] for l in range(3)
        ]
        upstream = []
        for m in range(9):
            l = 0 if m == 0 else (1 if m < 4 else 2)
            upstream.append(feats9[m, pl.ds(top, BAND), :] * up[l])
        for e in range(SLOTS):
            here = slice(e * ROWS, (e + 1) * ROWS)
            term = [shape_w[m, e : e + 1, :] * upstream[m] for m in range(9)]
            pull = (
                radial[pl.ds(top, BAND), here] * term[0]
                + radial[pl.ds(pl.multiple_of(CH + top, BAND), BAND), here]
                * (term[1] + term[2] + term[3])
                + radial[pl.ds(pl.multiple_of(2 * CH + top, BAND), BAND), here]
                * (term[4] + term[5] + term[6] + term[7] + term[8])
            )
            pulled[pl.ds(top, BAND), here] = pull.astype(BF16)
        return carry

    lax.fori_loop(0, CH // BAND, backward, 0)
    back = dot(pulled[...], hot[...], NT)
    early[0:CH, :] = dot(ext[...], back.astype(BF16), NT)


def half_row(miller):
    m0, m1, m2 = miller[0:1], miller[1:2], miller[2:3]
    sign = jnp.where(m0 < 0, -1, 1)
    return (sign * m0) * PLANE + (sign * m1 + TOP) * SIDE + (sign * m2 + TOP)


def turns(frac_row, first, count):
    width = frac_row.shape[1]
    m = (lax.broadcasted_iota(I32, (count, width), 0) + first).astype(F32)
    turn = m * frac_row
    turn = turn - jnp.floor(turn + 0.5)
    quarter = jnp.floor(turn * 4.0 + 0.5)
    arc = (turn - 0.25 * quarter) * (2.0 * math.pi)
    s2 = arc * arc
    sine = arc * (1.0 + s2 * (-1 / 6 + s2 * (1 / 120 + s2 * (-1 / 5040))))
    cosine = 1.0 + s2 * (-0.5 + s2 * (1 / 24 + s2 * (-1 / 720 + s2 * (1 / 40320))))
    odd = jnp.abs(quarter) == 1.0
    back = jnp.abs(quarter) == 2.0
    flip = jnp.where(quarter < 0.0, -1.0, 1.0)
    cos_out = jnp.where(odd, -flip * sine, jnp.where(back, -cosine, cosine))
    sin_out = jnp.where(odd, flip * cosine, jnp.where(back, -sine, sine))
    return cos_out, sin_out


def plane_tables(frac, cos_plane, sin_plane):
    c1, s1 = turns(frac[1:2], -TOP, 16)
    c2, s2 = turns(frac[2:3], -TOP, 16)
    for a in range(SIDE):
        ca, sa = c1[a : a + 1], s1[a : a + 1]
        rows = slice(a * SIDE, a * SIDE + 16 if a < SIDE - 1 else PLANE)
        many = 16 if a < SIDE - 1 else PLANE - a * SIDE
        if many <= 16:
            cos_plane[rows, :] = (ca * c2 - sa * s2)[0:many]
            sin_plane[rows, :] = (sa * c2 + ca * s2)[0:many]
        else:
            cos_plane[a * SIDE : a * SIDE + 16, :] = ca * c2 - sa * s2
            sin_plane[a * SIDE : a * SIDE + 16, :] = sa * c2 + ca * s2
            cos_plane[a * SIDE + 16 : PLANE, :] = jnp.zeros(
                (many - 16, ca.shape[1]), F32
            )
            sin_plane[a * SIDE + 16 : PLANE, :] = jnp.zeros(
                (many - 16, ca.shape[1]), F32
            )
    return turns(frac[0:1], 0, 8)


def lattice_kernel(miller, filter_weight, frac, folded, table, hot, cos_p, sin_p, pad):
    row = half_row(miller[...])
    hi, lo = split(filter_weight[...] * (1.0 / math.sqrt(KVEC * ATOMS)))
    point = lax.broadcasted_iota(I32, (HALF, 256), 0)
    for k in range(KVEC // 256):
        here = slice(k * 256, (k + 1) * 256)
        hot[:, here] = jnp.where(point == row[:, here], 1.0, 0.0).astype(BF16)
    both = dot(hot[...], jnp.concatenate([hi, lo], axis=1), NN)
    folded[...] = both[:, 0:CH] + both[:, CH : 2 * CH]
    pad[...] = jnp.zeros((8, ROWS), F32)
    pad[0:3, :] = frac[0]
    c0, s0 = plane_tables(pad[...], cos_p, sin_p)
    for m in range(TOP + 1):
        cm, sm = c0[m : m + 1], s0[m : m + 1]
        here = slice(m * PLANE, (m + 1) * PLANE)
        there = slice(HALF + m * PLANE, HALF + (m + 1) * PLANE)
        table[here, :] = (cm * cos_p[...] - sm * sin_p[...]).astype(BF16)
        table[there, :] = (sm * cos_p[...] + cm * sin_p[...]).astype(BF16)


def ewald_kernel(
    place,
    gathered,
    folded,
    table_own,
    miller_own,
    in_weight,
    feats,
    local,
    updated,
    parts,
    frac,
    values,
    cos_p,
    sin_p,
    table,
    factor,
    coef,
):
    for p in range(SLABS):
        here = slice(p * ROWS, (p + 1) * ROWS)
        values[0:CH, here] = gathered[p, 0:CH]
        values[CH : 2 * CH, here] = gathered[p, COT_AT:PAY]
        frac[:, here] = joined_frac(gathered[p, FRAC_AT:COT_AT])
    c0, s0 = plane_tables(frac[...], cos_p, sin_p)
    for m in range(TOP + 1):
        cm, sm = c0[m : m + 1], s0[m : m + 1]
        here = slice(m * PLANE, (m + 1) * PLANE)
        there = slice(HALF + m * PLANE, HALF + (m + 1) * PLANE)
        table[here, :] = (cm * cos_p[...] - sm * sin_p[...]).astype(BF16)
        table[there, :] = (sm * cos_p[...] + cm * sin_p[...]).astype(BF16)
    factor[...] = dot(table[...], values[...], NT)

    point = lax.broadcasted_iota(I32, (HALF, KSHARE), 0)
    hot = jnp.where(point == half_row(miller_own[...]), 1.0, 0.0).astype(BF16)
    feats_hi, feats_lo = split(factor[:, 0:CH])
    stacked = jnp.concatenate([in_weight[...], in_weight[...]], axis=0)
    s = dot(jnp.concatenate([feats_hi, feats_lo], axis=1), stacked, NN)
    g = factor[:, CH : 2 * CH]
    for k in range(2):
        here = slice(k * HALF, (k + 1) * HALF)
        coef[here, 0:CH] = (folded[...] * s[here]).astype(BF16)
        coef[here, CH : 2 * CH] = (folded[...] * g[here]).astype(BF16)
    scale = 1.0 / math.sqrt(KVEC * ATOMS)
    pair = scale * (s[0:HALF] * g[0:HALF] + s[HALF:] * g[HALF:])
    pair_hi, pair_lo = split(pair)
    both = dot(hot, jnp.concatenate([pair_hi, pair_lo], axis=1), TN)
    grad_filter = both[:, 0:CH] + both[:, CH : 2 * CH]
    ewald = dot(coef[:, 0:CH], table_own[...], TN)
    grad_in = dot(feats_hi, coef[:, CH : 2 * CH], TN)
    for d in range(STRUCTS):
        parts[d, 0:8, :] = grad_in[8 * d : 8 * d + 8]
        parts[d, 8:16, :] = grad_filter[8 * d : 8 * d + 8]
    live = lax.broadcasted_iota(I32, (CH, ROWS), 1) < place[1]
    updated[0] = jnp.where(
        live, feats[0].astype(F32) + local[...] + ewald, 0.0
    ).astype(BF16)


def exchange(x, axis):
    return lax.all_to_all(x, axis, 0, 0)


def to_all(x, axis, count):
    return exchange(jnp.broadcast_to(x[None], (count,) + x.shape), axis)


def shards(
    node_feats,
    frac,
    neighbours,
    images,
    neighbour_count,
    atom_count,
    miller,
    in_weight,
    radial_weight,
    out_weight,
    filter_weight,
    cotangent,
):
    slab = lax.axis_index("atom")
    first = slab * ROWS
    place = jnp.stack([first, atom_count[0] - first]).astype(I32)
    struct = jax.ShapeDtypeStruct

    pay = call(
        pack_kernel,
        struct((PAY, ROWS), BF16),
        [pltpu.VMEM((8, ROWS), F32)],
        16,
        10**6,
        place,
        node_feats,
        cotangent,
        frac,
    )
    halo = pay[0:COT_AT]
    ring = range(SLABS)
    left = lax.ppermute(halo, "atom", [(i, (i + 1) % SLABS) for i in ring])
    right = lax.ppermute(halo, "atom", [((i + 1) % SLABS, i) for i in ring])
    gathered = to_all(pay, "atom", SLABS)

    folded, table_own = call(
        lattice_kernel,
        (struct((HALF, CH), F32), struct((2 * HALF, ROWS), BF16)),
        [
            pltpu.VMEM((HALF, KVEC), BF16),
            pltpu.VMEM((PLANE, ROWS), F32),
            pltpu.VMEM((PLANE, ROWS), F32),
            pltpu.VMEM((8, ROWS), F32),
        ],
        40,
        3 * 10**9,
        miller,
        filter_weight,
        frac,
    )
    early, local = call(
        edge_kernel,
        (struct((4 * CH, CH), F32), struct((CH, ROWS), F32)),
        [
            pltpu.VMEM((CH, 2 * ROWS), BF16),
            pltpu.VMEM((2 * ROWS, EDGES), BF16),
            pltpu.VMEM((32, 3 * CH), F32),
            pltpu.VMEM((32, EDGES), F32),
            pltpu.VMEM((3 * CH, EDGES), F32),
            pltpu.VMEM((CH, EDGES), F32),
            pltpu.VMEM((9, SLOTS, ROWS), F32),
            pltpu.VMEM((SLOTS, ROWS), F32),
            pltpu.VMEM((9, CH, ROWS), F32),
            pltpu.VMEM((3 * CH, ROWS), F32),
            pltpu.VMEM((CH, EDGES), BF16),
            pltpu.VMEM((3 * CH, ROWS), BF16),
        ],
        40,
        3 * 10**9,
        place,
        pay,
        left,
        right,
        neighbours,
        images,
        neighbour_count,
        in_weight,
        radial_weight,
        out_weight,
    )
    chunk = exchange(early.reshape(STRUCTS, SLOTS, CH), "dp").sum(axis=0)
    chunk = to_all(chunk.astype(BF16), "atom", SLABS).astype(F32).sum(axis=0)

    miller_own = lax.dynamic_slice_in_dim(miller, slab * KSHARE, KSHARE, 1)
    updated, parts = call(
        ewald_kernel,
        (struct((1, CH, ROWS), BF16), struct((STRUCTS, 16, CH), F32)),
        [
            pltpu.VMEM((8, ATOMS), F32),
            pltpu.VMEM((2 * CH, ATOMS), BF16),
            pltpu.VMEM((PLANE, ATOMS), F32),
            pltpu.VMEM((PLANE, ATOMS), F32),
            pltpu.VMEM((2 * HALF, ATOMS), BF16),
            pltpu.VMEM((2 * HALF, 2 * CH), F32),
            pltpu.VMEM((2 * HALF, 2 * CH), BF16),
        ],
        48,
        10**10,
        place,
        gathered,
        folded,
        table_own,
        miller_own,
        in_weight,
        node_feats,
        local,
    )
    late = exchange(parts, "dp").sum(axis=0)
    last = jnp.concatenate([late, chunk], axis=0).astype(BF16)
    sums = to_all(last, "dp", STRUCTS).astype(F32)
    grad_early = sums[:, 16:].reshape(4 * CH, CH)
    grad_in = sums[:, 0:8].reshape(CH, CH) + grad_early[0:CH]
    grad_filter = sums[:, 8:16].reshape(KSHARE, CH)
    return (updated, grad_filter, grad_in, grad_early[CH:])


def solution(mesh):
    return jax.shard_map(
        shards,
        mesh=mesh,
        in_specs=(
            P("dp", None, "atom"),
            P("dp", None, "atom"),
            P("dp", None, "atom"),
            P("dp", None, "atom"),
            P("dp", "atom"),
            P("dp"),
            P(),
            P(),
            P(),
            P(),
            P(),
            P("dp", None, "atom"),
        ),
        out_specs=(P("dp", None, "atom"), P("atom", None), P(), P()),
        check_vma=False,
    )
```

```python
import math

import jax
import jax.numpy as jnp
from jax import lax
from jax.experimental import pallas as pl
from jax.experimental.pallas import tpu as pltpu
from jax.sharding import PartitionSpec as P

F32 = jnp.float32
BF16 = jnp.bfloat16
I32 = jnp.int32

CH = 128
ROWS = 128
SLABS = 16
STRUCTS = 16
ATOMS = ROWS * SLABS
SLOTS = 32
EDGES = SLOTS * ROWS
GHOST = 32
KVEC = 2048
KSHARE = KVEC // SLABS
NB = 8
TOP = 6
SIDE = 2 * TOP + 1
PLANE = 128
HALF = (TOP + 1) * PLANE
WAVES = SIDE
BASIS = WAVES * 2 * PLANE
TILE = 256
MINE = CH // SLABS
FRAC_AT = CH
COT_AT = CH + 16
PAY = COT_AT + 16

VMEM = pl.BlockSpec(memory_space=pltpu.VMEM)
SMEM = pl.BlockSpec(memory_space=pltpu.SMEM)
HBM = pl.BlockSpec(memory_space=pltpu.HBM)

NN = (((1,), (0,)), ((), ()))
NT = (((1,), (1,)), ((), ()))
TN = (((0,), (0,)), ((), ()))


def dot(a, b, dims):
    return lax.dot_general(a, b, dims, preferred_element_type=F32)


def split(x):
    hi = x.astype(BF16)
    return hi, (x - hi.astype(F32)).astype(BF16)


def call(kernel, outs, scratch, mib, flops, *args):
    return pl.pallas_call(
        kernel,
        out_shape=[shape for _, shape in outs],
        in_specs=[spec for spec, _ in args],
        out_specs=[spec for spec, _ in outs],
        scratch_shapes=scratch,
        compiler_params=pltpu.CompilerParams(vmem_limit_bytes=mib * 2**20),
        cost_estimate=pl.CostEstimate(
            flops=flops, bytes_accessed=2**16, transcendentals=0
        ),
    )(*[arg for _, arg in args])


def fetch(pairs, sems):
    copies = [
        pltpu.make_async_copy(src, dst, sems.at[n]) for n, (src, dst) in enumerate(pairs)
    ]
    for copy in copies:
        copy.start()
    return copies


def coordinates(frac):
    rows = jnp.pad(frac, ((0, 5), (0, 0)))
    first = jnp.floor(rows * 256.0) * (1.0 / 256.0)
    return jnp.concatenate([first, rows - first], axis=0).astype(BF16)


def joined_frac(block):
    wide = block.astype(F32)
    return wide[0:8] + wide[8:16]


ROOT3, ROOT5, ROOT15 = math.sqrt(3.0), math.sqrt(5.0), math.sqrt(15.0)
STEP = 1.75 / (NB - 1)
BAND = 16
EDGE_COST = 10**10


def edge_kernel(
    place,
    own,
    left,
    right,
    neighbours_hbm,
    images_hbm,
    count_hbm,
    in_weight_hbm,
    radial_weight_hbm,
    out_weight_hbm,
    cot_hbm,
    early,
    local,
    neighbours,
    images,
    count,
    in_weight,
    radial_weight,
    out_weight,
    cot,
    ext,
    hot,
    weights,
    basis,
    radial,
    moved,
    shape_w,
    length,
    feats9,
    up9,
    pulled,
    inv,
    sems,
):
    copies = fetch(
        (
            (neighbours_hbm, neighbours),
            (images_hbm, images),
            (count_hbm, count),
            (in_weight_hbm, in_weight),
            (radial_weight_hbm, radial_weight),
            (out_weight_hbm, out_weight),
            (cot_hbm, cot),
        ),
        sems,
    )
    for copy in copies:
        copy.wait()
    first, live_here, live_left, live_right = place[0], place[1], place[2], place[3]
    lane = lax.broadcasted_iota(I32, (CH, ROWS), 1)
    ext[:, 0:ROWS] = jnp.where(lane < live_here, own[0:CH].astype(F32), 0.0).astype(BF16)
    near_right = jnp.where(lane < live_right, right[0:CH].astype(F32), 0.0)
    near_left = jnp.where(lane < live_left, left[0:CH].astype(F32), 0.0)
    ext[:, ROWS : 2 * ROWS] = jnp.where(lane < GHOST, near_right, near_left).astype(BF16)
    hidden = dot(in_weight[...], ext[...], TN).astype(BF16)

    offset = (neighbours[0] - first) & (ATOMS - 1)
    column = jnp.where(offset < ROWS + GHOST, offset, offset - (ATOMS - 2 * ROWS))
    at = column & (ROWS - 1)
    in_slab = column < ROWS
    frac_own = joined_frac(own[FRAC_AT:COT_AT])
    frac_left = joined_frac(left[FRAC_AT:COT_AT])
    frac_right = joined_frac(right[FRAC_AT:COT_AT])
    lane8 = lax.broadcasted_iota(I32, (8, ROWS), 1)
    frac_far = jnp.where(lane8 < GHOST, frac_right, frac_left)

    code = images[0]
    ninth = (code * 57) >> 9
    third = (code * 171) >> 9
    shifts = (ninth, third - 3 * ninth, code - 3 * third)
    vector = []
    for d in range(3):
        near = jnp.broadcast_to(frac_own[d : d + 1], (SLOTS, ROWS))
        far = jnp.broadcast_to(frac_far[d : d + 1], (SLOTS, ROWS))
        other = jnp.where(
            in_slab,
            jnp.take_along_axis(near, at, axis=1),
            jnp.take_along_axis(far, at, axis=1),
        )
        vector.append(0.5 * (other - near + (shifts[d].astype(F32) - 1.0)))
    x, y, z = vector
    square = x * x + y * y + z * z
    slot = lax.broadcasted_iota(I32, (SLOTS, ROWS), 0)
    lane32 = lax.broadcasted_iota(I32, (SLOTS, ROWS), 1)
    used = (slot < count[...]) & (lane32 < live_here)
    weight = jnp.where(used, SLOTS**-0.5, 0.0)
    harmonics = (
        weight,
        weight * (ROOT3 * x),
        weight * (ROOT3 * y),
        weight * (ROOT3 * z),
        weight * (ROOT15 * x * y),
        weight * (ROOT15 * y * z),
        weight * (0.5 * ROOT5 * (3.0 * z * z - square)),
        weight * (ROOT15 * x * z),
        weight * (0.5 * ROOT15 * (x * x - y * y)),
    )
    for m in range(9):
        shape_w[m] = harmonics[m]
    length[...] = jnp.sqrt(square)

    rows256 = lax.broadcasted_iota(I32, (2 * ROWS, ROWS), 0)
    centre = lax.broadcasted_iota(I32, (NB, ROWS), 0).astype(F32) * STEP
    basis[24:32, :] = jnp.zeros((8, EDGES), F32)
    for e in range(SLOTS):
        here = slice(e * ROWS, (e + 1) * ROWS)
        hot[:, here] = jnp.where(rows256 == column[e : e + 1], 1.0, 0.0).astype(BF16)
        gap = (length[e : e + 1, :] - centre) * (1.0 / STEP)
        gauss = jnp.exp(-(gap * gap))
        hi, lo = split(gauss)
        basis[0:8, here] = hi.astype(F32)
        basis[8:16, here] = lo.astype(F32)
        basis[16:24, here] = hi.astype(F32)
    weights[...] = jnp.zeros((32, 3 * CH), F32)
    for l in range(3):
        hi, lo = split(radial_weight[l])
        part = slice(l * CH, (l + 1) * CH)
        weights[0:8, part] = hi.astype(F32)
        weights[8:16, part] = hi.astype(F32)
        weights[16:24, part] = lo.astype(F32)
    radial[...] = dot(weights[...].astype(BF16), basis[...].astype(BF16), TN)
    moved[...] = dot(hidden, hot[...], NN)

    def forward(step, carry):
        top = pl.multiple_of(step * BAND, BAND)
        total = [jnp.zeros((BAND, ROWS), F32) for _ in range(9)]
        for e in range(SLOTS):
            here = slice(e * ROWS, (e + 1) * ROWS)
            value = moved[pl.ds(top, BAND), here]
            parts = [
                radial[pl.ds(pl.multiple_of(l * CH + top, BAND), BAND), here] * value
                for l in range(3)
            ]
            for m in range(9):
                l = 0 if m == 0 else (1 if m < 4 else 2)
                total[m] = total[m] + shape_w[m, e : e + 1, :] * parts[l]
        for m in range(9):
            feats9[m, pl.ds(top, BAND), :] = total[m]
        squares = [t * t for t in total]
        inv[pl.ds(top, BAND), :] = squares[0].astype(BF16)
        inv[pl.ds(pl.multiple_of(CH + top, BAND), BAND), :] = (
            squares[1] + squares[2] + squares[3]
        ).astype(BF16)
        inv[pl.ds(pl.multiple_of(2 * CH + top, BAND), BAND), :] = (
            squares[4] + squares[5] + squares[6] + squares[7] + squares[8]
        ).astype(BF16)
        return carry

    lax.fori_loop(0, CH // BAND, forward, 0)

    masked = jnp.where(lane < live_here, cot[0].astype(F32), 0.0).astype(BF16)
    local[...] = dot(out_weight[...], inv[...], TN)
    up9[...] = 2.0 * dot(out_weight[...], masked, NN)
    grad_out = dot(inv[...], masked, NT)
    for d in range(4, STRUCTS):
        to = d * SLOTS
        early[to : to + SLOTS, :] = grad_out[(d - 4) * SLOTS : (d - 3) * SLOTS]

    def backward(step, carry):
        top = pl.multiple_of(step * BAND, BAND)
        up = [
            up9[pl.ds(pl.multiple_of(l * CH + top, BAND), BAND), :] for l in range(3)
        ]
        upstream = []
        for m in range(9):
            l = 0 if m == 0 else (1 if m < 4 else 2)
            upstream.append(feats9[m, pl.ds(top, BAND), :] * up[l])
        for e in range(SLOTS):
            here = slice(e * ROWS, (e + 1) * ROWS)
            term = [shape_w[m, e : e + 1, :] * upstream[m] for m in range(9)]
            pull = (
                radial[pl.ds(top, BAND), here] * term[0]
                + radial[pl.ds(pl.multiple_of(CH + top, BAND), BAND), here]
                * (term[1] + term[2] + term[3])
                + radial[pl.ds(pl.multiple_of(2 * CH + top, BAND), BAND), here]
                * (term[4] + term[5] + term[6] + term[7] + term[8])
            )
            pulled[pl.ds(top, BAND), here] = pull.astype(BF16)
        return carry

    lax.fori_loop(0, CH // BAND, backward, 0)
    back = dot(pulled[...], hot[...], NT)
    grad_in = dot(ext[...], back.astype(BF16), NT)
    for d in range(4):
        to = d * SLOTS
        early[to : to + SLOTS, :] = grad_in[d * SLOTS : (d + 1) * SLOTS]


def half_row(miller):
    m0, m1, m2 = miller[0:1], miller[1:2], miller[2:3]
    sign = jnp.where(m0 < 0, -1, 1)
    m0, m1, m2 = sign * m0, sign * m1, sign * m2
    minus = m1 < 0
    turn = jnp.where(minus, -1, 1)
    row = m0 * PLANE + turn * m1 * SIDE + (turn * m2 + TOP)
    return row + jnp.where(minus, HALF, 0)


def turns(frac_row, first, count):
    width = frac_row.shape[1]
    m = (lax.broadcasted_iota(I32, (count, width), 0) + first).astype(F32)
    turn = m * frac_row
    turn = turn - jnp.floor(turn + 0.5)
    quarter = jnp.floor(turn * 4.0 + 0.5)
    arc = (turn - 0.25 * quarter) * (2.0 * math.pi)
    s2 = arc * arc
    sine = arc * (1.0 + s2 * (-1 / 6 + s2 * (1 / 120 + s2 * (-1 / 5040))))
    cosine = 1.0 + s2 * (-0.5 + s2 * (1 / 24 + s2 * (-1 / 720 + s2 * (1 / 40320))))
    odd = jnp.abs(quarter) == 1.0
    back = jnp.abs(quarter) == 2.0
    flip = jnp.where(quarter < 0.0, -1.0, 1.0)
    cos_out = jnp.where(odd, -flip * sine, jnp.where(back, -cosine, cosine))
    sin_out = jnp.where(odd, flip * cosine, jnp.where(back, -sine, sine))
    return cos_out, sin_out


def waves(frac, plane):
    width = plane.shape[1]
    c1, s1 = turns(frac[1:2], 0, 8)
    c2, s2 = turns(frac[2:3], -TOP, 16)
    for k in (0, PLANE):
        plane[k + 88 : k + PLANE, :] = jnp.zeros((PLANE - 88, width), F32)
    for m in range(TOP + 1):
        cm, sm = c1[m : m + 1], s1[m : m + 1]
        plane[m * SIDE : m * SIDE + 16, :] = cm * c2 - sm * s2
        plane[PLANE + m * SIDE : PLANE + m * SIDE + 16, :] = sm * c2 + cm * s2
    c0, s0 = turns(frac[0:1], 0, 8)
    return [c0[m : m + 1] for m in range(TOP + 1)] + [
        s0[m : m + 1] for m in range(1, TOP + 1)
    ]


def one_hot(miller, hot):
    row = half_row(miller[...])
    point = lax.broadcasted_iota(I32, (2 * HALF, TILE), 0)
    for k in range(KVEC // TILE):
        here = slice(k * TILE, (k + 1) * TILE)
        hot[:, here] = jnp.where(point == row[:, here], 1.0, 0.0).astype(BF16)


def lattice_kernel(miller, filter_weight, frac, folded, table, hot, plane, pad):
    one_hot(miller, hot)
    hi, lo = split(filter_weight[...] * (1.0 / math.sqrt(KVEC * ATOMS)))
    both = dot(hot[...], jnp.concatenate([hi, lo], axis=1), NN)
    both = both[:, 0:CH] + both[:, CH : 2 * CH]
    folded[0:CH, :] = (both[0:HALF] + both[HALF : 2 * HALF]).T
    folded[CH : 2 * CH, :] = (both[0:HALF] - both[HALF : 2 * HALF]).T
    pad[...] = jnp.zeros((8, ROWS), F32)
    for d in range(3):
        pad[d : d + 1, :] = frac[d]
    for f, wave in enumerate(waves(pad[...], plane)):
        here = slice(f * 2 * PLANE, (f + 1) * 2 * PLANE)
        table[here, :] = (wave * plane[...]).astype(BF16)


def blocks(x, m):
    at = 2 * m * PLANE
    cc, cs = x[:, at : at + PLANE], x[:, at + PLANE : at + 2 * PLANE]
    if m == 0:
        return cc, None, None, cs
    at = 2 * (TOP + m) * PLANE
    sc, ss = x[:, at : at + PLANE], x[:, at + PLANE : at + 2 * PLANE]
    return cc, ss, sc, cs


def filtered(plus, minus, x):
    first, second = [], []
    for m in range(TOP + 1):
        here = slice(m * PLANE, (m + 1) * PLANE)
        p, d = plus[:, here], minus[:, here]
        cc, ss, sc, cs = blocks(x, m)
        if m == 0:
            first += [p * cc, p * cs]
        else:
            first += [p * cc - d * ss, p * cs + d * sc]
            second += [p * sc + d * cs, p * ss - d * cc]
    return first + second


def spectrum_kernel(
    place,
    gathered,
    folded,
    miller,
    own_weight,
    early,
    parts,
    factor,
    hot,
    frac,
    values,
    plane,
    wide,
):
    for p in range(SLABS):
        here = slice(p * ROWS, (p + 1) * ROWS)
        values[0:CH, here] = gathered[p, 0:CH]
        values[CH : CH + 16, here] = gathered[p, COT_AT:PAY]
        frac[:, here] = joined_frac(gathered[p, FRAC_AT:COT_AT])
    rows = CH + 16
    along = waves(frac[...], plane)
    live = (lax.broadcasted_iota(I32, (1, ATOMS), 1) < place[0] + place[1]).astype(F32)
    around = plane[...].astype(BF16)
    for low, high in ((0, TOP + 1), (TOP + 1, WAVES)):
        for f in range(low, high):
            wide[f * rows : (f + 1) * rows, :] = (
                values[...].astype(F32) * (along[f] * live)
            ).astype(BF16)
        both = dot(wide[low * rows : high * rows, :], around, NT)
        for f in range(low, high):
            here = slice(f * 2 * PLANE, (f + 1) * 2 * PLANE)
            factor[:, here] = both[(f - low) * rows : (f - low + 1) * rows]
        if low == 0:
            one_hot(miller, hot)

    top = pl.multiple_of(place[4], MINE)
    feats_hi, feats_lo = split(factor[0:CH, :])
    s = dot(own_weight[...], jnp.concatenate([feats_hi, feats_lo], axis=0), NN)[0:MINE]
    g = factor[CH : CH + MINE, :]
    plus = folded[pl.ds(top, MINE), :]
    minus = folded[pl.ds(pl.multiple_of(CH + top, MINE), MINE), :]
    grad = split(jnp.concatenate(filtered(plus, minus, g), axis=1))
    grad_in = dot(jnp.concatenate(grad, axis=0), feats_hi, NT)
    grad_in = grad_in[0:MINE] + grad_in[MINE : 2 * MINE]
    pair_plus, pair_minus = [], []
    for m in range(TOP + 1):
        cc, ss, sc, cs = blocks(s, m)
        gcc, gss, gsc, gcs = blocks(g, m)
        even, odd = cc * gcc + cs * gcs, 0.0
        if m > 0:
            even = even + ss * gss + sc * gsc
            odd = sc * gcs + cs * gsc - cc * gss - ss * gcc
        pair_plus.append(even + odd)
        pair_minus.append(even - odd)
    pair = jnp.concatenate(pair_plus + pair_minus, axis=1)
    pair = split(pair * (1.0 / math.sqrt(KVEC * ATOMS)))
    pair = dot(jnp.concatenate(pair, axis=0), hot[...], NN)
    pair = pair[0:MINE] + pair[MINE : 2 * MINE]
    for d in range(STRUCTS):
        parts[d, 0:16, :] = jnp.concatenate(
            [pair[:, d * KSHARE : (d + 1) * KSHARE], grad_in], axis=0
        ).astype(BF16)
        parts[d, 16:48, :] = early[d * SLOTS : (d + 1) * SLOTS, :].astype(BF16)


SPECTRUM_SCRATCH = [
    pltpu.VMEM((2 * HALF, KVEC), BF16),
    pltpu.VMEM((8, ATOMS), F32),
    pltpu.VMEM((CH + 16, ATOMS), BF16),
    pltpu.VMEM((2 * PLANE, ATOMS), F32),
    pltpu.VMEM((WAVES * (CH + 16), ATOMS), BF16),
]


def update_kernel(
    place, factor, folded, table_own, in_weight, feats, local, updated, coef
):
    both = jnp.concatenate(split(factor[0:CH, :]), axis=0)
    s = dot(in_weight[...], both, NN)
    pieces = filtered(folded[0:CH, :], folded[CH : 2 * CH, :], s)
    for n, piece in enumerate(pieces):
        coef[:, n * PLANE : (n + 1) * PLANE] = piece.astype(BF16)
    ewald = dot(coef[...], table_own[...], NN)
    here = lax.broadcasted_iota(I32, (CH, ROWS), 1) < place[1]
    updated[0] = jnp.where(
        here, feats[0].astype(F32) + local[...] + ewald, 0.0
    ).astype(BF16)


def middle_kernel(place, sums, last, grad_in):
    row = lax.broadcasted_iota(I32, (8, KSHARE), 0)
    lane = lax.broadcasted_iota(I32, (8, KSHARE), 1)
    pick = jnp.where(lane == row + place[4], 1.0, 0.0).astype(BF16)
    pairs = jnp.concatenate([sums[p, 0:16].astype(F32)[0:8] for p in range(SLABS)], axis=0)
    grads = jnp.concatenate([sums[p, 0:16].astype(F32)[8:16] for p in range(SLABS)], axis=0)
    grad_in[...] = grads.T
    total = sums[0, 16:48].astype(F32)
    for p in range(1, SLABS):
        total = total + sums[p, 16:48].astype(F32)
    last[0:32] = total.astype(BF16)
    picked = dot(pick, pairs.astype(BF16), NT)
    last[32:48] = jnp.concatenate([picked, picked], axis=0).astype(BF16)


def finish_kernel(sums, ewald_in, grad_filter, grad_in, grad_out):
    for d in range(STRUCTS):
        late = sums[d, 32:48].astype(F32)
        grad_filter[8 * d : 8 * d + 8, :] = late[0:8]
    for d in range(4):
        here = slice(d * SLOTS, (d + 1) * SLOTS)
        grad_in[here, :] = ewald_in[here, :] + sums[d, 0:32].astype(F32)
    for d in range(4, STRUCTS):
        grad_out[(d - 4) * SLOTS : (d - 3) * SLOTS, :] = sums[d, 0:32].astype(F32)


def exchange(x, axis):
    return lax.all_to_all(x, axis, 0, 0)


def to_all(x, axis, count):
    return exchange(jnp.broadcast_to(x[None], (count,) + x.shape), axis)


def shards(
    node_feats,
    frac,
    neighbours,
    images,
    neighbour_count,
    atom_count,
    miller,
    in_weight,
    radial_weight,
    out_weight,
    filter_weight,
    cotangent,
):
    slab = lax.axis_index("atom")
    first = slab * ROWS
    live = atom_count[0] - jnp.stack(
        [first, (first - ROWS) % ATOMS, (first + ROWS) % ATOMS]
    )
    place = jnp.concatenate([first[None], live, slab[None] * MINE]).astype(I32)
    struct = jax.ShapeDtypeStruct

    halo = jnp.concatenate([node_feats[0], coordinates(frac[0])], axis=0)
    ring = range(SLABS)
    left = lax.ppermute(halo, "atom", [(i, (i + 1) % SLABS) for i in ring])
    right = lax.ppermute(halo, "atom", [((i + 1) % SLABS, i) for i in ring])
    cot_parts = jnp.pad(cotangent.reshape(SLABS, MINE, ROWS), ((0, 0), (0, 8), (0, 0)))
    gathered = exchange(
        jnp.concatenate(
            [jnp.broadcast_to(halo[None], (SLABS, COT_AT, ROWS)), cot_parts], axis=1
        ),
        "atom",
    )
    frac = frac.transpose(1, 0, 2)

    order = (SLABS, STRUCTS, KVEC // SLABS // STRUCTS)
    miller = miller.reshape((3,) + order).transpose(0, 2, 1, 3).reshape(3, KVEC)
    filter_weight = (
        filter_weight.reshape(order + (CH,)).transpose(1, 0, 2, 3).reshape(KVEC, CH)
    )
    folded, table_own = call(
        lattice_kernel,
        [
            (VMEM, struct((2 * CH, HALF), F32)),
            (VMEM, struct((BASIS, ROWS), BF16)),
        ],
        [
            pltpu.VMEM((2 * HALF, KVEC), BF16),
            pltpu.VMEM((2 * PLANE, ROWS), F32),
            pltpu.VMEM((8, ROWS), F32),
        ],
        24,
        10**8,
        (VMEM, miller),
        (VMEM, filter_weight),
        (VMEM, frac),
    )
    early, local = call(
        edge_kernel,
        [(VMEM, struct((4 * CH, CH), F32)), (VMEM, struct((CH, ROWS), F32))],
        [
            pltpu.VMEM((1, SLOTS, ROWS), I32),
            pltpu.VMEM((1, SLOTS, ROWS), I32),
            pltpu.VMEM((1, ROWS), I32),
            pltpu.VMEM((CH, CH), BF16),
            pltpu.VMEM((3, NB, CH), F32),
            pltpu.VMEM((3 * CH, CH), BF16),
            pltpu.VMEM((1, CH, ROWS), BF16),
            pltpu.VMEM((CH, 2 * ROWS), BF16),
            pltpu.VMEM((2 * ROWS, EDGES), BF16),
            pltpu.VMEM((32, 3 * CH), F32),
            pltpu.VMEM((32, EDGES), F32),
            pltpu.VMEM((3 * CH, EDGES), F32),
            pltpu.VMEM((CH, EDGES), F32),
            pltpu.VMEM((9, SLOTS, ROWS), F32),
            pltpu.VMEM((SLOTS, ROWS), F32),
            pltpu.VMEM((9, CH, ROWS), F32),
            pltpu.VMEM((3 * CH, ROWS), F32),
            pltpu.VMEM((CH, EDGES), BF16),
            pltpu.VMEM((3 * CH, ROWS), BF16),
            pltpu.SemaphoreType.DMA((7,)),
        ],
        24,
        EDGE_COST,
        (SMEM, place),
        (VMEM, halo),
        (VMEM, left),
        (VMEM, right),
        (HBM, neighbours),
        (HBM, images),
        (HBM, neighbour_count),
        (HBM, in_weight),
        (HBM, radial_weight),
        (HBM, out_weight),
        (HBM, cotangent),
    )
    weight_t = jnp.concatenate([in_weight, in_weight], axis=0).T
    own_weight = lax.dynamic_slice_in_dim(in_weight, slab * MINE, MINE, 1)
    own_weight = jnp.pad(jnp.concatenate([own_weight, own_weight], axis=0).T, ((0, 8), (0, 0)))
    parts, factor = call(
        spectrum_kernel,
        [
            (VMEM, struct((STRUCTS, 48, CH), BF16)),
            (VMEM, struct((CH + 16, BASIS), F32)),
        ],
        SPECTRUM_SCRATCH,
        32,
        10**10,
        (SMEM, place),
        (VMEM, gathered),
        (VMEM, folded),
        (VMEM, miller),
        (VMEM, own_weight),
        (VMEM, early),
    )
    (updated,) = call(
        update_kernel,
        [(VMEM, struct((1, CH, ROWS), BF16))],
        [pltpu.VMEM((CH, BASIS), BF16)],
        24,
        10**9,
        (SMEM, place),
        (VMEM, factor),
        (VMEM, folded),
        (VMEM, table_own),
        (VMEM, weight_t),
        (VMEM, node_feats),
        (VMEM, local),
    )
    sums = exchange(parts, "dp").astype(F32).sum(axis=0).astype(BF16)
    last, ewald_in = call(
        middle_kernel,
        [(VMEM, struct((48, CH), BF16)), (VMEM, struct((CH, CH), F32))],
        [],
        16,
        10**6,
        (SMEM, place),
        (VMEM, to_all(sums, "atom", SLABS)),
    )
    grads = call(
        finish_kernel,
        [
            (VMEM, struct((KSHARE, CH), F32)),
            (VMEM, struct((CH, CH), F32)),
            (VMEM, struct((3 * CH, CH), F32)),
        ],
        [],
        16,
        10**6,
        (VMEM, to_all(last, "dp", STRUCTS)),
        (VMEM, ewald_in),
    )
    return (updated, *grads)


def solution(mesh):
    return jax.shard_map(
        shards,
        mesh=mesh,
        in_specs=(
            P("dp", None, "atom"),
            P("dp", None, "atom"),
            P("dp", None, "atom"),
            P("dp", None, "atom"),
            P("dp", "atom"),
            P("dp"),
            P(),
            P(),
            P(),
            P(),
            P(),
            P("dp", None, "atom"),
        ),
        out_specs=(P("dp", None, "atom"), P("atom", None), P(), P()),
        check_vma=False,
    )
```

```python
import math

import jax
import jax.numpy as jnp
from jax import lax
from jax.experimental import pallas as pl
from jax.experimental.pallas import tpu as pltpu
from jax.sharding import PartitionSpec as P

F32 = jnp.float32
BF16 = jnp.bfloat16
I32 = jnp.int32

CH = 128
ROWS = 128
SLABS = 16
STRUCTS = 16
ATOMS = ROWS * SLABS
SLOTS = 32
EDGES = SLOTS * ROWS
GHOST = 32
KVEC = 2048
KSHARE = KVEC // SLABS
NB = 8
TOP = 6
SIDE = 2 * TOP + 1
PLANE = 128
HALF = (TOP + 1) * PLANE
WAVES = SIDE
BASIS = WAVES * 2 * PLANE
TILE = 256
MINE = CH // SLABS
QUARTER = CH // 4
FRAC_AT = CH
HALO = CH + 16
COT_AT, HID_AT, PAY = QUARTER, 2 * QUARTER, 2 * QUARTER + 16

VMEM = pl.BlockSpec(memory_space=pltpu.VMEM)
SMEM = pl.BlockSpec(memory_space=pltpu.SMEM)

NN = (((1,), (0,)), ((), ()))
NT = (((1,), (1,)), ((), ()))
TN = (((0,), (0,)), ((), ()))


def dot(a, b, dims):
    return lax.dot_general(a, b, dims, preferred_element_type=F32)


def split(x):
    hi = x.astype(BF16)
    return hi, (x - hi.astype(F32)).astype(BF16)


def call(kernel, outs, scratch, mib, flops, *args):
    return pl.pallas_call(
        kernel,
        out_shape=[shape for _, shape in outs],
        in_specs=[spec for spec, _ in args],
        out_specs=[spec for spec, _ in outs],
        scratch_shapes=scratch,
        compiler_params=pltpu.CompilerParams(vmem_limit_bytes=mib * 2**20),
        cost_estimate=pl.CostEstimate(
            flops=flops, bytes_accessed=2**16, transcendentals=0
        ),
    )(*[arg for _, arg in args])


def coordinates(frac):
    rows = jnp.concatenate([frac, frac, jnp.zeros((10, frac.shape[1]), F32)], axis=0)
    first = jnp.floor(rows * 256.0) * (1.0 / 256.0)
    top = lax.broadcasted_iota(I32, rows.shape, 0) < 3
    return jnp.where(top, first, rows - first).astype(BF16)


def joined_frac(rows):
    wide = rows.astype(F32)
    return [wide[d : d + 1] + wide[d + 3 : d + 4] for d in range(3)]


ROOT3, ROOT5, ROOT15 = math.sqrt(3.0), math.sqrt(5.0), math.sqrt(15.0)
STEP = 1.75 / (NB - 1)
BAND = 16
EDGE_COST = 10**10


def edge_kernel(
    place,
    own,
    left,
    right,
    neighbours,
    images,
    count,
    in_weight,
    radial_weight,
    out_weight,
    cot,
    early,
    local,
    ext,
    hot,
    weights,
    basis,
    radial,
    moved,
    shape_w,
    length,
    feats9,
    up9,
    pulled,
    inv,
):
    first, live_here, live_left, live_right = place[0], place[1], place[2], place[3]
    lane = lax.broadcasted_iota(I32, (CH, ROWS), 1)
    ext[:, 0:ROWS] = jnp.where(lane < live_here, own[0:CH].astype(F32), 0.0).astype(BF16)
    near_right = jnp.where(lane < live_right, right[0:CH].astype(F32), 0.0)
    near_left = jnp.where(lane < live_left, left[0:CH].astype(F32), 0.0)
    ext[:, ROWS : 2 * ROWS] = jnp.where(lane < GHOST, near_right, near_left).astype(BF16)
    hidden = dot(in_weight[...], ext[...], TN).astype(BF16)

    offset = (neighbours[0] - first) & (ATOMS - 1)
    column = jnp.where(offset < ROWS + GHOST, offset, offset - (ATOMS - 2 * ROWS))
    at = column & (ROWS - 1)
    in_slab = column < ROWS
    frac_own = joined_frac(own[FRAC_AT:HALO])
    frac_left = joined_frac(left[FRAC_AT:HALO])
    frac_right = joined_frac(right[FRAC_AT:HALO])
    lane1 = lax.broadcasted_iota(I32, (1, ROWS), 1)

    code = images[0]
    ninth = (code * 57) >> 9
    third = (code * 171) >> 9
    shifts = (ninth, third - 3 * ninth, code - 3 * third)
    vector = []
    for d in range(3):
        near = jnp.broadcast_to(frac_own[d], (SLOTS, ROWS))
        far = jnp.where(lane1 < GHOST, frac_right[d], frac_left[d])
        far = jnp.broadcast_to(far, (SLOTS, ROWS))
        other = jnp.where(
            in_slab,
            jnp.take_along_axis(near, at, axis=1),
            jnp.take_along_axis(far, at, axis=1),
        )
        vector.append(0.5 * (other - near + (shifts[d].astype(F32) - 1.0)))
    x, y, z = vector
    square = x * x + y * y + z * z
    slot = lax.broadcasted_iota(I32, (SLOTS, ROWS), 0)
    lane32 = lax.broadcasted_iota(I32, (SLOTS, ROWS), 1)
    used = (slot < count[...]) & (lane32 < live_here)
    weight = jnp.where(used, SLOTS**-0.5, 0.0)
    harmonics = (
        weight,
        weight * (ROOT3 * x),
        weight * (ROOT3 * y),
        weight * (ROOT3 * z),
        weight * (ROOT15 * x * y),
        weight * (ROOT15 * y * z),
        weight * (0.5 * ROOT5 * (3.0 * z * z - square)),
        weight * (ROOT15 * x * z),
        weight * (0.5 * ROOT15 * (x * x - y * y)),
    )
    for m in range(9):
        shape_w[m] = harmonics[m]
    length[...] = jnp.sqrt(square)

    rows256 = lax.broadcasted_iota(I32, (2 * ROWS, ROWS), 0)
    centre = lax.broadcasted_iota(I32, (NB, ROWS), 0).astype(F32) * STEP
    basis[24:32, :] = jnp.zeros((8, EDGES), F32)
    for e in range(SLOTS):
        here = slice(e * ROWS, (e + 1) * ROWS)
        hot[:, here] = jnp.where(rows256 == column[e : e + 1], 1.0, 0.0).astype(BF16)
        gap = (length[e : e + 1, :] - centre) * (1.0 / STEP)
        gauss = jnp.exp(-(gap * gap))
        hi, lo = split(gauss)
        basis[0:8, here] = hi.astype(F32)
        basis[8:16, here] = lo.astype(F32)
        basis[16:24, here] = hi.astype(F32)
    weights[...] = jnp.zeros((32, 3 * CH), F32)
    for l in range(3):
        hi, lo = split(radial_weight[l])
        part = slice(l * CH, (l + 1) * CH)
        weights[0:8, part] = hi.astype(F32)
        weights[8:16, part] = hi.astype(F32)
        weights[16:24, part] = lo.astype(F32)
    radial[...] = dot(weights[...].astype(BF16), basis[...].astype(BF16), TN)
    moved[...] = dot(hidden, hot[...], NN)

    def forward(step, carry):
        top = pl.multiple_of(step * BAND, BAND)
        total = [jnp.zeros((BAND, ROWS), F32) for _ in range(9)]
        for e in range(SLOTS):
            here = slice(e * ROWS, (e + 1) * ROWS)
            value = moved[pl.ds(top, BAND), here]
            parts = [
                radial[pl.ds(pl.multiple_of(l * CH + top, BAND), BAND), here] * value
                for l in range(3)
            ]
            for m in range(9):
                l = 0 if m == 0 else (1 if m < 4 else 2)
                total[m] = total[m] + shape_w[m, e : e + 1, :] * parts[l]
        for m in range(9):
            feats9[m, pl.ds(top, BAND), :] = total[m]
        squares = [t * t for t in total]
        inv[pl.ds(top, BAND), :] = squares[0].astype(BF16)
        inv[pl.ds(pl.multiple_of(CH + top, BAND), BAND), :] = (
            squares[1] + squares[2] + squares[3]
        ).astype(BF16)
        inv[pl.ds(pl.multiple_of(2 * CH + top, BAND), BAND), :] = (
            squares[4] + squares[5] + squares[6] + squares[7] + squares[8]
        ).astype(BF16)
        return carry

    lax.fori_loop(0, CH // BAND, forward, 0)

    masked = jnp.where(lane < live_here, cot[0].astype(F32), 0.0).astype(BF16)
    local[...] = dot(out_weight[...], inv[...], TN)
    up9[...] = 2.0 * dot(out_weight[...], masked, NN)
    grad_out = dot(inv[...], masked, NT)
    for d in range(4, STRUCTS):
        to = d * SLOTS
        early[to : to + SLOTS, :] = grad_out[(d - 4) * SLOTS : (d - 3) * SLOTS]

    def backward(step, carry):
        top = pl.multiple_of(step * BAND, BAND)
        up = [
            up9[pl.ds(pl.multiple_of(l * CH + top, BAND), BAND), :] for l in range(3)
        ]
        upstream = []
        for m in range(9):
            l = 0 if m == 0 else (1 if m < 4 else 2)
            upstream.append(feats9[m, pl.ds(top, BAND), :] * up[l])
        for e in range(SLOTS):
            here = slice(e * ROWS, (e + 1) * ROWS)
            term = [shape_w[m, e : e + 1, :] * upstream[m] for m in range(9)]
            pull = (
                radial[pl.ds(top, BAND), here] * term[0]
                + radial[pl.ds(pl.multiple_of(CH + top, BAND), BAND), here]
                * (term[1] + term[2] + term[3])
                + radial[pl.ds(pl.multiple_of(2 * CH + top, BAND), BAND), here]
                * (term[4] + term[5] + term[6] + term[7] + term[8])
            )
            pulled[pl.ds(top, BAND), here] = pull.astype(BF16)
        return carry

    lax.fori_loop(0, CH // BAND, backward, 0)
    back = dot(pulled[...], hot[...], NT)
    grad_in = dot(ext[...], back.astype(BF16), NT)
    for d in range(4):
        to = d * SLOTS
        early[to : to + SLOTS, :] = grad_in[d * SLOTS : (d + 1) * SLOTS]


def half_point(miller):
    m0, m1, m2 = miller[0:1], miller[1:2], miller[2:3]
    sign = jnp.where(m0 < 0, -1, 1)
    m0, m1, m2 = sign * m0, sign * m1, sign * m2
    minus = m1 < 0
    turn = jnp.where(minus, -1, 1)
    plane = m0 + jnp.where(minus, TOP + 1, 0)
    return plane, turn * m1 * SIDE + (turn * m2 + TOP)


def one_hot(point):
    row = lax.broadcasted_iota(I32, (PLANE, KVEC), 0)
    return jnp.where(row == point, 1.0, 0.0).astype(BF16)


def turns(frac_row, first, count):
    width = frac_row.shape[1]
    m = (lax.broadcasted_iota(I32, (count, width), 0) + first).astype(F32)
    turn = m * frac_row
    turn = turn - jnp.floor(turn + 0.5)
    quarter = jnp.floor(turn * 4.0 + 0.5)
    arc = (turn - 0.25 * quarter) * (2.0 * math.pi)
    s2 = arc * arc
    sine = arc * (1.0 + s2 * (-1 / 6 + s2 * (1 / 120 + s2 * (-1 / 5040))))
    cosine = 1.0 + s2 * (-0.5 + s2 * (1 / 24 + s2 * (-1 / 720 + s2 * (1 / 40320))))
    odd = jnp.abs(quarter) == 1.0
    back = jnp.abs(quarter) == 2.0
    flip = jnp.where(quarter < 0.0, -1.0, 1.0)
    cos_out = jnp.where(odd, -flip * sine, jnp.where(back, -cosine, cosine))
    sin_out = jnp.where(odd, flip * cosine, jnp.where(back, -sine, sine))
    return cos_out, sin_out


def waves(frac, plane):
    width = plane.shape[1]
    c1, s1 = turns(frac[1], 0, 8)
    c2, s2 = turns(frac[2], -TOP, 16)
    for k in (0, PLANE):
        plane[k + 88 : k + PLANE, :] = jnp.zeros((PLANE - 88, width), F32)
    for m in range(TOP + 1):
        cm, sm = c1[m : m + 1], s1[m : m + 1]
        plane[m * SIDE : m * SIDE + 16, :] = cm * c2 - sm * s2
        plane[PLANE + m * SIDE : PLANE + m * SIDE + 16, :] = sm * c2 + cm * s2
    c0, s0 = turns(frac[0], 0, 8)
    return [c0[m : m + 1] for m in range(TOP + 1)] + [
        s0[m : m + 1] for m in range(1, TOP + 1)
    ]


def lattice_kernel(place, miller, filter_weight, folded, turned, wide):
    plane, point = half_point(miller[...])
    turned[...] = filter_weight[...].T * (1.0 / math.sqrt(KVEC * ATOMS))
    mine = turned[pl.ds(pl.multiple_of(place[5], QUARTER), QUARTER), :]
    for b in range(2 * (TOP + 1)):
        here = slice(b * QUARTER, (b + 1) * QUARTER)
        wide[here, :] = jnp.where(plane == b, mine, 0.0).astype(BF16)
    sums = dot(wide[...], one_hot(point), NT)
    half = (TOP + 1) * QUARTER
    for m in range(TOP + 1):
        here = slice(m * QUARTER, (m + 1) * QUARTER)
        there = slice(half + m * QUARTER, half + (m + 1) * QUARTER)
        lanes = slice(m * PLANE, (m + 1) * PLANE)
        folded[0:QUARTER, lanes] = sums[here] + sums[there]
        folded[QUARTER : 2 * QUARTER, lanes] = sums[here] - sums[there]


def blocks(x, m):
    at = 2 * m * PLANE
    cc, cs = x[:, at : at + PLANE], x[:, at + PLANE : at + 2 * PLANE]
    if m == 0:
        return cc, None, None, cs
    at = 2 * (TOP + m) * PLANE
    sc, ss = x[:, at : at + PLANE], x[:, at + PLANE : at + 2 * PLANE]
    return cc, ss, sc, cs


def filtered(plus, minus, x):
    first, second = [], []
    for m in range(TOP + 1):
        here = slice(m * PLANE, (m + 1) * PLANE)
        p, d = plus[:, here], minus[:, here]
        cc, ss, sc, cs = blocks(x, m)
        if m == 0:
            first += [p * cc, p * cs]
        else:
            first += [p * cc - d * ss, p * cs + d * sc]
            second += [p * sc + d * cs, p * ss - d * cc]
    return first + second


def spectrum_kernel(
    place, gathered, folded, miller, early, parts, ewald, factor, frac, values, plane, wide
):
    for p in range(SLABS):
        here = slice(p * ROWS, (p + 1) * ROWS)
        values[:, here] = gathered[p]
        tail = gathered[p, HID_AT:PAY].astype(F32)
        frac[0:3, here] = tail[MINE : MINE + 3] + tail[MINE + 3 : MINE + 6]
    along = waves([frac[d : d + 1, :] for d in range(3)], plane)
    live = (lax.broadcasted_iota(I32, (1, ATOMS), 1) < place[0] + place[1]).astype(F32)
    around = plane[...].astype(BF16)
    for low, high in ((0, TOP + 1), (TOP + 1, WAVES)):
        for f in range(low, high):
            wide[f * PAY : (f + 1) * PAY, :] = (
                values[...].astype(F32) * (along[f] * live)
            ).astype(BF16)
        both = dot(wide[low * PAY : high * PAY, :], around, NT)
        for f in range(low, high):
            here = slice(f * 2 * PLANE, (f + 1) * 2 * PLANE)
            factor[:, here] = both[(f - low) * PAY : (f - low + 1) * PAY]

    at = pl.multiple_of(place[4] - place[5], MINE)
    s = factor[HID_AT : HID_AT + MINE, :]
    g = factor[pl.ds(pl.multiple_of(COT_AT + at, MINE), MINE), :]
    plus = folded[pl.ds(at, MINE), :]
    minus = folded[pl.ds(pl.multiple_of(QUARTER + at, MINE), MINE), :]
    pair_plus, pair_minus = [], []
    for m in range(TOP + 1):
        cc, ss, sc, cs = blocks(s, m)
        gcc, gss, gsc, gcs = blocks(g, m)
        even, odd = cc * gcc + cs * gcs, 0.0
        if m > 0:
            even = even + ss * gss + sc * gsc
            odd = sc * gcs + cs * gsc - cc * gss - ss * gcc
        pair_plus.append(even + odd)
        pair_minus.append(even - odd)
    pair = jnp.concatenate(pair_plus + pair_minus, axis=0)
    pair = split(pair * (1.0 / math.sqrt(KVEC * ATOMS)))
    around_plane, point = half_point(miller[...])
    found = dot(jnp.concatenate(pair, axis=0), one_hot(point), NN)
    planes = 2 * (TOP + 1)
    pair = jnp.zeros((MINE, KVEC), F32)
    for b in range(planes):
        value = found[b * MINE : (b + 1) * MINE] + found[(planes + b) * MINE : (planes + b + 1) * MINE]
        pair = jnp.where(around_plane == b, value, pair)
    grad = filtered(
        folded[0:QUARTER, :],
        folded[QUARTER : 2 * QUARTER, :],
        factor[COT_AT:HID_AT, :],
    )
    grad = jnp.concatenate(split(jnp.concatenate(grad, axis=1)), axis=0)
    block = dot(grad, factor[0:QUARTER, :].astype(BF16), NT)
    block = block[0:QUARTER] + block[QUARTER : 2 * QUARTER]
    block = jnp.concatenate([block[8 * q : 8 * q + 8] for q in range(4)], axis=1)
    for d in range(STRUCTS):
        parts[d, 0:16, :] = jnp.concatenate(
            [pair[:, d * KSHARE : (d + 1) * KSHARE], block], axis=0
        ).astype(BF16)
        parts[d, 16:48, :] = early[d * SLOTS : (d + 1) * SLOTS, :].astype(BF16)
    coef = filtered(plus, minus, s)
    coef = [
        jnp.concatenate([coef[2 * f], coef[2 * f + 1]], axis=1) for f in range(WAVES)
    ]
    field = dot(jnp.concatenate(coef, axis=0).astype(BF16), around, NN)
    total = field[0:MINE] * along[0]
    for f in range(1, WAVES):
        total = total + field[f * MINE : (f + 1) * MINE] * along[f]
    for p in range(SLABS):
        ewald[p] = total[:, p * ROWS : (p + 1) * ROWS].astype(BF16)


SPECTRUM_SCRATCH = [
    pltpu.VMEM((PAY, BASIS), F32),
    pltpu.VMEM((8, ATOMS), F32),
    pltpu.VMEM((PAY, ATOMS), BF16),
    pltpu.VMEM((2 * PLANE, ATOMS), F32),
    pltpu.VMEM((WAVES * PAY, ATOMS), BF16),
]


def middle_kernel(place, sums, feats, local, last, grad_in, updated):
    row = lax.broadcasted_iota(I32, (8, KSHARE), 0)
    lane = lax.broadcasted_iota(I32, (8, KSHARE), 1)
    pick = jnp.where(lane == row + place[4], 1.0, 0.0).astype(BF16)
    blocks = [sums[p].astype(F32) for p in range(SLABS)]
    pairs = jnp.concatenate([block[0:8] for block in blocks], axis=0)
    picked = dot(pick, pairs.astype(BF16), NT)
    total = blocks[0][16:48]
    for block in blocks[1:]:
        total = total + block[16:48]
    out = jnp.concatenate([total, picked, picked], axis=0).astype(BF16)
    for d in range(STRUCTS):
        last[d] = out
    grads = []
    for c in range(0, CH, 8):
        at, g = c % QUARTER // 8, c // QUARTER
        eight = blocks[4 * g][8:16]
        eight = pltpu.roll(eight, (0 - at) * QUARTER % CH, 1)
        for q in range(1, 4):
            turned = pltpu.roll(blocks[4 * g + q][8:16], (q - at) * QUARTER % CH, 1)
            eight = jnp.where(lane < q * QUARTER, eight, turned)
        grads.append(eight)
    grad_in[...] = jnp.concatenate(grads, axis=0).T
    ewald = jnp.concatenate([block[48:56] for block in blocks], axis=0)
    here = lax.broadcasted_iota(I32, (CH, ROWS), 1) < place[1]
    updated[0] = jnp.where(
        here, feats[0].astype(F32) + local[...] + ewald, 0.0
    ).astype(BF16)


def finish_kernel(sums, ewald_in, grad_filter, grad_in, grad_out):
    for d in range(STRUCTS):
        late = sums[d, 32:48].astype(F32)
        grad_filter[8 * d : 8 * d + 8, :] = late[0:8]
    for d in range(4):
        here = slice(d * SLOTS, (d + 1) * SLOTS)
        grad_in[here, :] = ewald_in[here, :] + sums[d, 0:32].astype(F32)
    for d in range(4, STRUCTS):
        grad_out[(d - 4) * SLOTS : (d - 3) * SLOTS, :] = sums[d, 0:32].astype(F32)


def exchange(x, axis):
    return lax.all_to_all(x, axis, 0, 0)


def shards(
    node_feats,
    frac,
    neighbours,
    images,
    neighbour_count,
    atom_count,
    miller,
    in_weight,
    radial_weight,
    out_weight,
    filter_weight,
    cotangent,
):
    slab = lax.axis_index("atom")
    first = slab * ROWS
    live = atom_count[0] - jnp.stack(
        [first, (first - ROWS) % ATOMS, (first + ROWS) % ATOMS]
    )
    place = jnp.stack([slab * MINE, slab // 4 * QUARTER])
    place = jnp.concatenate([first[None], live, place]).astype(I32)
    struct = jax.ShapeDtypeStruct

    feats = node_feats[0]
    halo = jnp.concatenate([feats, coordinates(frac[0])], axis=0)
    where = halo[FRAC_AT : FRAC_AT + 8]
    ring = range(SLABS)
    left = lax.ppermute(halo, "atom", [(i, (i + 1) % SLABS) for i in ring])
    right = lax.ppermute(halo, "atom", [((i + 1) % SLABS, i) for i in ring])
    hidden = dot(in_weight, feats, TN).astype(BF16)
    square = (4, 4, QUARTER, ROWS)
    payload = [
        jnp.broadcast_to(feats.reshape(1, 4, QUARTER, ROWS), square),
        jnp.broadcast_to(cotangent[0].reshape(4, 1, QUARTER, ROWS), square),
        hidden.reshape(4, 4, MINE, ROWS),
        jnp.broadcast_to(where, (4, 4, 8, ROWS)),
    ]
    payload = jnp.concatenate(payload, axis=2).reshape(SLABS, PAY, ROWS)
    gathered = exchange(payload, "atom")

    (folded,) = call(
        lattice_kernel,
        [(VMEM, struct((2 * QUARTER, HALF), F32))],
        [
            pltpu.VMEM((CH, KVEC), F32),
            pltpu.VMEM((2 * (TOP + 1) * QUARTER, KVEC), BF16),
        ],
        12,
        10**8,
        (SMEM, place),
        (VMEM, miller),
        (VMEM, filter_weight),
    )
    order = (3, SLABS, STRUCTS, KVEC // SLABS // STRUCTS)
    miller = miller.reshape(order).transpose(0, 2, 1, 3).reshape(3, KVEC)
    early, local = call(
        edge_kernel,
        [(VMEM, struct((4 * CH, CH), F32)), (VMEM, struct((CH, ROWS), F32))],
        [
            pltpu.VMEM((CH, 2 * ROWS), BF16),
            pltpu.VMEM((2 * ROWS, EDGES), BF16),
            pltpu.VMEM((32, 3 * CH), F32),
            pltpu.VMEM((32, EDGES), F32),
            pltpu.VMEM((3 * CH, EDGES), F32),
            pltpu.VMEM((CH, EDGES), F32),
            pltpu.VMEM((9, SLOTS, ROWS), F32),
            pltpu.VMEM((SLOTS, ROWS), F32),
            pltpu.VMEM((9, CH, ROWS), F32),
            pltpu.VMEM((3 * CH, ROWS), F32),
            pltpu.VMEM((CH, EDGES), BF16),
            pltpu.VMEM((3 * CH, ROWS), BF16),
        ],
        20,
        EDGE_COST,
        (SMEM, place),
        (VMEM, halo),
        (VMEM, left),
        (VMEM, right),
        (VMEM, neighbours),
        (VMEM, images),
        (VMEM, neighbour_count),
        (VMEM, in_weight),
        (VMEM, radial_weight),
        (VMEM, out_weight),
        (VMEM, cotangent),
    )
    parts, ewald = call(
        spectrum_kernel,
        [
            (VMEM, struct((STRUCTS, 48, CH), BF16)),
            (VMEM, struct((SLABS, MINE, ROWS), BF16)),
        ],
        SPECTRUM_SCRATCH,
        20,
        10**10,
        (SMEM, place),
        (VMEM, gathered),
        (VMEM, folded),
        (VMEM, miller),
        (VMEM, early),
    )
    sums = exchange(parts, "dp").astype(F32).sum(axis=0).astype(BF16)
    sums = jnp.broadcast_to(sums[None], (SLABS, 48, CH))
    last, ewald_in, updated = call(
        middle_kernel,
        [
            (VMEM, struct((STRUCTS, 48, CH), BF16)),
            (VMEM, struct((CH, CH), F32)),
            (VMEM, struct((1, CH, ROWS), BF16)),
        ],
        [],
        16,
        10**6,
        (SMEM, place),
        (VMEM, exchange(jnp.concatenate([sums, ewald], axis=1), "atom")),
        (VMEM, node_feats),
        (VMEM, local),
    )
    grads = call(
        finish_kernel,
        [
            (VMEM, struct((KSHARE, CH), F32)),
            (VMEM, struct((CH, CH), F32)),
            (VMEM, struct((3 * CH, CH), F32)),
        ],
        [],
        16,
        10**6,
        (VMEM, exchange(last, "dp")),
        (VMEM, ewald_in),
    )
    return (updated, *grads)


def solution(mesh):
    return jax.shard_map(
        shards,
        mesh=mesh,
        in_specs=(
            P("dp", None, "atom"),
            P("dp", None, "atom"),
            P("dp", None, "atom"),
            P("dp", None, "atom"),
            P("dp", "atom"),
            P("dp"),
            P(),
            P(),
            P(),
            P(),
            P(),
            P("dp", None, "atom"),
        ),
        out_specs=(P("dp", None, "atom"), P("atom", None), P(), P()),
        check_vma=False,
    )
```

```python
import math

import jax
import jax.numpy as jnp
from jax import lax
from jax.experimental import pallas as pl
from jax.experimental.pallas import tpu as pltpu
from jax.sharding import PartitionSpec as P

F32 = jnp.float32
BF16 = jnp.bfloat16
I32 = jnp.int32

CH = 128
ROWS = 128
SLABS = 16
STRUCTS = 16
ATOMS = ROWS * SLABS
SLOTS = 32
EDGES = SLOTS * ROWS
GHOST = 32
KVEC = 2048
KSHARE = KVEC // SLABS
NB = 8
TOP = 6
SIDE = 2 * TOP + 1
PLANE = 128
HALF = (TOP + 1) * PLANE
WAVES = SIDE
BASIS = WAVES * 2 * PLANE
TILE = 256
MINE = CH // SLABS
QUARTER = CH // 4
FRAC_AT = CH
HALO = CH + 16
COT_AT, HID_AT, PAY = QUARTER, 2 * QUARTER, 2 * QUARTER + 16

VMEM = pl.BlockSpec(memory_space=pltpu.VMEM)
SMEM = pl.BlockSpec(memory_space=pltpu.SMEM)
HBM = pl.BlockSpec(memory_space=pltpu.HBM)

NN = (((1,), (0,)), ((), ()))
NT = (((1,), (1,)), ((), ()))
TN = (((0,), (0,)), ((), ()))


def dot(a, b, dims):
    return lax.dot_general(a, b, dims, preferred_element_type=F32)


def split(x):
    hi = x.astype(BF16)
    return hi, (x - hi.astype(F32)).astype(BF16)


def call(kernel, outs, scratch, mib, flops, *args):
    return pl.pallas_call(
        kernel,
        out_shape=[shape for _, shape in outs],
        in_specs=[spec for spec, _ in args],
        out_specs=[spec for spec, _ in outs],
        scratch_shapes=scratch,
        compiler_params=pltpu.CompilerParams(vmem_limit_bytes=mib * 2**20),
        cost_estimate=pl.CostEstimate(
            flops=flops, bytes_accessed=2**16, transcendentals=0
        ),
    )(*[arg for _, arg in args])


def pack_kernel(
    feats_hbm, cot_hbm, frac_hbm, weight_hbm, halo, payload_hbm, feats, cot, frac, weight, payload, rows, sems
):
    pairs = ((frac_hbm, frac), (feats_hbm, feats), (weight_hbm, weight), (cot_hbm, cot))
    copies = [
        pltpu.make_async_copy(src, dst, sems.at[n]) for n, (src, dst) in enumerate(pairs)
    ]
    for copy in copies:
        copy.start()
    copies[0].wait()
    rows[...] = jnp.zeros((16, ROWS), F32)
    for d in range(3):
        first = jnp.floor(frac[d] * 256.0) * (1.0 / 256.0)
        rows[d : d + 1, :] = first
        rows[d + 3 : d + 4, :] = frac[d] - first
    where = rows[...]
    halo[FRAC_AT:HALO] = where.astype(BF16)
    copies[1].wait()
    halo[0:CH] = feats[0]
    for a in range(SLABS):
        payload[a, 0:COT_AT] = feats[0, a % 4 * QUARTER : (a % 4 + 1) * QUARTER]
    copies[2].wait()
    hidden = dot(weight[...], feats[0], TN)
    for a in range(SLABS):
        payload[a, HID_AT:PAY] = jnp.concatenate(
            [hidden[a * MINE : (a + 1) * MINE], where[0:8]], axis=0
        ).astype(BF16)
    copies[3].wait()
    for a in range(SLABS):
        payload[a, COT_AT:HID_AT] = cot[0, a // 4 * QUARTER : (a // 4 + 1) * QUARTER]
    sent = pltpu.make_async_copy(payload, payload_hbm, sems.at[4])
    sent.start()
    sent.wait()


def joined_frac(rows):
    wide = rows.astype(F32)
    return [wide[d : d + 1] + wide[d + 3 : d + 4] for d in range(3)]


ROOT3, ROOT5, ROOT15 = math.sqrt(3.0), math.sqrt(5.0), math.sqrt(15.0)
STEP = 1.75 / (NB - 1)
BAND = 16
EDGE_COST = 10**10


def edge_kernel(
    place,
    own,
    first_swap,
    second_swap,
    neighbours,
    images,
    count,
    in_weight,
    radial_weight,
    out_weight,
    cot,
    early,
    local,
    ext,
    hot,
    weights,
    basis,
    radial,
    moved,
    shape_w,
    length,
    feats9,
    up9,
    pulled,
    inv,
):
    first, live_here, live_left, live_right = place[0], place[1], place[2], place[3]
    lane = lax.broadcasted_iota(I32, (CH, ROWS), 1)
    ext[:, 0:ROWS] = jnp.where(lane < live_here, own[0:CH].astype(F32), 0.0).astype(BF16)
    even = place[6] == 0
    swaps = first_swap[...].astype(F32), second_swap[...].astype(F32)
    right = jnp.where(even, swaps[0], swaps[1])
    left = jnp.where(even, swaps[1], swaps[0])
    near_right = jnp.where(lane < live_right, right[0:CH], 0.0)
    near_left = jnp.where(lane < live_left, left[0:CH], 0.0)
    ext[:, ROWS : 2 * ROWS] = jnp.where(lane < GHOST, near_right, near_left).astype(BF16)
    hidden = dot(in_weight[...], ext[...], TN).astype(BF16)

    offset = (neighbours[0] - first) & (ATOMS - 1)
    column = jnp.where(offset < ROWS + GHOST, offset, offset - (ATOMS - 2 * ROWS))
    at = column & (ROWS - 1)
    in_slab = column < ROWS
    frac_own = joined_frac(own[FRAC_AT:HALO])
    frac_left = joined_frac(left[FRAC_AT:HALO])
    frac_right = joined_frac(right[FRAC_AT:HALO])
    lane1 = lax.broadcasted_iota(I32, (1, ROWS), 1)

    code = images[0]
    ninth = (code * 57) >> 9
    third = (code * 171) >> 9
    shifts = (ninth, third - 3 * ninth, code - 3 * third)
    vector = []
    for d in range(3):
        near = jnp.broadcast_to(frac_own[d], (SLOTS, ROWS))
        far = jnp.where(lane1 < GHOST, frac_right[d], frac_left[d])
        far = jnp.broadcast_to(far, (SLOTS, ROWS))
        other = jnp.where(
            in_slab,
            jnp.take_along_axis(near, at, axis=1),
            jnp.take_along_axis(far, at, axis=1),
        )
        vector.append(0.5 * (other - near + (shifts[d].astype(F32) - 1.0)))
    x, y, z = vector
    square = x * x + y * y + z * z
    slot = lax.broadcasted_iota(I32, (SLOTS, ROWS), 0)
    lane32 = lax.broadcasted_iota(I32, (SLOTS, ROWS), 1)
    used = (slot < count[...]) & (lane32 < live_here)
    weight = jnp.where(used, SLOTS**-0.5, 0.0)
    harmonics = (
        weight,
        weight * (ROOT3 * x),
        weight * (ROOT3 * y),
        weight * (ROOT3 * z),
        weight * (ROOT15 * x * y),
        weight * (ROOT15 * y * z),
        weight * (0.5 * ROOT5 * (3.0 * z * z - square)),
        weight * (ROOT15 * x * z),
        weight * (0.5 * ROOT15 * (x * x - y * y)),
    )
    for m in range(9):
        shape_w[m] = harmonics[m]
    length[...] = jnp.sqrt(square)

    rows256 = lax.broadcasted_iota(I32, (2 * ROWS, ROWS), 0)
    centre = lax.broadcasted_iota(I32, (NB, ROWS), 0).astype(F32) * STEP
    basis[24:32, :] = jnp.zeros((8, EDGES), F32)
    for e in range(SLOTS):
        here = slice(e * ROWS, (e + 1) * ROWS)
        hot[:, here] = jnp.where(rows256 == column[e : e + 1], 1.0, 0.0).astype(BF16)
        gap = (length[e : e + 1, :] - centre) * (1.0 / STEP)
        gauss = jnp.exp(-(gap * gap))
        hi, lo = split(gauss)
        basis[0:8, here] = hi.astype(F32)
        basis[8:16, here] = lo.astype(F32)
        basis[16:24, here] = hi.astype(F32)
    weights[...] = jnp.zeros((32, 3 * CH), F32)
    for l in range(3):
        hi, lo = split(radial_weight[l])
        part = slice(l * CH, (l + 1) * CH)
        weights[0:8, part] = hi.astype(F32)
        weights[8:16, part] = hi.astype(F32)
        weights[16:24, part] = lo.astype(F32)
    radial[...] = dot(weights[...].astype(BF16), basis[...].astype(BF16), TN)
    moved[...] = dot(hidden, hot[...], NN)

    def forward(step, carry):
        top = pl.multiple_of(step * BAND, BAND)
        total = [jnp.zeros((BAND, ROWS), F32) for _ in range(9)]
        for e in range(SLOTS):
            here = slice(e * ROWS, (e + 1) * ROWS)
            value = moved[pl.ds(top, BAND), here]
            parts = [
                radial[pl.ds(pl.multiple_of(l * CH + top, BAND), BAND), here] * value
                for l in range(3)
            ]
            for m in range(9):
                l = 0 if m == 0 else (1 if m < 4 else 2)
                total[m] = total[m] + shape_w[m, e : e + 1, :] * parts[l]
        for m in range(9):
            feats9[m, pl.ds(top, BAND), :] = total[m]
        squares = [t * t for t in total]
        inv[pl.ds(top, BAND), :] = squares[0].astype(BF16)
        inv[pl.ds(pl.multiple_of(CH + top, BAND), BAND), :] = (
            squares[1] + squares[2] + squares[3]
        ).astype(BF16)
        inv[pl.ds(pl.multiple_of(2 * CH + top, BAND), BAND), :] = (
            squares[4] + squares[5] + squares[6] + squares[7] + squares[8]
        ).astype(BF16)
        return carry

    lax.fori_loop(0, CH // BAND, forward, 0)

    masked = jnp.where(lane < live_here, cot[0].astype(F32), 0.0).astype(BF16)
    local[...] = dot(out_weight[...], inv[...], TN)
    up9[...] = 2.0 * dot(out_weight[...], masked, NN)
    grad_out = dot(inv[...], masked, NT)
    for d in range(4, STRUCTS):
        to = d * SLOTS
        early[to : to + SLOTS, :] = grad_out[(d - 4) * SLOTS : (d - 3) * SLOTS]

    def backward(step, carry):
        top = pl.multiple_of(step * BAND, BAND)
        up = [
            up9[pl.ds(pl.multiple_of(l * CH + top, BAND), BAND), :] for l in range(3)
        ]
        upstream = []
        for m in range(9):
            l = 0 if m == 0 else (1 if m < 4 else 2)
            upstream.append(feats9[m, pl.ds(top, BAND), :] * up[l])
        for e in range(SLOTS):
            here = slice(e * ROWS, (e + 1) * ROWS)
            term = [shape_w[m, e : e + 1, :] * upstream[m] for m in range(9)]
            pull = (
                radial[pl.ds(top, BAND), here] * term[0]
                + radial[pl.ds(pl.multiple_of(CH + top, BAND), BAND), here]
                * (term[1] + term[2] + term[3])
                + radial[pl.ds(pl.multiple_of(2 * CH + top, BAND), BAND), here]
                * (term[4] + term[5] + term[6] + term[7] + term[8])
            )
            pulled[pl.ds(top, BAND), here] = pull.astype(BF16)
        return carry

    lax.fori_loop(0, CH // BAND, backward, 0)
    back = dot(pulled[...], hot[...], NT)
    grad_in = dot(ext[...], back.astype(BF16), NT)
    for d in range(4):
        to = d * SLOTS
        early[to : to + SLOTS, :] = grad_in[d * SLOTS : (d + 1) * SLOTS]


def half_point(miller):
    m0, m1, m2 = miller[0:1], miller[1:2], miller[2:3]
    sign = jnp.where(m0 < 0, -1, 1)
    m0, m1, m2 = sign * m0, sign * m1, sign * m2
    minus = m1 < 0
    turn = jnp.where(minus, -1, 1)
    plane = m0 + jnp.where(minus, TOP + 1, 0)
    return plane, turn * m1 * SIDE + (turn * m2 + TOP)


def one_hot(point):
    row = lax.broadcasted_iota(I32, (PLANE, KVEC), 0)
    return jnp.where(row == point, 1.0, 0.0).astype(BF16)


def turns(frac_row, first, count):
    width = frac_row.shape[1]
    m = (lax.broadcasted_iota(I32, (count, width), 0) + first).astype(F32)
    turn = m * frac_row
    turn = turn - jnp.floor(turn + 0.5)
    quarter = jnp.floor(turn * 4.0 + 0.5)
    arc = (turn - 0.25 * quarter) * (2.0 * math.pi)
    s2 = arc * arc
    sine = arc * (1.0 + s2 * (-1 / 6 + s2 * (1 / 120 + s2 * (-1 / 5040))))
    cosine = 1.0 + s2 * (-0.5 + s2 * (1 / 24 + s2 * (-1 / 720 + s2 * (1 / 40320))))
    odd = jnp.abs(quarter) == 1.0
    back = jnp.abs(quarter) == 2.0
    flip = jnp.where(quarter < 0.0, -1.0, 1.0)
    cos_out = jnp.where(odd, -flip * sine, jnp.where(back, -cosine, cosine))
    sin_out = jnp.where(odd, flip * cosine, jnp.where(back, -sine, sine))
    return cos_out, sin_out


def waves(frac, plane):
    width = plane.shape[1]
    c1, s1 = turns(frac[1], 0, 8)
    c2, s2 = turns(frac[2], -TOP, 16)
    for k in (0, PLANE):
        plane[k + 88 : k + PLANE, :] = jnp.zeros((PLANE - 88, width), F32)
    for m in range(TOP + 1):
        cm, sm = c1[m : m + 1], s1[m : m + 1]
        plane[m * SIDE : m * SIDE + 16, :] = cm * c2 - sm * s2
        plane[PLANE + m * SIDE : PLANE + m * SIDE + 16, :] = sm * c2 + cm * s2
    c0, s0 = turns(frac[0], 0, 8)
    return [c0[m : m + 1] for m in range(TOP + 1)] + [
        s0[m : m + 1] for m in range(1, TOP + 1)
    ]


def lattice_kernel(place, miller, filter_weight, folded, turned, wide):
    plane, point = half_point(miller[...])
    turned[...] = filter_weight[...].T * (1.0 / math.sqrt(KVEC * ATOMS))
    mine = turned[pl.ds(pl.multiple_of(place[5], QUARTER), QUARTER), :]
    for b in range(2 * (TOP + 1)):
        here = slice(b * QUARTER, (b + 1) * QUARTER)
        wide[here, :] = jnp.where(plane == b, mine, 0.0).astype(BF16)
    sums = dot(wide[...], one_hot(point), NT)
    half = (TOP + 1) * QUARTER
    for m in range(TOP + 1):
        here = slice(m * QUARTER, (m + 1) * QUARTER)
        there = slice(half + m * QUARTER, half + (m + 1) * QUARTER)
        lanes = slice(m * PLANE, (m + 1) * PLANE)
        folded[0:QUARTER, lanes] = sums[here] + sums[there]
        folded[QUARTER : 2 * QUARTER, lanes] = sums[here] - sums[there]


def by_lane_group(pieces):
    group = lax.broadcasted_iota(I32, pieces[0].shape, 1) // 8
    for bit in (1, 2, 4, 8):
        low = group & bit == 0
        pieces = [
            jnp.where(low, piece, pltpu.roll(pieces[n + bit], 8 * bit, 1))
            if n & bit == 0
            else jnp.where(low, pltpu.roll(pieces[n - bit], CH - 8 * bit, 1), piece)
            for n, piece in enumerate(pieces)
        ]
    return pieces


def blocks(x, m):
    at = 2 * m * PLANE
    cc, cs = x[:, at : at + PLANE], x[:, at + PLANE : at + 2 * PLANE]
    if m == 0:
        return cc, None, None, cs
    at = 2 * (TOP + m) * PLANE
    sc, ss = x[:, at : at + PLANE], x[:, at + PLANE : at + 2 * PLANE]
    return cc, ss, sc, cs


def filtered(plus, minus, x):
    first, second = [], []
    for m in range(TOP + 1):
        here = slice(m * PLANE, (m + 1) * PLANE)
        p, d = plus[:, here], minus[:, here]
        cc, ss, sc, cs = blocks(x, m)
        if m == 0:
            first += [p * cc, p * cs]
        else:
            first += [p * cc - d * ss, p * cs + d * sc]
            second += [p * sc + d * cs, p * ss - d * cc]
    return first + second


def spectrum_kernel(
    place, gathered, folded, miller, early, parts, ewald, factor, frac, values, plane, wide
):
    for p in range(SLABS):
        here = slice(p * ROWS, (p + 1) * ROWS)
        values[:, here] = gathered[p]
        tail = gathered[p, HID_AT:PAY].astype(F32)
        frac[0:3, here] = tail[MINE : MINE + 3] + tail[MINE + 3 : MINE + 6]
    along = waves([frac[d : d + 1, :] for d in range(3)], plane)
    live = (lax.broadcasted_iota(I32, (1, ATOMS), 1) < place[0] + place[1]).astype(F32)
    around = plane[...].astype(BF16)
    for low, high in ((0, TOP + 1), (TOP + 1, WAVES)):
        for f in range(low, high):
            wide[f * PAY : (f + 1) * PAY, :] = (
                values[...].astype(F32) * (along[f] * live)
            ).astype(BF16)
        both = dot(wide[low * PAY : high * PAY, :], around, NT)
        for f in range(low, high):
            here = slice(f * 2 * PLANE, (f + 1) * 2 * PLANE)
            factor[:, here] = both[(f - low) * PAY : (f - low + 1) * PAY]

    at = pl.multiple_of(place[4] - place[5], MINE)
    s = factor[HID_AT : HID_AT + MINE, :]
    g = factor[pl.ds(pl.multiple_of(COT_AT + at, MINE), MINE), :]
    plus = folded[pl.ds(at, MINE), :]
    minus = folded[pl.ds(pl.multiple_of(QUARTER + at, MINE), MINE), :]
    pair_plus, pair_minus = [], []
    for m in range(TOP + 1):
        cc, ss, sc, cs = blocks(s, m)
        gcc, gss, gsc, gcs = blocks(g, m)
        even, odd = cc * gcc + cs * gcs, 0.0
        if m > 0:
            even = even + ss * gss + sc * gsc
            odd = sc * gcs + cs * gsc - cc * gss - ss * gcc
        pair_plus.append(even + odd)
        pair_minus.append(even - odd)
    pair = jnp.concatenate(pair_plus + pair_minus, axis=0)
    pair = split(pair * (1.0 / math.sqrt(KVEC * ATOMS)))
    around_plane, point = half_point(miller[...])
    found = dot(jnp.concatenate(pair, axis=0), one_hot(point), NN)
    planes = 2 * (TOP + 1)
    pair = jnp.zeros((MINE, KVEC), F32)
    for b in range(planes):
        value = found[b * MINE : (b + 1) * MINE] + found[(planes + b) * MINE : (planes + b + 1) * MINE]
        pair = jnp.where(around_plane == b, value, pair)
    pair = by_lane_group([pair[:, d * ROWS : (d + 1) * ROWS] for d in range(SLABS)])
    grad = filtered(
        folded[0:QUARTER, :],
        folded[QUARTER : 2 * QUARTER, :],
        factor[COT_AT:HID_AT, :],
    )
    grad = jnp.concatenate(split(jnp.concatenate(grad, axis=1)), axis=0)
    block = dot(grad, factor[0:QUARTER, :].astype(BF16), NT)
    block = block[0:QUARTER] + block[QUARTER : 2 * QUARTER]
    block = jnp.concatenate([block[8 * q : 8 * q + 8] for q in range(4)], axis=1)
    for d in range(STRUCTS):
        parts[d, 0:16, :] = jnp.concatenate(
            [pair[d], block], axis=0
        ).astype(BF16)
        parts[d, 16:48, :] = early[d * SLOTS : (d + 1) * SLOTS, :].astype(BF16)
    coef = filtered(plus, minus, s)
    coef = [
        jnp.concatenate([coef[2 * f], coef[2 * f + 1]], axis=1) for f in range(WAVES)
    ]
    field = dot(jnp.concatenate(coef, axis=0).astype(BF16), around, NN)
    total = field[0:MINE] * along[0]
    for f in range(1, WAVES):
        total = total + field[f * MINE : (f + 1) * MINE] * along[f]
    for p in range(SLABS):
        ewald[p] = total[:, p * ROWS : (p + 1) * ROWS].astype(BF16)


SPECTRUM_SCRATCH = [
    pltpu.VMEM((PAY, BASIS), F32),
    pltpu.VMEM((8, ATOMS), F32),
    pltpu.VMEM((PAY, ATOMS), BF16),
    pltpu.VMEM((2 * PLANE, ATOMS), F32),
    pltpu.VMEM((WAVES * PAY, ATOMS), BF16),
]


def middle_kernel(place, sums, feats, local, last, grad_in, updated):
    row = lax.broadcasted_iota(I32, (8, KSHARE), 0)
    lane = lax.broadcasted_iota(I32, (8, KSHARE), 1)
    pick = jnp.where(lane == row + place[4], 1.0, 0.0).astype(BF16)
    blocks = [sums[p].astype(F32) for p in range(SLABS)]
    pairs = jnp.concatenate([block[0:8] for block in blocks], axis=0)
    picked = dot(pick, pairs.astype(BF16), NT)
    total = blocks[0][16:48]
    for block in blocks[1:]:
        total = total + block[16:48]
    out = jnp.concatenate([total, picked, picked], axis=0).astype(BF16)
    for d in range(STRUCTS):
        last[d] = out
    grads = []
    for c in range(0, CH, 8):
        at, g = c % QUARTER // 8, c // QUARTER
        eight = blocks[4 * g][8:16]
        eight = pltpu.roll(eight, (0 - at) * QUARTER % CH, 1)
        for q in range(1, 4):
            turned = pltpu.roll(blocks[4 * g + q][8:16], (q - at) * QUARTER % CH, 1)
            eight = jnp.where(lane < q * QUARTER, eight, turned)
        grads.append(eight)
    grad_in[...] = jnp.concatenate(grads, axis=0).T
    ewald = jnp.concatenate([block[48:56] for block in blocks], axis=0)
    here = lax.broadcasted_iota(I32, (CH, ROWS), 1) < place[1]
    updated[0] = jnp.where(
        here, feats[0].astype(F32) + local[...] + ewald, 0.0
    ).astype(BF16)


def finish_kernel(sums, ewald_in, grad_filter, grad_in, grad_out):
    for d in range(STRUCTS):
        late = sums[d, 32:48].astype(F32)
        grad_filter[8 * d : 8 * d + 8, :] = late[0:8]
    for d in range(4):
        here = slice(d * SLOTS, (d + 1) * SLOTS)
        grad_in[here, :] = ewald_in[here, :] + sums[d, 0:32].astype(F32)
    for d in range(4, STRUCTS):
        grad_out[(d - 4) * SLOTS : (d - 3) * SLOTS, :] = sums[d, 0:32].astype(F32)


def exchange(x, axis):
    return lax.all_to_all(x, axis, 0, 0)


def shards(
    node_feats,
    frac,
    neighbours,
    images,
    neighbour_count,
    atom_count,
    miller,
    in_weight,
    radial_weight,
    out_weight,
    filter_weight,
    cotangent,
):
    slab = lax.axis_index("atom")
    first = slab * ROWS
    live = atom_count[0] - jnp.stack(
        [first, (first - ROWS) % ATOMS, (first + ROWS) % ATOMS]
    )
    place = jnp.stack([slab * MINE, slab // 4 * QUARTER, slab % 2])
    place = jnp.concatenate([first[None], live, place]).astype(I32)
    struct = jax.ShapeDtypeStruct

    halo, payload = call(
        pack_kernel,
        [
            (VMEM, struct((HALO, ROWS), BF16)),
            (HBM, struct((SLABS, PAY, ROWS), BF16)),
        ],
        [
            pltpu.VMEM((1, CH, ROWS), BF16),
            pltpu.VMEM((1, CH, ROWS), BF16),
            pltpu.VMEM((3, 1, ROWS), F32),
            pltpu.VMEM((CH, CH), BF16),
            pltpu.VMEM((SLABS, PAY, ROWS), BF16),
            pltpu.VMEM((16, ROWS), F32),
            pltpu.SemaphoreType.DMA((5,)),
        ],
        60,
        10**6,
        (HBM, node_feats),
        (HBM, cotangent),
        (HBM, frac.transpose(1, 0, 2)),
        (HBM, in_weight),
    )
    evens = range(0, SLABS, 2)
    pairs = [(n, n + 1) for n in evens], [(n + 1, (n + 2) % SLABS) for n in evens]
    first_swap, second_swap = (
        lax.ppermute(halo, "atom", [*pair, *((j, i) for i, j in pair)]) for pair in pairs
    )
    gathered = exchange(payload, "atom")

    early, local = call(
        edge_kernel,
        [(VMEM, struct((4 * CH, CH), F32)), (VMEM, struct((CH, ROWS), F32))],
        [
            pltpu.VMEM((CH, 2 * ROWS), BF16),
            pltpu.VMEM((2 * ROWS, EDGES), BF16),
            pltpu.VMEM((32, 3 * CH), F32),
            pltpu.VMEM((32, EDGES), F32),
            pltpu.VMEM((3 * CH, EDGES), F32),
            pltpu.VMEM((CH, EDGES), F32),
            pltpu.VMEM((9, SLOTS, ROWS), F32),
            pltpu.VMEM((SLOTS, ROWS), F32),
            pltpu.VMEM((9, CH, ROWS), F32),
            pltpu.VMEM((3 * CH, ROWS), F32),
            pltpu.VMEM((CH, EDGES), BF16),
            pltpu.VMEM((3 * CH, ROWS), BF16),
        ],
        20,
        EDGE_COST,
        (SMEM, place),
        (VMEM, halo),
        (VMEM, first_swap),
        (VMEM, second_swap),
        (VMEM, neighbours),
        (VMEM, images),
        (VMEM, neighbour_count),
        (VMEM, in_weight),
        (VMEM, radial_weight),
        (VMEM, out_weight),
        (VMEM, cotangent),
    )
    early, miller = lax.optimization_barrier((early, miller))
    (folded,) = call(
        lattice_kernel,
        [(VMEM, struct((2 * QUARTER, HALF), F32))],
        [
            pltpu.VMEM((CH, KVEC), F32),
            pltpu.VMEM((2 * (TOP + 1) * QUARTER, KVEC), BF16),
        ],
        12,
        10**8,
        (SMEM, place),
        (VMEM, miller),
        (VMEM, filter_weight),
    )
    parts, ewald = call(
        spectrum_kernel,
        [
            (VMEM, struct((STRUCTS, 48, CH), BF16)),
            (VMEM, struct((SLABS, MINE, ROWS), BF16)),
        ],
        SPECTRUM_SCRATCH,
        20,
        10**10,
        (SMEM, place),
        (VMEM, gathered),
        (VMEM, folded),
        (VMEM, miller),
        (VMEM, early),
    )
    sums = exchange(parts, "dp").astype(F32).sum(axis=0).astype(BF16)
    sums = jnp.broadcast_to(sums[None], (SLABS, 48, CH))
    last, ewald_in, updated = call(
        middle_kernel,
        [
            (VMEM, struct((STRUCTS, 48, CH), BF16)),
            (VMEM, struct((CH, CH), F32)),
            (VMEM, struct((1, CH, ROWS), BF16)),
        ],
        [],
        16,
        10**6,
        (SMEM, place),
        (VMEM, exchange(jnp.concatenate([sums, ewald], axis=1), "atom")),
        (VMEM, node_feats),
        (VMEM, local),
    )
    grads = call(
        finish_kernel,
        [
            (VMEM, struct((KSHARE, CH), F32)),
            (VMEM, struct((CH, CH), F32)),
            (VMEM, struct((3 * CH, CH), F32)),
        ],
        [],
        16,
        10**6,
        (VMEM, exchange(last, "dp")),
        (VMEM, ewald_in),
    )
    return (updated, *grads)


def solution(mesh):
    return jax.shard_map(
        shards,
        mesh=mesh,
        in_specs=(
            P("dp", None, "atom"),
            P("dp", None, "atom"),
            P("dp", None, "atom"),
            P("dp", None, "atom"),
            P("dp", "atom"),
            P("dp"),
            P(),
            P(),
            P(),
            P(),
            P(),
            P("dp", None, "atom"),
        ),
        out_specs=(P("dp", None, "atom"), P("atom", None), P(), P()),
        check_vma=False,
    )
```

```python
import math

import jax
import jax.numpy as jnp
from jax import lax
from jax.experimental import pallas as pl
from jax.experimental.pallas import tpu as pltpu
from jax.sharding import PartitionSpec as P

F32 = jnp.float32
BF16 = jnp.bfloat16
I32 = jnp.int32

CH = 128
ROWS = 128
SLABS = 16
STRUCTS = 16
ATOMS = ROWS * SLABS
SLOTS = 32
EDGES = SLOTS * ROWS
GHOST = 32
KVEC = 2048
KSHARE = KVEC // SLABS
NB = 8
TOP = 6
SIDE = 2 * TOP + 1
PLANE = 128
HALF = (TOP + 1) * PLANE
WAVES = SIDE
BASIS = WAVES * 2 * PLANE
TILE = 256
MINE = CH // SLABS
QUARTER = CH // 4
FRAC_AT = CH
HALO = CH + 16
COT_AT, HID_AT, PAY = QUARTER, 2 * QUARTER, 2 * QUARTER + 16

VMEM = pl.BlockSpec(memory_space=pltpu.VMEM)
HBM = pl.BlockSpec(memory_space=pltpu.HBM)

NN = (((1,), (0,)), ((), ()))
NT = (((1,), (1,)), ((), ()))
TN = (((0,), (0,)), ((), ()))


def dot(a, b, dims):
    return lax.dot_general(a, b, dims, preferred_element_type=F32)


def split(x):
    hi = x.astype(BF16)
    return hi, (x - hi.astype(F32)).astype(BF16)


def call(kernel, outs, scratch, mib, flops, *args):
    return pl.pallas_call(
        kernel,
        out_shape=[shape for _, shape in outs],
        in_specs=[spec for spec, _ in args],
        out_specs=[spec for spec, _ in outs],
        scratch_shapes=scratch,
        compiler_params=pltpu.CompilerParams(vmem_limit_bytes=mib * 2**20),
        cost_estimate=pl.CostEstimate(
            flops=flops, bytes_accessed=2**16, transcendentals=0
        ),
    )(*[arg for _, arg in args])


def pack_kernel(
    feats_hbm, cot_hbm, frac_hbm, weight_hbm, count_hbm, halo, payload_hbm, feats, cot, frac, weight, count, payload, rows, sems
):
    pairs = (
        (frac_hbm, frac),
        (feats_hbm, feats),
        (weight_hbm, weight),
        (cot_hbm, cot),
        (count_hbm, count),
    )
    copies = [
        pltpu.make_async_copy(src, dst, sems.at[n]) for n, (src, dst) in enumerate(pairs)
    ]
    for copy in copies:
        copy.start()
    copies[0].wait()
    rows[...] = jnp.zeros((16, ROWS), F32)
    for d in range(3):
        first = jnp.floor(frac[d] * 256.0) * (1.0 / 256.0)
        rows[d : d + 1, :] = first
        rows[d + 3 : d + 4, :] = frac[d] - first
    copies[4].wait()
    rows[6:7, :] = jnp.broadcast_to((count[...] >> 4).astype(F32), (1, ROWS))
    rows[7:8, :] = jnp.broadcast_to((count[...] & 15).astype(F32), (1, ROWS))
    where = rows[...]
    halo[FRAC_AT:HALO] = where.astype(BF16)
    copies[1].wait()
    halo[0:CH] = feats[0]
    for a in range(SLABS):
        payload[a, 0:COT_AT] = feats[0, a % 4 * QUARTER : (a % 4 + 1) * QUARTER]
    copies[2].wait()
    hidden = dot(weight[...], feats[0], TN)
    for a in range(SLABS):
        payload[a, HID_AT:PAY] = jnp.concatenate(
            [hidden[a * MINE : (a + 1) * MINE], where[0:8]], axis=0
        ).astype(BF16)
    copies[3].wait()
    for a in range(SLABS):
        payload[a, COT_AT:HID_AT] = cot[0, a // 4 * QUARTER : (a // 4 + 1) * QUARTER]
    sent = pltpu.make_async_copy(payload, payload_hbm, sems.at[5])
    sent.start()
    sent.wait()


def joined_count(rows):
    wide = rows.astype(F32)
    return 16.0 * wide[6:7] + wide[7:8]


def joined_frac(rows):
    wide = rows.astype(F32)
    return [wide[d : d + 1] + wide[d + 3 : d + 4] for d in range(3)]


ROOT3, ROOT5, ROOT15 = math.sqrt(3.0), math.sqrt(5.0), math.sqrt(15.0)
STEP = 1.75 / (NB - 1)
BAND = 16
EDGE_COST = 10**10


def edge_kernel(
    own,
    first_swap,
    second_swap,
    neighbours,
    images,
    count,
    in_weight,
    radial_weight,
    out_weight,
    cot,
    early,
    local,
    ext,
    hot,
    weights,
    basis,
    radial,
    moved,
    shape_w,
    length,
    feats9,
    up9,
    pulled,
    inv,
):
    slab = lax.axis_index("atom")
    first = slab * ROWS
    atoms = joined_count(own[FRAC_AT:HALO]).astype(I32)
    live_here = atoms - first
    live_left = atoms - ((first - ROWS) & (ATOMS - 1))
    live_right = atoms - ((first + ROWS) & (ATOMS - 1))
    lane = lax.broadcasted_iota(I32, (CH, ROWS), 1)
    ext[:, 0:ROWS] = jnp.where(lane < live_here, own[0:CH].astype(F32), 0.0).astype(BF16)
    even = (slab & 1) == 0
    swaps = first_swap[...].astype(F32), second_swap[...].astype(F32)
    right = jnp.where(even, swaps[0], swaps[1])
    left = jnp.where(even, swaps[1], swaps[0])
    near_right = jnp.where(lane < live_right, right[0:CH], 0.0)
    near_left = jnp.where(lane < live_left, left[0:CH], 0.0)
    ext[:, ROWS : 2 * ROWS] = jnp.where(lane < GHOST, near_right, near_left).astype(BF16)
    hidden = dot(in_weight[...], ext[...], TN).astype(BF16)

    offset = (neighbours[0] - first) & (ATOMS - 1)
    column = jnp.where(offset < ROWS + GHOST, offset, offset - (ATOMS - 2 * ROWS))
    at = column & (ROWS - 1)
    in_slab = column < ROWS
    frac_own = joined_frac(own[FRAC_AT:HALO])
    frac_left = joined_frac(left[FRAC_AT:HALO])
    frac_right = joined_frac(right[FRAC_AT:HALO])
    lane1 = lax.broadcasted_iota(I32, (1, ROWS), 1)

    code = images[0]
    ninth = (code * 57) >> 9
    third = (code * 171) >> 9
    shifts = (ninth, third - 3 * ninth, code - 3 * third)
    vector = []
    for d in range(3):
        near = jnp.broadcast_to(frac_own[d], (SLOTS, ROWS))
        far = jnp.where(lane1 < GHOST, frac_right[d], frac_left[d])
        far = jnp.broadcast_to(far, (SLOTS, ROWS))
        other = jnp.where(
            in_slab,
            jnp.take_along_axis(near, at, axis=1),
            jnp.take_along_axis(far, at, axis=1),
        )
        vector.append(0.5 * (other - near + (shifts[d].astype(F32) - 1.0)))
    x, y, z = vector
    square = x * x + y * y + z * z
    slot = lax.broadcasted_iota(I32, (SLOTS, ROWS), 0)
    lane32 = lax.broadcasted_iota(I32, (SLOTS, ROWS), 1)
    used = (slot < count[...]) & (lane32 < live_here)
    weight = jnp.where(used, SLOTS**-0.5, 0.0)
    harmonics = (
        weight,
        weight * (ROOT3 * x),
        weight * (ROOT3 * y),
        weight * (ROOT3 * z),
        weight * (ROOT15 * x * y),
        weight * (ROOT15 * y * z),
        weight * (0.5 * ROOT5 * (3.0 * z * z - square)),
        weight * (ROOT15 * x * z),
        weight * (0.5 * ROOT15 * (x * x - y * y)),
    )
    for m in range(9):
        shape_w[m] = harmonics[m]
    length[...] = jnp.sqrt(square)

    rows256 = lax.broadcasted_iota(I32, (2 * ROWS, ROWS), 0)
    centre = lax.broadcasted_iota(I32, (NB, ROWS), 0).astype(F32) * STEP
    basis[24:32, :] = jnp.zeros((8, EDGES), F32)
    for e in range(SLOTS):
        here = slice(e * ROWS, (e + 1) * ROWS)
        hot[:, here] = jnp.where(rows256 == column[e : e + 1], 1.0, 0.0).astype(BF16)
        gap = (length[e : e + 1, :] - centre) * (1.0 / STEP)
        gauss = jnp.exp(-(gap * gap))
        hi, lo = split(gauss)
        basis[0:8, here] = hi.astype(F32)
        basis[8:16, here] = lo.astype(F32)
        basis[16:24, here] = hi.astype(F32)
    weights[...] = jnp.zeros((32, 3 * CH), F32)
    for l in range(3):
        hi, lo = split(radial_weight[l])
        part = slice(l * CH, (l + 1) * CH)
        weights[0:8, part] = hi.astype(F32)
        weights[8:16, part] = hi.astype(F32)
        weights[16:24, part] = lo.astype(F32)
    radial[...] = dot(weights[...].astype(BF16), basis[...].astype(BF16), TN)
    moved[...] = dot(hidden, hot[...], NN)

    def forward(step, carry):
        top = pl.multiple_of(step * BAND, BAND)
        total = [jnp.zeros((BAND, ROWS), F32) for _ in range(9)]
        for e in range(SLOTS):
            here = slice(e * ROWS, (e + 1) * ROWS)
            value = moved[pl.ds(top, BAND), here]
            parts = [
                radial[pl.ds(pl.multiple_of(l * CH + top, BAND), BAND), here] * value
                for l in range(3)
            ]
            for m in range(9):
                l = 0 if m == 0 else (1 if m < 4 else 2)
                total[m] = total[m] + shape_w[m, e : e + 1, :] * parts[l]
        for m in range(9):
            feats9[m, pl.ds(top, BAND), :] = total[m]
        squares = [t * t for t in total]
        inv[pl.ds(top, BAND), :] = squares[0].astype(BF16)
        inv[pl.ds(pl.multiple_of(CH + top, BAND), BAND), :] = (
            squares[1] + squares[2] + squares[3]
        ).astype(BF16)
        inv[pl.ds(pl.multiple_of(2 * CH + top, BAND), BAND), :] = (
            squares[4] + squares[5] + squares[6] + squares[7] + squares[8]
        ).astype(BF16)
        return carry

    lax.fori_loop(0, CH // BAND, forward, 0)

    masked = jnp.where(lane < live_here, cot[0].astype(F32), 0.0).astype(BF16)
    local[...] = dot(out_weight[...], inv[...], TN)
    up9[...] = 2.0 * dot(out_weight[...], masked, NN)
    grad_out = dot(inv[...], masked, NT)
    for d in range(4, STRUCTS):
        to = d * SLOTS
        early[to : to + SLOTS, :] = grad_out[(d - 4) * SLOTS : (d - 3) * SLOTS]

    def backward(step, carry):
        top = pl.multiple_of(step * BAND, BAND)
        up = [
            up9[pl.ds(pl.multiple_of(l * CH + top, BAND), BAND), :] for l in range(3)
        ]
        upstream = []
        for m in range(9):
            l = 0 if m == 0 else (1 if m < 4 else 2)
            upstream.append(feats9[m, pl.ds(top, BAND), :] * up[l])
        for e in range(SLOTS):
            here = slice(e * ROWS, (e + 1) * ROWS)
            term = [shape_w[m, e : e + 1, :] * upstream[m] for m in range(9)]
            pull = (
                radial[pl.ds(top, BAND), here] * term[0]
                + radial[pl.ds(pl.multiple_of(CH + top, BAND), BAND), here]
                * (term[1] + term[2] + term[3])
                + radial[pl.ds(pl.multiple_of(2 * CH + top, BAND), BAND), here]
                * (term[4] + term[5] + term[6] + term[7] + term[8])
            )
            pulled[pl.ds(top, BAND), here] = pull.astype(BF16)
        return carry

    lax.fori_loop(0, CH // BAND, backward, 0)
    back = dot(pulled[...], hot[...], NT)
    grad_in = dot(ext[...], back.astype(BF16), NT)
    for d in range(4):
        to = d * SLOTS
        early[to : to + SLOTS, :] = grad_in[d * SLOTS : (d + 1) * SLOTS]


def half_point(miller):
    m0, m1, m2 = miller[0:1], miller[1:2], miller[2:3]
    sign = jnp.where(m0 < 0, -1, 1)
    m0, m1, m2 = sign * m0, sign * m1, sign * m2
    minus = m1 < 0
    turn = jnp.where(minus, -1, 1)
    plane = m0 + jnp.where(minus, TOP + 1, 0)
    return plane, turn * m1 * SIDE + (turn * m2 + TOP)


def one_hot(point):
    row = lax.broadcasted_iota(I32, (PLANE, KVEC), 0)
    return jnp.where(row == point, 1.0, 0.0).astype(BF16)


def turns(frac_row, first, count):
    width = frac_row.shape[1]
    m = (lax.broadcasted_iota(I32, (count, width), 0) + first).astype(F32)
    turn = m * frac_row
    turn = turn - jnp.floor(turn + 0.5)
    quarter = jnp.floor(turn * 4.0 + 0.5)
    arc = (turn - 0.25 * quarter) * (2.0 * math.pi)
    s2 = arc * arc
    sine = arc * (1.0 + s2 * (-1 / 6 + s2 * (1 / 120 + s2 * (-1 / 5040))))
    cosine = 1.0 + s2 * (-0.5 + s2 * (1 / 24 + s2 * (-1 / 720 + s2 * (1 / 40320))))
    odd = jnp.abs(quarter) == 1.0
    back = jnp.abs(quarter) == 2.0
    flip = jnp.where(quarter < 0.0, -1.0, 1.0)
    cos_out = jnp.where(odd, -flip * sine, jnp.where(back, -cosine, cosine))
    sin_out = jnp.where(odd, flip * cosine, jnp.where(back, -sine, sine))
    return cos_out, sin_out


def waves(frac, plane):
    width = plane.shape[1]
    c1, s1 = turns(frac[1], 0, 8)
    c2, s2 = turns(frac[2], -TOP, 16)
    for k in (0, PLANE):
        plane[k + 88 : k + PLANE, :] = jnp.zeros((PLANE - 88, width), F32)
    for m in range(TOP + 1):
        cm, sm = c1[m : m + 1], s1[m : m + 1]
        plane[m * SIDE : m * SIDE + 16, :] = cm * c2 - sm * s2
        plane[PLANE + m * SIDE : PLANE + m * SIDE + 16, :] = sm * c2 + cm * s2
    c0, s0 = turns(frac[0], 0, 8)
    return [c0[m : m + 1] for m in range(TOP + 1)] + [
        s0[m : m + 1] for m in range(1, TOP + 1)
    ]


def lattice_kernel(miller, filter_weight, folded, turned, wide):
    plane, point = half_point(miller[...])
    turned[...] = filter_weight[...].T * (1.0 / math.sqrt(KVEC * ATOMS))
    quarter = lax.axis_index("atom") >> 2
    mine = turned[pl.ds(pl.multiple_of(quarter * QUARTER, QUARTER), QUARTER), :]
    for b in range(2 * (TOP + 1)):
        here = slice(b * QUARTER, (b + 1) * QUARTER)
        wide[here, :] = jnp.where(plane == b, mine, 0.0).astype(BF16)
    sums = dot(wide[...], one_hot(point), NT)
    half = (TOP + 1) * QUARTER
    for m in range(TOP + 1):
        here = slice(m * QUARTER, (m + 1) * QUARTER)
        there = slice(half + m * QUARTER, half + (m + 1) * QUARTER)
        lanes = slice(m * PLANE, (m + 1) * PLANE)
        folded[0:QUARTER, lanes] = sums[here] + sums[there]
        folded[QUARTER : 2 * QUARTER, lanes] = sums[here] - sums[there]


def by_lane_group(pieces):
    group = lax.broadcasted_iota(I32, pieces[0].shape, 1) // 8
    for bit in (1, 2, 4, 8):
        low = group & bit == 0
        pieces = [
            jnp.where(low, piece, pltpu.roll(pieces[n + bit], 8 * bit, 1))
            if n & bit == 0
            else jnp.where(low, pltpu.roll(pieces[n - bit], CH - 8 * bit, 1), piece)
            for n, piece in enumerate(pieces)
        ]
    return pieces


def blocks(x, m):
    at = 2 * m * PLANE
    cc, cs = x[:, at : at + PLANE], x[:, at + PLANE : at + 2 * PLANE]
    if m == 0:
        return cc, None, None, cs
    at = 2 * (TOP + m) * PLANE
    sc, ss = x[:, at : at + PLANE], x[:, at + PLANE : at + 2 * PLANE]
    return cc, ss, sc, cs


def filtered(plus, minus, x):
    first, second = [], []
    for m in range(TOP + 1):
        here = slice(m * PLANE, (m + 1) * PLANE)
        p, d = plus[:, here], minus[:, here]
        cc, ss, sc, cs = blocks(x, m)
        if m == 0:
            first += [p * cc, p * cs]
        else:
            first += [p * cc - d * ss, p * cs + d * sc]
            second += [p * sc + d * cs, p * ss - d * cc]
    return first + second


def spectrum_kernel(
    gathered, folded, miller, early, parts, ewald, factor, frac, values, plane, wide
):
    for p in range(SLABS):
        here = slice(p * ROWS, (p + 1) * ROWS)
        values[:, here] = gathered[p]
        tail = gathered[p, HID_AT:PAY].astype(F32)
        frac[0:3, here] = tail[MINE : MINE + 3] + tail[MINE + 3 : MINE + 6]
    along = waves([frac[d : d + 1, :] for d in range(3)], plane)
    atoms = joined_count(gathered[0, HID_AT:PAY].astype(F32)[MINE:16]).astype(I32)
    live = lax.broadcasted_iota(I32, (1, ATOMS), 1) < atoms[:, 0:1]
    live = jnp.where(live, 1.0, 0.0)
    around = plane[...].astype(BF16)
    for low, high in ((0, TOP + 1), (TOP + 1, WAVES)):
        for f in range(low, high):
            wide[f * PAY : (f + 1) * PAY, :] = (
                values[...].astype(F32) * (along[f] * live)
            ).astype(BF16)
        both = dot(wide[low * PAY : high * PAY, :], around, NT)
        for f in range(low, high):
            here = slice(f * 2 * PLANE, (f + 1) * 2 * PLANE)
            factor[:, here] = both[(f - low) * PAY : (f - low + 1) * PAY]

    at = pl.multiple_of((lax.axis_index("atom") & 3) * MINE, MINE)
    s = factor[HID_AT : HID_AT + MINE, :]
    g = factor[pl.ds(pl.multiple_of(COT_AT + at, MINE), MINE), :]
    plus = folded[pl.ds(at, MINE), :]
    minus = folded[pl.ds(pl.multiple_of(QUARTER + at, MINE), MINE), :]
    pair_plus, pair_minus = [], []
    for m in range(TOP + 1):
        cc, ss, sc, cs = blocks(s, m)
        gcc, gss, gsc, gcs = blocks(g, m)
        even, odd = cc * gcc + cs * gcs, 0.0
        if m > 0:
            even = even + ss * gss + sc * gsc
            odd = sc * gcs + cs * gsc - cc * gss - ss * gcc
        pair_plus.append(even + odd)
        pair_minus.append(even - odd)
    pair = jnp.concatenate(pair_plus + pair_minus, axis=0)
    pair = split(pair * (1.0 / math.sqrt(KVEC * ATOMS)))
    around_plane, point = half_point(miller[...])
    found = dot(jnp.concatenate(pair, axis=0), one_hot(point), NN)
    planes = 2 * (TOP + 1)
    pair = jnp.zeros((MINE, KVEC), F32)
    for b in range(planes):
        value = found[b * MINE : (b + 1) * MINE] + found[(planes + b) * MINE : (planes + b + 1) * MINE]
        pair = jnp.where(around_plane == b, value, pair)
    pair = by_lane_group([pair[:, d * ROWS : (d + 1) * ROWS] for d in range(SLABS)])
    grad = filtered(
        folded[0:QUARTER, :],
        folded[QUARTER : 2 * QUARTER, :],
        factor[COT_AT:HID_AT, :],
    )
    grad = jnp.concatenate(split(jnp.concatenate(grad, axis=1)), axis=0)
    block = dot(grad, factor[0:QUARTER, :].astype(BF16), NT)
    block = block[0:QUARTER] + block[QUARTER : 2 * QUARTER]
    block = jnp.concatenate([block[8 * q : 8 * q + 8] for q in range(4)], axis=1)
    for d in range(STRUCTS):
        parts[d, 0:16, :] = jnp.concatenate(
            [pair[d], block], axis=0
        ).astype(BF16)
        parts[d, 16:48, :] = early[d * SLOTS : (d + 1) * SLOTS, :].astype(BF16)
    coef = filtered(plus, minus, s)
    coef = [
        jnp.concatenate([coef[2 * f], coef[2 * f + 1]], axis=1) for f in range(WAVES)
    ]
    field = dot(jnp.concatenate(coef, axis=0).astype(BF16), around, NN)
    total = field[0:MINE] * along[0]
    for f in range(1, WAVES):
        total = total + field[f * MINE : (f + 1) * MINE] * along[f]
    for p in range(SLABS):
        ewald[p] = total[:, p * ROWS : (p + 1) * ROWS].astype(BF16)


SPECTRUM_SCRATCH = [
    pltpu.VMEM((PAY, BASIS), F32),
    pltpu.VMEM((8, ATOMS), F32),
    pltpu.VMEM((PAY, ATOMS), BF16),
    pltpu.VMEM((2 * PLANE, ATOMS), F32),
    pltpu.VMEM((WAVES * PAY, ATOMS), BF16),
]


def middle_kernel(sums, own, local, last, grad_in, field):
    row = lax.broadcasted_iota(I32, (8, KSHARE), 0)
    lane = lax.broadcasted_iota(I32, (8, KSHARE), 1)
    pick = jnp.where(lane == row + MINE * lax.axis_index("atom"), 1.0, 0.0).astype(BF16)
    blocks = [sums[p].astype(F32) for p in range(SLABS)]
    pairs = jnp.concatenate([block[0:8] for block in blocks], axis=0)
    picked = dot(pick, pairs.astype(BF16), NT)
    total = blocks[0][16:48]
    for block in blocks[1:]:
        total = total + block[16:48]
    out = jnp.concatenate([total, picked, picked], axis=0).astype(BF16)
    for d in range(STRUCTS):
        last[d] = out
    grads = []
    for c in range(0, CH, 8):
        at, g = c % QUARTER // 8, c // QUARTER
        eight = blocks[4 * g][8:16]
        eight = pltpu.roll(eight, (0 - at) * QUARTER % CH, 1)
        for q in range(1, 4):
            turned = pltpu.roll(blocks[4 * g + q][8:16], (q - at) * QUARTER % CH, 1)
            eight = jnp.where(lane < q * QUARTER, eight, turned)
        grads.append(eight)
    grad_in[...] = jnp.concatenate(grads, axis=0).T
    ewald = jnp.concatenate([block[48:56] for block in blocks], axis=0)
    live = joined_count(own[FRAC_AT:HALO]).astype(I32) - lax.axis_index("atom") * ROWS
    live = lax.broadcasted_iota(I32, (CH, ROWS), 1) < live
    field[...] = jnp.where(live, own[0:CH].astype(F32) + local[...] + ewald, 0.0)


def finish_kernel(
    sums, ewald_in, field, updated, grad_filter, grad_in, grad_out
):
    updated[0] = field[...].astype(BF16)
    for d in range(STRUCTS):
        late = sums[d, 32:48].astype(F32)
        grad_filter[8 * d : 8 * d + 8, :] = late[0:8]
    for d in range(4):
        here = slice(d * SLOTS, (d + 1) * SLOTS)
        grad_in[here, :] = ewald_in[here, :] + sums[d, 0:32].astype(F32)
    for d in range(4, STRUCTS):
        grad_out[(d - 4) * SLOTS : (d - 3) * SLOTS, :] = sums[d, 0:32].astype(F32)


def exchange(x, axis):
    return lax.all_to_all(x, axis, 0, 0)


def shards(
    node_feats,
    frac,
    neighbours,
    images,
    neighbour_count,
    atom_count,
    miller,
    in_weight,
    radial_weight,
    out_weight,
    filter_weight,
    cotangent,
):
    struct = jax.ShapeDtypeStruct

    halo, payload = call(
        pack_kernel,
        [
            (VMEM, struct((HALO, ROWS), BF16)),
            (HBM, struct((SLABS, PAY, ROWS), BF16)),
        ],
        [
            pltpu.VMEM((1, CH, ROWS), BF16),
            pltpu.VMEM((1, CH, ROWS), BF16),
            pltpu.VMEM((3, 1, ROWS), F32),
            pltpu.VMEM((CH, CH), BF16),
            pltpu.VMEM((1, 1), I32),
            pltpu.VMEM((SLABS, PAY, ROWS), BF16),
            pltpu.VMEM((16, ROWS), F32),
            pltpu.SemaphoreType.DMA((6,)),
        ],
        60,
        10**6,
        (HBM, node_feats),
        (HBM, cotangent),
        (HBM, frac.transpose(1, 0, 2)),
        (HBM, in_weight),
        (HBM, atom_count.reshape(1, 1)),
    )
    evens = range(0, SLABS, 2)
    pairs = [(n, n + 1) for n in evens], [(n + 1, (n + 2) % SLABS) for n in evens]
    first_swap, second_swap = (
        lax.ppermute(halo, "atom", [*pair, *((j, i) for i, j in pair)]) for pair in pairs
    )
    gathered = exchange(payload, "atom")

    early, local = call(
        edge_kernel,
        [(VMEM, struct((4 * CH, CH), F32)), (VMEM, struct((CH, ROWS), F32))],
        [
            pltpu.VMEM((CH, 2 * ROWS), BF16),
            pltpu.VMEM((2 * ROWS, EDGES), BF16),
            pltpu.VMEM((32, 3 * CH), F32),
            pltpu.VMEM((32, EDGES), F32),
            pltpu.VMEM((3 * CH, EDGES), F32),
            pltpu.VMEM((CH, EDGES), F32),
            pltpu.VMEM((9, SLOTS, ROWS), F32),
            pltpu.VMEM((SLOTS, ROWS), F32),
            pltpu.VMEM((9, CH, ROWS), F32),
            pltpu.VMEM((3 * CH, ROWS), F32),
            pltpu.VMEM((CH, EDGES), BF16),
            pltpu.VMEM((3 * CH, ROWS), BF16),
        ],
        20,
        EDGE_COST,
        (VMEM, halo),
        (VMEM, first_swap),
        (VMEM, second_swap),
        (VMEM, neighbours),
        (VMEM, images),
        (VMEM, neighbour_count),
        (VMEM, in_weight),
        (VMEM, radial_weight),
        (VMEM, out_weight),
        (VMEM, cotangent),
    )
    early, miller = lax.optimization_barrier((early, miller))
    (folded,) = call(
        lattice_kernel,
        [(VMEM, struct((2 * QUARTER, HALF), F32))],
        [
            pltpu.VMEM((CH, KVEC), F32),
            pltpu.VMEM((2 * (TOP + 1) * QUARTER, KVEC), BF16),
        ],
        12,
        10**8,
        (VMEM, miller),
        (VMEM, filter_weight),
    )
    parts, ewald = call(
        spectrum_kernel,
        [
            (VMEM, struct((STRUCTS, 48, CH), BF16)),
            (VMEM, struct((SLABS, MINE, ROWS), BF16)),
        ],
        SPECTRUM_SCRATCH,
        20,
        10**10,
        (VMEM, gathered),
        (VMEM, folded),
        (VMEM, miller),
        (VMEM, early),
    )
    sums = exchange(parts, "dp").astype(F32).sum(axis=0).astype(BF16)
    sums = jnp.broadcast_to(sums[None], (SLABS, 48, CH))
    last, ewald_in, field = call(
        middle_kernel,
        [
            (VMEM, struct((STRUCTS, 48, CH), BF16)),
            (VMEM, struct((CH, CH), F32)),
            (VMEM, struct((CH, ROWS), F32)),
        ],
        [],
        16,
        10**6,
        (VMEM, exchange(jnp.concatenate([sums, ewald], axis=1), "atom")),
        (VMEM, halo),
        (VMEM, local),
    )
    return tuple(call(
        finish_kernel,
        [
            (VMEM, struct((1, CH, ROWS), BF16)),
            (VMEM, struct((KSHARE, CH), F32)),
            (VMEM, struct((CH, CH), F32)),
            (VMEM, struct((3 * CH, CH), F32)),
        ],
        [],
        16,
        10**6,
        (VMEM, exchange(last, "dp")),
        (VMEM, ewald_in),
        (VMEM, field),
    ))


def solution(mesh):
    return jax.shard_map(
        shards,
        mesh=mesh,
        in_specs=(
            P("dp", None, "atom"),
            P("dp", None, "atom"),
            P("dp", None, "atom"),
            P("dp", None, "atom"),
            P("dp", "atom"),
            P("dp"),
            P(),
            P(),
            P(),
            P(),
            P(),
            P("dp", None, "atom"),
        ),
        out_specs=(P("dp", None, "atom"), P("atom", None), P(), P()),
        check_vma=False,
    )
```

```python
import math

import jax
import jax.numpy as jnp
from jax import lax
from jax.experimental import pallas as pl
from jax.experimental.pallas import tpu as pltpu
from jax.sharding import PartitionSpec as P

F32 = jnp.float32
BF16 = jnp.bfloat16
I32 = jnp.int32

CH = 128
ROWS = 128
SLABS = 16
STRUCTS = 16
ATOMS = ROWS * SLABS
SLOTS = 32
EDGES = SLOTS * ROWS
GHOST = 32
KVEC = 2048
KSHARE = KVEC // SLABS
NB = 8
TOP = 6
SIDE = 2 * TOP + 1
PLANE = 128
HALF = (TOP + 1) * PLANE
WAVES = SIDE
BASIS = WAVES * 2 * PLANE
TILE = 256
MINE = CH // SLABS
QUARTER = CH // 4
FRAC_AT = CH
HALO = CH + 16
COT_AT, HID_AT, PAY = QUARTER, 2 * QUARTER, 2 * QUARTER + 16

VMEM = pl.BlockSpec(memory_space=pltpu.VMEM)
HBM = pl.BlockSpec(memory_space=pltpu.HBM)

NN = (((1,), (0,)), ((), ()))
NT = (((1,), (1,)), ((), ()))
TN = (((0,), (0,)), ((), ()))


def dot(a, b, dims):
    return lax.dot_general(a, b, dims, preferred_element_type=F32)


def split(x):
    hi = x.astype(BF16)
    return hi, (x - hi.astype(F32)).astype(BF16)


def call(kernel, outs, scratch, mib, flops, *args):
    return pl.pallas_call(
        kernel,
        out_shape=[shape for _, shape in outs],
        in_specs=[spec for spec, _ in args],
        out_specs=[spec for spec, _ in outs],
        scratch_shapes=scratch,
        compiler_params=pltpu.CompilerParams(vmem_limit_bytes=mib * 2**20),
        cost_estimate=pl.CostEstimate(
            flops=flops, bytes_accessed=2**16, transcendentals=0
        ),
    )(*[arg for _, arg in args])


def pack_kernel(
    feats_hbm, cot_hbm, frac_hbm, weight_hbm, count_hbm, halo_hbm, payload_hbm, feats, cot, frac, weight, count, halo, payload, rows, sems
):
    pairs = (
        (frac_hbm, frac),
        (feats_hbm, feats),
        (weight_hbm, weight),
        (cot_hbm, cot),
        (count_hbm, count),
    )
    copies = [
        pltpu.make_async_copy(src, dst, sems.at[n]) for n, (src, dst) in enumerate(pairs)
    ]
    for copy in copies:
        copy.start()
    copies[0].wait()
    rows[...] = jnp.zeros((16, ROWS), F32)
    for d in range(3):
        first = jnp.floor(frac[d] * 256.0) * (1.0 / 256.0)
        rows[d : d + 1, :] = first
        rows[d + 3 : d + 4, :] = frac[d] - first
    copies[4].wait()
    rows[6:7, :] = jnp.broadcast_to((count[...] >> 4).astype(F32), (1, ROWS))
    rows[7:8, :] = jnp.broadcast_to((count[...] & 15).astype(F32), (1, ROWS))
    where = rows[...]
    halo[FRAC_AT:HALO] = where.astype(BF16)
    copies[1].wait()
    halo[0:CH] = feats[0]
    sent = [pltpu.make_async_copy(halo, halo_hbm, sems.at[5])]
    sent[0].start()
    for a in range(SLABS):
        payload[a, 0:COT_AT] = feats[0, a % 4 * QUARTER : (a % 4 + 1) * QUARTER]
    copies[3].wait()
    for a in range(SLABS):
        payload[a, COT_AT:HID_AT] = cot[0, a // 4 * QUARTER : (a // 4 + 1) * QUARTER]
    parts = slice(0, HID_AT), slice(HID_AT, PAY)
    sent += [
        pltpu.make_async_copy(payload.at[:, part], payload_hbm.at[:, part], sems.at[6 + n])
        for n, part in enumerate(parts)
    ]
    sent[1].start()
    copies[2].wait()
    hidden = dot(weight[...], feats[0], TN)
    for a in range(SLABS):
        payload[a, HID_AT:PAY] = jnp.concatenate(
            [hidden[a * MINE : (a + 1) * MINE], where[0:8]], axis=0
        ).astype(BF16)
    sent[2].start()
    for copy in sent:
        copy.wait()


def joined_count(rows):
    wide = rows.astype(F32)
    return 16.0 * wide[6:7] + wide[7:8]


def joined_frac(rows):
    wide = rows.astype(F32)
    return [wide[d : d + 1] + wide[d + 3 : d + 4] for d in range(3)]


ROOT3, ROOT5, ROOT15 = math.sqrt(3.0), math.sqrt(5.0), math.sqrt(15.0)
STEP = 1.75 / (NB - 1)
BAND = 16
EDGE_COST = 10**10


def edge_kernel(
    own,
    first_swap,
    second_swap,
    neighbours,
    images,
    count,
    in_weight,
    radial_weight,
    out_weight,
    cot,
    early,
    local,
    ext,
    hot,
    weights,
    basis,
    radial,
    moved,
    shape_w,
    length,
    feats9,
    up9,
    pulled,
    inv,
):
    slab = lax.axis_index("atom")
    first = slab * ROWS
    atoms = joined_count(own[FRAC_AT:HALO]).astype(I32)
    live_here = atoms - first
    live_left = atoms - ((first - ROWS) & (ATOMS - 1))
    live_right = atoms - ((first + ROWS) & (ATOMS - 1))
    lane = lax.broadcasted_iota(I32, (CH, ROWS), 1)
    ext[:, 0:ROWS] = jnp.where(lane < live_here, own[0:CH].astype(F32), 0.0).astype(BF16)
    even = (slab & 1) == 0
    swaps = first_swap[...].astype(F32), second_swap[...].astype(F32)
    right = jnp.where(even, swaps[0], swaps[1])
    left = jnp.where(even, swaps[1], swaps[0])
    near_right = jnp.where(lane < live_right, right[0:CH], 0.0)
    near_left = jnp.where(lane < live_left, left[0:CH], 0.0)
    ext[:, ROWS : 2 * ROWS] = jnp.where(lane < GHOST, near_right, near_left).astype(BF16)
    hidden = dot(in_weight[...], ext[...], TN).astype(BF16)

    offset = (neighbours[0] - first) & (ATOMS - 1)
    column = jnp.where(offset < ROWS + GHOST, offset, offset - (ATOMS - 2 * ROWS))
    at = column & (ROWS - 1)
    in_slab = column < ROWS
    frac_own = joined_frac(own[FRAC_AT:HALO])
    frac_left = joined_frac(left[FRAC_AT:HALO])
    frac_right = joined_frac(right[FRAC_AT:HALO])
    lane1 = lax.broadcasted_iota(I32, (1, ROWS), 1)

    code = images[0]
    ninth = (code * 57) >> 9
    third = (code * 171) >> 9
    shifts = (ninth, third - 3 * ninth, code - 3 * third)
    vector = []
    for d in range(3):
        near = jnp.broadcast_to(frac_own[d], (SLOTS, ROWS))
        far = jnp.where(lane1 < GHOST, frac_right[d], frac_left[d])
        far = jnp.broadcast_to(far, (SLOTS, ROWS))
        other = jnp.where(
            in_slab,
            jnp.take_along_axis(near, at, axis=1),
            jnp.take_along_axis(far, at, axis=1),
        )
        vector.append(0.5 * (other - near + (shifts[d].astype(F32) - 1.0)))
    x, y, z = vector
    square = x * x + y * y + z * z
    slot = lax.broadcasted_iota(I32, (SLOTS, ROWS), 0)
    lane32 = lax.broadcasted_iota(I32, (SLOTS, ROWS), 1)
    used = (slot < count[...]) & (lane32 < live_here)
    column = jnp.where(used, column, -1)
    harmonics = (
        ROOT3 * x,
        ROOT3 * y,
        ROOT3 * z,
        ROOT15 * x * y,
        ROOT15 * y * z,
        0.5 * ROOT5 * (3.0 * z * z - square),
        ROOT15 * x * z,
        0.5 * ROOT15 * (x * x - y * y),
    )
    for m in range(8):
        shape_w[m] = harmonics[m]
    length[...] = jnp.sqrt(square)

    rows256 = lax.broadcasted_iota(I32, (2 * ROWS, ROWS), 0)
    centre = lax.broadcasted_iota(I32, (NB, ROWS), 0).astype(F32) * STEP
    basis[24:32, :] = jnp.zeros((8, EDGES), F32)
    for e in range(SLOTS):
        here = slice(e * ROWS, (e + 1) * ROWS)
        hot[:, here] = jnp.where(rows256 == column[e : e + 1], 1.0, 0.0).astype(BF16)
        gap = (length[e : e + 1, :] - centre) * (1.0 / STEP)
        gauss = jnp.exp(-(gap * gap))
        hi, lo = split(gauss)
        basis[0:8, here] = hi.astype(F32)
        basis[8:16, here] = lo.astype(F32)
        basis[16:24, here] = hi.astype(F32)
    weights[...] = jnp.zeros((32, 3 * CH), F32)
    for l in range(3):
        hi, lo = split(radial_weight[l] * SLOTS**-0.5)
        part = slice(l * CH, (l + 1) * CH)
        weights[0:8, part] = hi.astype(F32)
        weights[8:16, part] = hi.astype(F32)
        weights[16:24, part] = lo.astype(F32)
    radial[...] = dot(weights[...].astype(BF16), basis[...].astype(BF16), TN)
    moved[...] = dot(hidden, hot[...], NN)

    def forward(step, carry):
        top = pl.multiple_of(step * BAND, BAND)
        total = [jnp.zeros((BAND, ROWS), F32) for _ in range(9)]
        for e in range(SLOTS):
            here = slice(e * ROWS, (e + 1) * ROWS)
            value = moved[pl.ds(top, BAND), here]
            parts = [
                radial[pl.ds(pl.multiple_of(l * CH + top, BAND), BAND), here] * value
                for l in range(3)
            ]
            total[0] = total[0] + parts[0]
            for m in range(1, 9):
                l = 1 if m < 4 else 2
                total[m] = total[m] + shape_w[m - 1, e : e + 1, :] * parts[l]
        for m in range(9):
            feats9[m, pl.ds(top, BAND), :] = total[m]
        squares = [t * t for t in total]
        inv[pl.ds(top, BAND), :] = squares[0].astype(BF16)
        inv[pl.ds(pl.multiple_of(CH + top, BAND), BAND), :] = (
            squares[1] + squares[2] + squares[3]
        ).astype(BF16)
        inv[pl.ds(pl.multiple_of(2 * CH + top, BAND), BAND), :] = (
            squares[4] + squares[5] + squares[6] + squares[7] + squares[8]
        ).astype(BF16)
        return carry

    lax.fori_loop(0, CH // BAND, forward, 0)

    masked = jnp.where(lane < live_here, cot[0].astype(F32), 0.0).astype(BF16)
    local[...] = dot(out_weight[...], inv[...], TN)
    up9[...] = 2.0 * dot(out_weight[...], masked, NN)
    grad_out = dot(inv[...], masked, NT)
    for d in range(4, STRUCTS):
        to = d * SLOTS
        early[to : to + SLOTS, :] = grad_out[(d - 4) * SLOTS : (d - 3) * SLOTS]

    def backward(step, carry):
        top = pl.multiple_of(step * BAND, BAND)
        up = [
            up9[pl.ds(pl.multiple_of(l * CH + top, BAND), BAND), :] for l in range(3)
        ]
        upstream = []
        for m in range(9):
            l = 0 if m == 0 else (1 if m < 4 else 2)
            upstream.append(feats9[m, pl.ds(top, BAND), :] * up[l])
        for e in range(SLOTS):
            here = slice(e * ROWS, (e + 1) * ROWS)
            term = [upstream[0]] + [
                shape_w[m - 1, e : e + 1, :] * upstream[m] for m in range(1, 9)
            ]
            pull = (
                radial[pl.ds(top, BAND), here] * term[0]
                + radial[pl.ds(pl.multiple_of(CH + top, BAND), BAND), here]
                * (term[1] + term[2] + term[3])
                + radial[pl.ds(pl.multiple_of(2 * CH + top, BAND), BAND), here]
                * (term[4] + term[5] + term[6] + term[7] + term[8])
            )
            pulled[pl.ds(top, BAND), here] = pull.astype(BF16)
        return carry

    lax.fori_loop(0, CH // BAND, backward, 0)
    back = dot(pulled[...], hot[...], NT)
    grad_in = dot(ext[...], back.astype(BF16), NT)
    for d in range(4):
        to = d * SLOTS
        early[to : to + SLOTS, :] = grad_in[d * SLOTS : (d + 1) * SLOTS]


def half_point(miller):
    m0, m1, m2 = miller[0:1], miller[1:2], miller[2:3]
    sign = jnp.where(m0 < 0, -1, 1)
    m0, m1, m2 = sign * m0, sign * m1, sign * m2
    minus = m1 < 0
    turn = jnp.where(minus, -1, 1)
    plane = m0 + jnp.where(minus, TOP + 1, 0)
    return plane, turn * m1 * SIDE + (turn * m2 + TOP)


def one_hot(point):
    row = lax.broadcasted_iota(I32, (PLANE, KVEC), 0)
    return jnp.where(row == point, 1.0, 0.0).astype(BF16)


def turns(frac_row, first, count):
    width = frac_row.shape[1]
    m = (lax.broadcasted_iota(I32, (count, width), 0) + first).astype(F32)
    turn = m * frac_row
    turn = turn - jnp.floor(turn + 0.5)
    quarter = jnp.floor(turn * 4.0 + 0.5)
    arc = (turn - 0.25 * quarter) * (2.0 * math.pi)
    s2 = arc * arc
    sine = arc * (1.0 + s2 * (-1 / 6 + s2 * (1 / 120 + s2 * (-1 / 5040))))
    cosine = 1.0 + s2 * (-0.5 + s2 * (1 / 24 + s2 * (-1 / 720 + s2 * (1 / 40320))))
    odd = jnp.abs(quarter) == 1.0
    back = jnp.abs(quarter) == 2.0
    flip = jnp.where(quarter < 0.0, -1.0, 1.0)
    cos_out = jnp.where(odd, -flip * sine, jnp.where(back, -cosine, cosine))
    sin_out = jnp.where(odd, flip * cosine, jnp.where(back, -sine, sine))
    return cos_out, sin_out


def waves(frac, plane):
    width = plane.shape[1]
    c1, s1 = turns(frac[1], 0, 8)
    c2, s2 = turns(frac[2], -TOP, 16)
    for k in (0, PLANE):
        plane[k + 88 : k + PLANE, :] = jnp.zeros((PLANE - 88, width), F32)
    for m in range(TOP + 1):
        cm, sm = c1[m : m + 1], s1[m : m + 1]
        plane[m * SIDE : m * SIDE + 16, :] = cm * c2 - sm * s2
        plane[PLANE + m * SIDE : PLANE + m * SIDE + 16, :] = sm * c2 + cm * s2
    c0, s0 = turns(frac[0], 0, 8)
    return [c0[m : m + 1] for m in range(TOP + 1)] + [
        s0[m : m + 1] for m in range(1, TOP + 1)
    ]


def lattice_kernel(miller, filter_weight, folded, turned, wide):
    plane, point = half_point(miller[...])
    turned[...] = filter_weight[...].T * (1.0 / math.sqrt(KVEC * ATOMS))
    quarter = lax.axis_index("atom") >> 2
    mine = turned[pl.ds(pl.multiple_of(quarter * QUARTER, QUARTER), QUARTER), :]
    for b in range(2 * (TOP + 1)):
        here = slice(b * QUARTER, (b + 1) * QUARTER)
        wide[here, :] = jnp.where(plane == b, mine, 0.0).astype(BF16)
    sums = dot(wide[...], one_hot(point), NT)
    half = (TOP + 1) * QUARTER
    for m in range(TOP + 1):
        here = slice(m * QUARTER, (m + 1) * QUARTER)
        there = slice(half + m * QUARTER, half + (m + 1) * QUARTER)
        lanes = slice(m * PLANE, (m + 1) * PLANE)
        folded[0:QUARTER, lanes] = sums[here] + sums[there]
        folded[QUARTER : 2 * QUARTER, lanes] = sums[here] - sums[there]


def by_lane_group(pieces):
    group = lax.broadcasted_iota(I32, pieces[0].shape, 1) // 8
    for bit in (1, 2, 4, 8):
        low = group & bit == 0
        pieces = [
            jnp.where(low, piece, pltpu.roll(pieces[n + bit], 8 * bit, 1))
            if n & bit == 0
            else jnp.where(low, pltpu.roll(pieces[n - bit], CH - 8 * bit, 1), piece)
            for n, piece in enumerate(pieces)
        ]
    return pieces


def blocks(x, m):
    at = 2 * m * PLANE
    cc, cs = x[:, at : at + PLANE], x[:, at + PLANE : at + 2 * PLANE]
    if m == 0:
        return cc, None, None, cs
    at = 2 * (TOP + m) * PLANE
    sc, ss = x[:, at : at + PLANE], x[:, at + PLANE : at + 2 * PLANE]
    return cc, ss, sc, cs


def filtered(plus, minus, x):
    first, second = [], []
    for m in range(TOP + 1):
        here = slice(m * PLANE, (m + 1) * PLANE)
        p, d = plus[:, here], minus[:, here]
        cc, ss, sc, cs = blocks(x, m)
        if m == 0:
            first += [p * cc, p * cs]
        else:
            first += [p * cc - d * ss, p * cs + d * sc]
            second += [p * sc + d * cs, p * ss - d * cc]
    return first + second


def spectrum_kernel(
    gathered, folded, miller, early, parts, ewald, factor, frac, values, plane, wide
):
    for p in range(SLABS):
        here = slice(p * ROWS, (p + 1) * ROWS)
        values[:, here] = gathered[p]
        tail = gathered[p, HID_AT:PAY].astype(F32)
        frac[0:3, here] = tail[MINE : MINE + 3] + tail[MINE + 3 : MINE + 6]
    along = waves([frac[d : d + 1, :] for d in range(3)], plane)
    atoms = joined_count(gathered[0, HID_AT:PAY].astype(F32)[MINE:16]).astype(I32)
    live = lax.broadcasted_iota(I32, (1, ATOMS), 1) < atoms[:, 0:1]
    live = jnp.where(live, 1.0, 0.0)
    around = plane[...].astype(BF16)
    for low, high in ((0, TOP + 1), (TOP + 1, WAVES)):
        for f in range(low, high):
            wide[f * PAY : (f + 1) * PAY, :] = (
                values[...].astype(F32) * (along[f] * live)
            ).astype(BF16)
        both = dot(wide[low * PAY : high * PAY, :], around, NT)
        for f in range(low, high):
            here = slice(f * 2 * PLANE, (f + 1) * 2 * PLANE)
            factor[:, here] = both[(f - low) * PAY : (f - low + 1) * PAY]

    at = pl.multiple_of((lax.axis_index("atom") & 3) * MINE, MINE)
    s = factor[HID_AT : HID_AT + MINE, :]
    g = factor[pl.ds(pl.multiple_of(COT_AT + at, MINE), MINE), :]
    plus = folded[pl.ds(at, MINE), :]
    minus = folded[pl.ds(pl.multiple_of(QUARTER + at, MINE), MINE), :]
    pair_plus, pair_minus = [], []
    for m in range(TOP + 1):
        cc, ss, sc, cs = blocks(s, m)
        gcc, gss, gsc, gcs = blocks(g, m)
        even, odd = cc * gcc + cs * gcs, 0.0
        if m > 0:
            even = even + ss * gss + sc * gsc
            odd = sc * gcs + cs * gsc - cc * gss - ss * gcc
        pair_plus.append(even + odd)
        pair_minus.append(even - odd)
    pair = jnp.concatenate(pair_plus + pair_minus, axis=0)
    pair = split(pair * (1.0 / math.sqrt(KVEC * ATOMS)))
    around_plane, point = half_point(miller[...])
    found = dot(jnp.concatenate(pair, axis=0), one_hot(point), NN)
    planes = 2 * (TOP + 1)
    pair = jnp.zeros((MINE, KVEC), F32)
    for b in range(planes):
        value = found[b * MINE : (b + 1) * MINE] + found[(planes + b) * MINE : (planes + b + 1) * MINE]
        pair = jnp.where(around_plane == b, value, pair)
    pair = by_lane_group([pair[:, d * ROWS : (d + 1) * ROWS] for d in range(SLABS)])
    grad = filtered(
        folded[0:QUARTER, :],
        folded[QUARTER : 2 * QUARTER, :],
        factor[COT_AT:HID_AT, :],
    )
    grad = jnp.concatenate(split(jnp.concatenate(grad, axis=1)), axis=0)
    block = dot(grad, factor[0:QUARTER, :].astype(BF16), NT)
    block = block[0:QUARTER] + block[QUARTER : 2 * QUARTER]
    block = jnp.concatenate([block[8 * q : 8 * q + 8] for q in range(4)], axis=1)
    for d in range(STRUCTS):
        parts[d, 0:16, :] = jnp.concatenate(
            [pair[d], block], axis=0
        ).astype(BF16)
        parts[d, 16:48, :] = early[d * SLOTS : (d + 1) * SLOTS, :].astype(BF16)
    coef = filtered(plus, minus, s)
    coef = [
        jnp.concatenate([coef[2 * f], coef[2 * f + 1]], axis=1) for f in range(WAVES)
    ]
    field = dot(jnp.concatenate(coef, axis=0).astype(BF16), around, NN)
    total = field[0:MINE] * along[0]
    for f in range(1, WAVES):
        total = total + field[f * MINE : (f + 1) * MINE] * along[f]
    for p in range(SLABS):
        ewald[p] = total[:, p * ROWS : (p + 1) * ROWS].astype(BF16)


SPECTRUM_SCRATCH = [
    pltpu.VMEM((PAY, BASIS), F32),
    pltpu.VMEM((8, ATOMS), F32),
    pltpu.VMEM((PAY, ATOMS), BF16),
    pltpu.VMEM((2 * PLANE, ATOMS), F32),
    pltpu.VMEM((WAVES * PAY, ATOMS), BF16),
]


def middle_kernel(sums, own, local, last, grad_in, field):
    row = lax.broadcasted_iota(I32, (8, KSHARE), 0)
    lane = lax.broadcasted_iota(I32, (8, KSHARE), 1)
    pick = jnp.where(lane == row + MINE * lax.axis_index("atom"), 1.0, 0.0).astype(BF16)
    blocks = [sums[p].astype(F32) for p in range(SLABS)]
    pairs = jnp.concatenate([block[0:8] for block in blocks], axis=0)
    picked = dot(pick, pairs.astype(BF16), NT)
    total = blocks[0][16:48]
    for block in blocks[1:]:
        total = total + block[16:48]
    out = jnp.concatenate([total, picked, picked], axis=0).astype(BF16)
    for d in range(STRUCTS):
        last[d] = out
    grads = []
    for c in range(0, CH, 8):
        at, g = c % QUARTER // 8, c // QUARTER
        eight = blocks[4 * g][8:16]
        eight = pltpu.roll(eight, (0 - at) * QUARTER % CH, 1)
        for q in range(1, 4):
            turned = pltpu.roll(blocks[4 * g + q][8:16], (q - at) * QUARTER % CH, 1)
            eight = jnp.where(lane < q * QUARTER, eight, turned)
        grads.append(eight)
    grad_in[...] = jnp.concatenate(grads, axis=0).T
    ewald = jnp.concatenate([block[48:56] for block in blocks], axis=0)
    live = joined_count(own[FRAC_AT:HALO]).astype(I32) - lax.axis_index("atom") * ROWS
    live = lax.broadcasted_iota(I32, (CH, ROWS), 1) < live
    field[...] = jnp.where(live, own[0:CH].astype(F32) + local[...] + ewald, 0.0)


def finish_kernel(
    sums, ewald_in, field, updated, grad_filter, grad_in, grad_out
):
    updated[0] = field[...].astype(BF16)
    for d in range(STRUCTS):
        late = sums[d, 32:48].astype(F32)
        grad_filter[8 * d : 8 * d + 8, :] = late[0:8]
    for d in range(4):
        here = slice(d * SLOTS, (d + 1) * SLOTS)
        grad_in[here, :] = ewald_in[here, :] + sums[d, 0:32].astype(F32)
    for d in range(4, STRUCTS):
        grad_out[(d - 4) * SLOTS : (d - 3) * SLOTS, :] = sums[d, 0:32].astype(F32)


def exchange(x, axis):
    return lax.all_to_all(x, axis, 0, 0)


def shards(
    node_feats,
    frac,
    neighbours,
    images,
    neighbour_count,
    atom_count,
    miller,
    in_weight,
    radial_weight,
    out_weight,
    filter_weight,
    cotangent,
):
    struct = jax.ShapeDtypeStruct

    halo, payload = call(
        pack_kernel,
        [
            (HBM, struct((HALO, ROWS), BF16)),
            (HBM, struct((SLABS, PAY, ROWS), BF16)),
        ],
        [
            pltpu.VMEM((1, CH, ROWS), BF16),
            pltpu.VMEM((1, CH, ROWS), BF16),
            pltpu.VMEM((3, 1, ROWS), F32),
            pltpu.VMEM((CH, CH), BF16),
            pltpu.VMEM((1, 1), I32),
            pltpu.VMEM((HALO, ROWS), BF16),
            pltpu.VMEM((SLABS, PAY, ROWS), BF16),
            pltpu.VMEM((16, ROWS), F32),
            pltpu.SemaphoreType.DMA((8,)),
        ],
        60,
        10**6,
        (HBM, node_feats),
        (HBM, cotangent),
        (HBM, frac.transpose(1, 0, 2)),
        (HBM, in_weight),
        (HBM, atom_count.reshape(1, 1)),
    )
    evens = range(0, SLABS, 2)
    pairs = [(n, n + 1) for n in evens], [(n + 1, (n + 2) % SLABS) for n in evens]
    first_swap, second_swap = (
        lax.ppermute(halo, "atom", [*pair, *((j, i) for i, j in pair)]) for pair in pairs
    )
    gathered = exchange(payload, "atom")

    early, local = call(
        edge_kernel,
        [(VMEM, struct((4 * CH, CH), F32)), (VMEM, struct((CH, ROWS), F32))],
        [
            pltpu.VMEM((CH, 2 * ROWS), BF16),
            pltpu.VMEM((2 * ROWS, EDGES), BF16),
            pltpu.VMEM((32, 3 * CH), F32),
            pltpu.VMEM((32, EDGES), F32),
            pltpu.VMEM((3 * CH, EDGES), F32),
            pltpu.VMEM((CH, EDGES), F32),
            pltpu.VMEM((8, SLOTS, ROWS), F32),
            pltpu.VMEM((SLOTS, ROWS), F32),
            pltpu.VMEM((9, CH, ROWS), F32),
            pltpu.VMEM((3 * CH, ROWS), F32),
            pltpu.VMEM((CH, EDGES), BF16),
            pltpu.VMEM((3 * CH, ROWS), BF16),
        ],
        20,
        EDGE_COST,
        (VMEM, halo),
        (VMEM, first_swap),
        (VMEM, second_swap),
        (VMEM, neighbours),
        (VMEM, images),
        (VMEM, neighbour_count),
        (VMEM, in_weight),
        (VMEM, radial_weight),
        (VMEM, out_weight),
        (VMEM, cotangent),
    )
    early, miller = lax.optimization_barrier((early, miller))
    (folded,) = call(
        lattice_kernel,
        [(VMEM, struct((2 * QUARTER, HALF), F32))],
        [
            pltpu.VMEM((CH, KVEC), F32),
            pltpu.VMEM((2 * (TOP + 1) * QUARTER, KVEC), BF16),
        ],
        12,
        10**8,
        (VMEM, miller),
        (VMEM, filter_weight),
    )
    parts, ewald = call(
        spectrum_kernel,
        [
            (VMEM, struct((STRUCTS, 48, CH), BF16)),
            (VMEM, struct((SLABS, MINE, ROWS), BF16)),
        ],
        SPECTRUM_SCRATCH,
        20,
        10**10,
        (VMEM, gathered),
        (VMEM, folded),
        (VMEM, miller),
        (VMEM, early),
    )
    sums = exchange(parts, "dp").astype(F32).sum(axis=0).astype(BF16)
    sums = jnp.broadcast_to(sums[None], (SLABS, 48, CH))
    last, ewald_in, field = call(
        middle_kernel,
        [
            (VMEM, struct((STRUCTS, 48, CH), BF16)),
            (VMEM, struct((CH, CH), F32)),
            (VMEM, struct((CH, ROWS), F32)),
        ],
        [],
        16,
        10**6,
        (VMEM, exchange(jnp.concatenate([sums, ewald], axis=1), "atom")),
        (VMEM, halo),
        (VMEM, local),
    )
    return tuple(call(
        finish_kernel,
        [
            (VMEM, struct((1, CH, ROWS), BF16)),
            (VMEM, struct((KSHARE, CH), F32)),
            (VMEM, struct((CH, CH), F32)),
            (VMEM, struct((3 * CH, CH), F32)),
        ],
        [],
        16,
        10**6,
        (VMEM, exchange(last, "dp")),
        (VMEM, ewald_in),
        (VMEM, field),
    ))


def solution(mesh):
    return jax.shard_map(
        shards,
        mesh=mesh,
        in_specs=(
            P("dp", None, "atom"),
            P("dp", None, "atom"),
            P("dp", None, "atom"),
            P("dp", None, "atom"),
            P("dp", "atom"),
            P("dp"),
            P(),
            P(),
            P(),
            P(),
            P(),
            P("dp", None, "atom"),
        ),
        out_specs=(P("dp", None, "atom"), P("atom", None), P(), P()),
        check_vma=False,
    )
```

```python
import math

import jax
import jax.numpy as jnp
from jax import lax
from jax.experimental import pallas as pl
from jax.experimental.pallas import tpu as pltpu
from jax.sharding import PartitionSpec as P

F32 = jnp.float32
BF16 = jnp.bfloat16
I32 = jnp.int32

CH = 128
ROWS = 128
SLABS = 16
STRUCTS = 16
ATOMS = ROWS * SLABS
SLOTS = 32
EDGES = SLOTS * ROWS
GHOST = 32
KVEC = 2048
KSHARE = KVEC // SLABS
NB = 8
TOP = 6
SIDE = 2 * TOP + 1
PLANE = 128
HALF = (TOP + 1) * PLANE
WAVES = SIDE
BASIS = WAVES * 2 * PLANE
TILE = 256
MINE = CH // SLABS
QUARTER = CH // 4
FRAC_AT = CH
HALO = CH + 16
COT_AT, HID_AT, PAY = QUARTER, 2 * QUARTER, 2 * QUARTER + 16

VMEM = pl.BlockSpec(memory_space=pltpu.VMEM)
HBM = pl.BlockSpec(memory_space=pltpu.HBM)

NN = (((1,), (0,)), ((), ()))
NT = (((1,), (1,)), ((), ()))
TN = (((0,), (0,)), ((), ()))


def dot(a, b, dims):
    return lax.dot_general(a, b, dims, preferred_element_type=F32)


def split(x):
    hi = x.astype(BF16)
    return hi, (x - hi.astype(F32)).astype(BF16)


def call(kernel, outs, scratch, mib, flops, *args):
    return pl.pallas_call(
        kernel,
        out_shape=[shape for _, shape in outs],
        in_specs=[spec for spec, _ in args],
        out_specs=[spec for spec, _ in outs],
        scratch_shapes=scratch,
        compiler_params=pltpu.CompilerParams(vmem_limit_bytes=mib * 2**20),
        cost_estimate=pl.CostEstimate(
            flops=flops, bytes_accessed=2**16, transcendentals=0
        ),
    )(*[arg for _, arg in args])


def pack_kernel(
    feats_hbm, cot_hbm, frac_hbm, weight_hbm, count_hbm, halo_hbm, payload_hbm, feats, cot, frac, weight, count, halo, payload, rows, sems
):
    pairs = (
        (frac_hbm, frac),
        (feats_hbm, feats),
        (weight_hbm, weight),
        (cot_hbm, cot),
        (count_hbm, count),
    )
    copies = [
        pltpu.make_async_copy(src, dst, sems.at[n]) for n, (src, dst) in enumerate(pairs)
    ]
    for copy in copies:
        copy.start()
    copies[0].wait()
    rows[...] = jnp.zeros((16, ROWS), F32)
    for d in range(3):
        first = jnp.floor(frac[d] * 256.0) * (1.0 / 256.0)
        rows[d : d + 1, :] = first
        rows[d + 3 : d + 4, :] = frac[d] - first
    copies[4].wait()
    rows[6:7, :] = jnp.broadcast_to((count[...] >> 4).astype(F32), (1, ROWS))
    rows[7:8, :] = jnp.broadcast_to((count[...] & 15).astype(F32), (1, ROWS))
    where = rows[...]
    halo[FRAC_AT:HALO] = where.astype(BF16)
    copies[1].wait()
    halo[0:CH] = feats[0]
    sent = [pltpu.make_async_copy(halo, halo_hbm, sems.at[5])]
    sent[0].start()
    for a in range(SLABS):
        payload[a, 0:COT_AT] = feats[0, a % 4 * QUARTER : (a % 4 + 1) * QUARTER]
    copies[3].wait()
    for a in range(SLABS):
        payload[a, COT_AT:HID_AT] = cot[0, a // 4 * QUARTER : (a // 4 + 1) * QUARTER]
    parts = slice(0, HID_AT), slice(HID_AT, PAY)
    sent += [
        pltpu.make_async_copy(payload.at[:, part], payload_hbm.at[:, part], sems.at[6 + n])
        for n, part in enumerate(parts)
    ]
    sent[1].start()
    copies[2].wait()
    hidden = dot(weight[...], feats[0], TN)
    for a in range(SLABS):
        payload[a, HID_AT:PAY] = jnp.concatenate(
            [hidden[a * MINE : (a + 1) * MINE], where[0:8]], axis=0
        ).astype(BF16)
    sent[2].start()
    for copy in sent:
        copy.wait()


def joined_count(rows):
    wide = rows.astype(F32)
    return 16.0 * wide[6:7] + wide[7:8]


def joined_frac(rows):
    wide = rows.astype(F32)
    return [wide[d : d + 1] + wide[d + 3 : d + 4] for d in range(3)]


ROOT3, ROOT5, ROOT15 = math.sqrt(3.0), math.sqrt(5.0), math.sqrt(15.0)
STEP = 1.75 / (NB - 1)
BAND = 16
EDGE_COST = 10**10


def edge_kernel(
    own,
    first_swap,
    second_swap,
    neighbours,
    images,
    count,
    in_weight,
    radial_weight,
    out_weight,
    cot,
    early,
    local,
    ext,
    hot,
    weights,
    basis,
    radial,
    moved,
    shape_w,
    length,
    feats9,
    up9,
    pulled,
    inv,
):
    slab = lax.axis_index("atom")
    first = slab * ROWS
    atoms = joined_count(own[FRAC_AT:HALO]).astype(I32)
    live_here = atoms - first
    live_left = atoms - ((first - ROWS) & (ATOMS - 1))
    live_right = atoms - ((first + ROWS) & (ATOMS - 1))
    lane = lax.broadcasted_iota(I32, (CH, ROWS), 1)
    ext[:, 0:ROWS] = jnp.where(lane < live_here, own[0:CH].astype(F32), 0.0).astype(BF16)
    even = (slab & 1) == 0
    swaps = first_swap[...].astype(F32), second_swap[...].astype(F32)
    right = jnp.where(even, swaps[0], swaps[1])
    left = jnp.where(even, swaps[1], swaps[0])
    near_right = jnp.where(lane < live_right, right[0:CH], 0.0)
    near_left = jnp.where(lane < live_left, left[0:CH], 0.0)
    ext[:, ROWS : 2 * ROWS] = jnp.where(lane < GHOST, near_right, near_left).astype(BF16)
    hidden = dot(in_weight[...], ext[...], TN).astype(BF16)

    offset = (neighbours[0] - first) & (ATOMS - 1)
    column = jnp.where(offset < ROWS + GHOST, offset, offset - (ATOMS - 2 * ROWS))
    at = column & (ROWS - 1)
    in_slab = column < ROWS
    frac_own = joined_frac(own[FRAC_AT:HALO])
    frac_left = joined_frac(left[FRAC_AT:HALO])
    frac_right = joined_frac(right[FRAC_AT:HALO])
    lane1 = lax.broadcasted_iota(I32, (1, ROWS), 1)

    code = images[0]
    ninth = (code * 57) >> 9
    third = (code * 171) >> 9
    shifts = (ninth, third - 3 * ninth, code - 3 * third)
    vector = []
    for d in range(3):
        near = jnp.broadcast_to(frac_own[d], (SLOTS, ROWS))
        far = jnp.where(lane1 < GHOST, frac_right[d], frac_left[d])
        far = jnp.broadcast_to(far, (SLOTS, ROWS))
        other = jnp.where(
            in_slab,
            jnp.take_along_axis(near, at, axis=1),
            jnp.take_along_axis(far, at, axis=1),
        )
        vector.append(0.5 * (other - near + (shifts[d].astype(F32) - 1.0)))
    x, y, z = vector
    square = x * x + y * y + z * z
    slot = lax.broadcasted_iota(I32, (SLOTS, ROWS), 0)
    lane32 = lax.broadcasted_iota(I32, (SLOTS, ROWS), 1)
    used = (slot < count[...]) & (lane32 < live_here)
    column = jnp.where(used, column, -1)
    harmonics = (
        ROOT3 * x,
        ROOT3 * y,
        ROOT3 * z,
        ROOT15 * x * y,
        ROOT15 * y * z,
        0.5 * ROOT5 * (3.0 * z * z - square),
        ROOT15 * x * z,
        0.5 * ROOT15 * (x * x - y * y),
    )
    for m in range(8):
        shape_w[m] = harmonics[m]
    length[...] = jnp.sqrt(square)

    rows256 = lax.broadcasted_iota(I32, (2 * ROWS, ROWS), 0)
    centre = lax.broadcasted_iota(I32, (NB, ROWS), 0).astype(F32) * STEP
    basis[24:32, :] = jnp.zeros((8, EDGES), F32)
    for e in range(SLOTS):
        here = slice(e * ROWS, (e + 1) * ROWS)
        hot[:, here] = jnp.where(rows256 == column[e : e + 1], 1.0, 0.0).astype(BF16)
        gap = (length[e : e + 1, :] - centre) * (1.0 / STEP)
        gauss = jnp.exp(-(gap * gap))
        hi, lo = split(gauss)
        basis[0:8, here] = hi.astype(F32)
        basis[8:16, here] = lo.astype(F32)
        basis[16:24, here] = hi.astype(F32)
    weights[...] = jnp.zeros((32, 3 * CH), F32)
    for l in range(3):
        hi, lo = split(radial_weight[l] * SLOTS**-0.5)
        part = slice(l * CH, (l + 1) * CH)
        weights[0:8, part] = hi.astype(F32)
        weights[8:16, part] = hi.astype(F32)
        weights[16:24, part] = lo.astype(F32)
    radial[...] = dot(weights[...].astype(BF16), basis[...].astype(BF16), TN)
    moved[...] = dot(hidden, hot[...], NN)

    def forward(step, carry):
        top = pl.multiple_of(step * BAND, BAND)
        total = [jnp.zeros((BAND, ROWS), F32) for _ in range(9)]
        for e in range(SLOTS):
            here = slice(e * ROWS, (e + 1) * ROWS)
            value = moved[pl.ds(top, BAND), here]
            parts = [
                radial[pl.ds(pl.multiple_of(l * CH + top, BAND), BAND), here] * value
                for l in range(3)
            ]
            total[0] = total[0] + parts[0]
            for m in range(1, 9):
                l = 1 if m < 4 else 2
                total[m] = total[m] + shape_w[m - 1, e : e + 1, :] * parts[l]
        for m in range(9):
            feats9[m, pl.ds(top, BAND), :] = total[m]
        squares = [t * t for t in total]
        inv[pl.ds(top, BAND), :] = squares[0].astype(BF16)
        inv[pl.ds(pl.multiple_of(CH + top, BAND), BAND), :] = (
            squares[1] + squares[2] + squares[3]
        ).astype(BF16)
        inv[pl.ds(pl.multiple_of(2 * CH + top, BAND), BAND), :] = (
            squares[4] + squares[5] + squares[6] + squares[7] + squares[8]
        ).astype(BF16)
        return carry

    lax.fori_loop(0, CH // BAND, forward, 0)

    masked = jnp.where(lane < live_here, cot[0].astype(F32), 0.0).astype(BF16)
    local[...] = dot(out_weight[...], inv[...], TN)
    up9[...] = 2.0 * dot(out_weight[...], masked, NN)
    grad_out = dot(inv[...], masked, NT)
    for d in range(4, STRUCTS):
        to = d * SLOTS
        early[to : to + SLOTS, :] = grad_out[(d - 4) * SLOTS : (d - 3) * SLOTS]

    def backward(step, carry):
        top = pl.multiple_of(step * BAND, BAND)
        up = [
            up9[pl.ds(pl.multiple_of(l * CH + top, BAND), BAND), :] for l in range(3)
        ]
        upstream = []
        for m in range(9):
            l = 0 if m == 0 else (1 if m < 4 else 2)
            upstream.append(feats9[m, pl.ds(top, BAND), :] * up[l])
        for e in range(SLOTS):
            here = slice(e * ROWS, (e + 1) * ROWS)
            term = [upstream[0]] + [
                shape_w[m - 1, e : e + 1, :] * upstream[m] for m in range(1, 9)
            ]
            pull = (
                radial[pl.ds(top, BAND), here] * term[0]
                + radial[pl.ds(pl.multiple_of(CH + top, BAND), BAND), here]
                * (term[1] + term[2] + term[3])
                + radial[pl.ds(pl.multiple_of(2 * CH + top, BAND), BAND), here]
                * (term[4] + term[5] + term[6] + term[7] + term[8])
            )
            pulled[pl.ds(top, BAND), here] = pull.astype(BF16)
        return carry

    lax.fori_loop(0, CH // BAND, backward, 0)
    back = dot(pulled[...], hot[...], NT)
    grad_in = dot(ext[...], back.astype(BF16), NT)
    for d in range(4):
        to = d * SLOTS
        early[to : to + SLOTS, :] = grad_in[d * SLOTS : (d + 1) * SLOTS]


def half_point(miller):
    m0, m1, m2 = miller[0:1], miller[1:2], miller[2:3]
    sign = jnp.where(m0 < 0, -1, 1)
    m0, m1, m2 = sign * m0, sign * m1, sign * m2
    minus = m1 < 0
    turn = jnp.where(minus, -1, 1)
    plane = m0 + jnp.where(minus, TOP + 1, 0)
    return plane, turn * m1 * SIDE + (turn * m2 + TOP)


def one_hot(point):
    row = lax.broadcasted_iota(I32, (PLANE, KVEC), 0)
    return jnp.where(row == point, 1.0, 0.0).astype(BF16)


def turns(frac_row, first, count):
    width = frac_row.shape[1]
    m = (lax.broadcasted_iota(I32, (count, width), 0) + first).astype(F32)
    turn = m * frac_row
    turn = turn - jnp.floor(turn + 0.5)
    quarter = jnp.floor(turn * 4.0 + 0.5)
    arc = (turn - 0.25 * quarter) * (2.0 * math.pi)
    s2 = arc * arc
    sine = arc * (1.0 + s2 * (-1 / 6 + s2 * (1 / 120 + s2 * (-1 / 5040))))
    cosine = 1.0 + s2 * (-0.5 + s2 * (1 / 24 + s2 * (-1 / 720 + s2 * (1 / 40320))))
    odd = jnp.abs(quarter) == 1.0
    back = jnp.abs(quarter) == 2.0
    flip = jnp.where(quarter < 0.0, -1.0, 1.0)
    cos_out = jnp.where(odd, -flip * sine, jnp.where(back, -cosine, cosine))
    sin_out = jnp.where(odd, flip * cosine, jnp.where(back, -sine, sine))
    return cos_out, sin_out


def waves(frac, plane):
    width = plane.shape[1]
    c1, s1 = turns(frac[1], 0, 8)
    c2, s2 = turns(frac[2], -TOP, 16)
    for k in (0, PLANE):
        plane[k + 88 : k + PLANE, :] = jnp.zeros((PLANE - 88, width), F32)
    for m in range(TOP + 1):
        cm, sm = c1[m : m + 1], s1[m : m + 1]
        plane[m * SIDE : m * SIDE + 16, :] = cm * c2 - sm * s2
        plane[PLANE + m * SIDE : PLANE + m * SIDE + 16, :] = sm * c2 + cm * s2
    c0, s0 = turns(frac[0], 0, 8)
    return [c0[m : m + 1] for m in range(TOP + 1)] + [
        s0[m : m + 1] for m in range(1, TOP + 1)
    ]


def lattice_kernel(miller, filter_weight, folded, turned, wide):
    plane, point = half_point(miller[...])
    turned[...] = filter_weight[...].T * (1.0 / math.sqrt(KVEC * ATOMS))
    quarter = lax.axis_index("atom") >> 2
    mine = turned[pl.ds(pl.multiple_of(quarter * QUARTER, QUARTER), QUARTER), :]
    for b in range(2 * (TOP + 1)):
        here = slice(b * QUARTER, (b + 1) * QUARTER)
        wide[here, :] = jnp.where(plane == b, mine, 0.0).astype(BF16)
    sums = dot(wide[...], one_hot(point), NT)
    half = (TOP + 1) * QUARTER
    for m in range(TOP + 1):
        here = slice(m * QUARTER, (m + 1) * QUARTER)
        there = slice(half + m * QUARTER, half + (m + 1) * QUARTER)
        lanes = slice(m * PLANE, (m + 1) * PLANE)
        folded[0:QUARTER, lanes] = sums[here] + sums[there]
        folded[QUARTER : 2 * QUARTER, lanes] = sums[here] - sums[there]


def by_lane_group(pieces):
    group = lax.broadcasted_iota(I32, pieces[0].shape, 1) // 8
    for bit in (1, 2, 4, 8):
        low = group & bit == 0
        pieces = [
            jnp.where(low, piece, pltpu.roll(pieces[n + bit], 8 * bit, 1))
            if n & bit == 0
            else jnp.where(low, pltpu.roll(pieces[n - bit], CH - 8 * bit, 1), piece)
            for n, piece in enumerate(pieces)
        ]
    return pieces


def blocks(x, m):
    at = 2 * m * PLANE
    cc, cs = x[:, at : at + PLANE], x[:, at + PLANE : at + 2 * PLANE]
    if m == 0:
        return cc, None, None, cs
    at = 2 * (TOP + m) * PLANE
    sc, ss = x[:, at : at + PLANE], x[:, at + PLANE : at + 2 * PLANE]
    return cc, ss, sc, cs


def filtered(plus, minus, x):
    first, second = [], []
    for m in range(TOP + 1):
        here = slice(m * PLANE, (m + 1) * PLANE)
        p, d = plus[:, here], minus[:, here]
        cc, ss, sc, cs = blocks(x, m)
        if m == 0:
            first += [p * cc, p * cs]
        else:
            first += [p * cc - d * ss, p * cs + d * sc]
            second += [p * sc + d * cs, p * ss - d * cc]
    return first + second


def spectrum_kernel(
    gathered, folded, miller, early, parts, ewald, factor, frac, values, plane, wide
):
    for p in range(SLABS):
        here = slice(p * ROWS, (p + 1) * ROWS)
        values[:, here] = gathered[p]
        tail = gathered[p, HID_AT:PAY].astype(F32)
        frac[0:3, here] = tail[MINE : MINE + 3] + tail[MINE + 3 : MINE + 6]
    along = waves([frac[d : d + 1, :] for d in range(3)], plane)
    atoms = joined_count(gathered[0, HID_AT:PAY].astype(F32)[MINE:16]).astype(I32)
    live = lax.broadcasted_iota(I32, (1, ATOMS), 1) < atoms[:, 0:1]
    live = jnp.where(live, 1.0, 0.0)
    around = plane[...].astype(BF16)
    for low, high in ((0, TOP + 1), (TOP + 1, WAVES)):
        for f in range(low, high):
            wide[f * PAY : (f + 1) * PAY, :] = (
                values[...].astype(F32) * (along[f] * live)
            ).astype(BF16)
        both = dot(wide[low * PAY : high * PAY, :], around, NT)
        for f in range(low, high):
            here = slice(f * 2 * PLANE, (f + 1) * 2 * PLANE)
            factor[:, here] = both[(f - low) * PAY : (f - low + 1) * PAY]

    at = pl.multiple_of((lax.axis_index("atom") & 3) * MINE, MINE)
    s = factor[HID_AT : HID_AT + MINE, :]
    g = factor[pl.ds(pl.multiple_of(COT_AT + at, MINE), MINE), :]
    plus = folded[pl.ds(at, MINE), :]
    minus = folded[pl.ds(pl.multiple_of(QUARTER + at, MINE), MINE), :]
    pair_plus, pair_minus = [], []
    for m in range(TOP + 1):
        cc, ss, sc, cs = blocks(s, m)
        gcc, gss, gsc, gcs = blocks(g, m)
        even, odd = cc * gcc + cs * gcs, 0.0
        if m > 0:
            even = even + ss * gss + sc * gsc
            odd = sc * gcs + cs * gsc - cc * gss - ss * gcc
        pair_plus.append(even + odd)
        pair_minus.append(even - odd)
    pair = jnp.concatenate(pair_plus + pair_minus, axis=0)
    pair = split(pair * (1.0 / math.sqrt(KVEC * ATOMS)))
    around_plane, point = half_point(miller[...])
    found = dot(jnp.concatenate(pair, axis=0), one_hot(point), NN)
    planes = 2 * (TOP + 1)
    pair = jnp.zeros((MINE, KVEC), F32)
    for b in range(planes):
        value = found[b * MINE : (b + 1) * MINE] + found[(planes + b) * MINE : (planes + b + 1) * MINE]
        pair = jnp.where(around_plane == b, value, pair)
    pair = by_lane_group([pair[:, d * ROWS : (d + 1) * ROWS] for d in range(SLABS)])
    grad = filtered(
        folded[0:QUARTER, :],
        folded[QUARTER : 2 * QUARTER, :],
        factor[COT_AT:HID_AT, :],
    )
    grad = jnp.concatenate(split(jnp.concatenate(grad, axis=1)), axis=0)
    block = dot(grad, factor[0:QUARTER, :].astype(BF16), NT)
    block = block[0:QUARTER] + block[QUARTER : 2 * QUARTER]
    block = jnp.concatenate([block[8 * q : 8 * q + 8] for q in range(4)], axis=1)
    for d in range(STRUCTS):
        parts[d, 0:16, :] = jnp.concatenate(
            [pair[d], block], axis=0
        ).astype(BF16)
        parts[d, 16:48, :] = early[d * SLOTS : (d + 1) * SLOTS, :].astype(BF16)
    coef = filtered(plus, minus, s)
    coef = [
        jnp.concatenate([coef[2 * f], coef[2 * f + 1]], axis=1) for f in range(WAVES)
    ]
    field = dot(jnp.concatenate(coef, axis=0).astype(BF16), around, NN)
    total = field[0:MINE] * along[0]
    for f in range(1, WAVES):
        total = total + field[f * MINE : (f + 1) * MINE] * along[f]
    for p in range(SLABS):
        ewald[p] = total[:, p * ROWS : (p + 1) * ROWS]


SPECTRUM_SCRATCH = [
    pltpu.VMEM((PAY, BASIS), F32),
    pltpu.VMEM((8, ATOMS), F32),
    pltpu.VMEM((PAY, ATOMS), BF16),
    pltpu.VMEM((2 * PLANE, ATOMS), F32),
    pltpu.VMEM((WAVES * PAY, ATOMS), BF16),
]


def turn_kernel(sums, ewald, out):
    total = sums[0].astype(F32)
    for d in range(1, STRUCTS):
        total = total + sums[d].astype(F32)
    lane = lax.broadcasted_iota(I32, (MINE, CH), 1)
    share = pltpu.roll(total[8:16], (8 - 8 * lax.axis_index("dp")) & (CH - 1), 1)
    for p in range(SLABS):
        picked = pltpu.roll(total[0:8], (CH - 8 * p) % CH, 1)
        out[p] = jnp.concatenate(
            [total[16:48], jnp.where(lane < 8, picked, share), ewald[p]], axis=0
        ).astype(BF16)


def middle_kernel(sums, own, local, last, field):
    row = lax.broadcasted_iota(I32, (8, CH), 0)
    lane = lax.broadcasted_iota(I32, (8, CH), 1)
    pick = jnp.where(lane == row, 1.0, 0.0).astype(BF16)
    blocks = [sums[p].astype(F32) for p in range(SLABS)]
    pairs = jnp.concatenate([block[32:40] for block in blocks], axis=0)
    picked = dot(pick, pairs.astype(BF16), NT)
    total, share = blocks[0][0:32], jnp.zeros((8, CH), F32)
    for block in blocks[1:]:
        total = total + block[0:32]
    for p, block in enumerate(blocks):
        turned = pltpu.roll(block[32:40], (8 * p - 8) % CH, 1)
        share = jnp.where(lane >> 3 == p, turned, share)
    out = jnp.concatenate([total, picked, share], axis=0).astype(BF16)
    for d in range(STRUCTS):
        last[d] = out
    ewald = jnp.concatenate([block[40:48] for block in blocks], axis=0)
    live = joined_count(own[FRAC_AT:HALO]).astype(I32) - lax.axis_index("atom") * ROWS
    live = lax.broadcasted_iota(I32, (CH, ROWS), 1) < live
    field[...] = jnp.where(live, own[0:CH].astype(F32) + local[...] + ewald, 0.0)


def finish_kernel(sums, field, updated, grad_filter, grad_in, grad_out):
    updated[0] = field[...].astype(BF16)
    lane8 = lax.broadcasted_iota(I32, (8, CH), 1)
    heads = [sums[d, 32:48].astype(F32) for d in range(STRUCTS)]
    for d in range(STRUCTS):
        grad_filter[8 * d : 8 * d + 8, :] = heads[d][0:8]
    grads = []
    for c in range(0, CH, 8):
        g, q = c // QUARTER, c % QUARTER // 8
        eight = pltpu.roll(heads[4 * q][8:16], (0 - g) * QUARTER % CH, 1)
        for u in range(1, 4):
            turned = pltpu.roll(heads[4 * q + u][8:16], (u - g) * QUARTER % CH, 1)
            eight = jnp.where(lane8 < u * QUARTER, eight, turned)
        grads.append(eight)
    row = lax.broadcasted_iota(I32, (CH, CH), 0)
    lane = lax.broadcasted_iota(I32, (CH, CH), 1)
    channel = 32 * ((lane >> 3) & 3) + 8 * (lane >> 5) + (lane & 7)
    order = jnp.where(row == channel, 1.0, 0.0).astype(BF16)
    ewald_in = dot(order, jnp.concatenate(grads, axis=0).astype(BF16), NT)
    for d in range(4):
        here = slice(d * SLOTS, (d + 1) * SLOTS)
        grad_in[here, :] = ewald_in[here] + sums[d, 0:32].astype(F32)
    for d in range(4, STRUCTS):
        grad_out[(d - 4) * SLOTS : (d - 3) * SLOTS, :] = sums[d, 0:32].astype(F32)


def exchange(x, axis):
    return lax.all_to_all(x, axis, 0, 0)


def shards(
    node_feats,
    frac,
    neighbours,
    images,
    neighbour_count,
    atom_count,
    miller,
    in_weight,
    radial_weight,
    out_weight,
    filter_weight,
    cotangent,
):
    struct = jax.ShapeDtypeStruct

    halo, payload = call(
        pack_kernel,
        [
            (HBM, struct((HALO, ROWS), BF16)),
            (HBM, struct((SLABS, PAY, ROWS), BF16)),
        ],
        [
            pltpu.VMEM((1, CH, ROWS), BF16),
            pltpu.VMEM((1, CH, ROWS), BF16),
            pltpu.VMEM((3, 1, ROWS), F32),
            pltpu.VMEM((CH, CH), BF16),
            pltpu.VMEM((1, 1), I32),
            pltpu.VMEM((HALO, ROWS), BF16),
            pltpu.VMEM((SLABS, PAY, ROWS), BF16),
            pltpu.VMEM((16, ROWS), F32),
            pltpu.SemaphoreType.DMA((8,)),
        ],
        60,
        10**6,
        (HBM, node_feats),
        (HBM, cotangent),
        (HBM, frac.transpose(1, 0, 2)),
        (HBM, in_weight),
        (HBM, atom_count.reshape(1, 1)),
    )
    evens = range(0, SLABS, 2)
    pairs = [(n, n + 1) for n in evens], [(n + 1, (n + 2) % SLABS) for n in evens]
    first_swap, second_swap = (
        lax.ppermute(halo, "atom", [*pair, *((j, i) for i, j in pair)]) for pair in pairs
    )
    gathered = exchange(payload, "atom")

    early, local = call(
        edge_kernel,
        [(VMEM, struct((4 * CH, CH), F32)), (VMEM, struct((CH, ROWS), F32))],
        [
            pltpu.VMEM((CH, 2 * ROWS), BF16),
            pltpu.VMEM((2 * ROWS, EDGES), BF16),
            pltpu.VMEM((32, 3 * CH), F32),
            pltpu.VMEM((32, EDGES), F32),
            pltpu.VMEM((3 * CH, EDGES), F32),
            pltpu.VMEM((CH, EDGES), F32),
            pltpu.VMEM((8, SLOTS, ROWS), F32),
            pltpu.VMEM((SLOTS, ROWS), F32),
            pltpu.VMEM((9, CH, ROWS), F32),
            pltpu.VMEM((3 * CH, ROWS), F32),
            pltpu.VMEM((CH, EDGES), BF16),
            pltpu.VMEM((3 * CH, ROWS), BF16),
        ],
        20,
        EDGE_COST,
        (VMEM, halo),
        (VMEM, first_swap),
        (VMEM, second_swap),
        (VMEM, neighbours),
        (VMEM, images),
        (VMEM, neighbour_count),
        (VMEM, in_weight),
        (VMEM, radial_weight),
        (VMEM, out_weight),
        (VMEM, cotangent),
    )
    early, miller = lax.optimization_barrier((early, miller))
    (folded,) = call(
        lattice_kernel,
        [(VMEM, struct((2 * QUARTER, HALF), F32))],
        [
            pltpu.VMEM((CH, KVEC), F32),
            pltpu.VMEM((2 * (TOP + 1) * QUARTER, KVEC), BF16),
        ],
        12,
        10**8,
        (VMEM, miller),
        (VMEM, filter_weight),
    )
    parts, ewald = call(
        spectrum_kernel,
        [
            (VMEM, struct((STRUCTS, 48, CH), BF16)),
            (VMEM, struct((SLABS, MINE, ROWS), F32)),
        ],
        SPECTRUM_SCRATCH,
        20,
        10**10,
        (VMEM, gathered),
        (VMEM, folded),
        (VMEM, miller),
        (VMEM, early),
    )
    (sums,) = call(
        turn_kernel,
        [(VMEM, struct((SLABS, 48, CH), BF16))],
        [],
        16,
        10**6,
        (VMEM, exchange(parts, "dp")),
        (VMEM, ewald),
    )
    last, field = call(
        middle_kernel,
        [
            (VMEM, struct((STRUCTS, 48, CH), BF16)),
            (VMEM, struct((CH, ROWS), F32)),
        ],
        [],
        16,
        10**6,
        (VMEM, exchange(sums, "atom")),
        (VMEM, halo),
        (VMEM, local),
    )
    return tuple(
        call(
            finish_kernel,
            [
                (VMEM, struct((1, CH, ROWS), BF16)),
                (VMEM, struct((KSHARE, CH), F32)),
                (VMEM, struct((CH, CH), F32)),
                (VMEM, struct((3 * CH, CH), F32)),
            ],
            [],
            16,
            10**6,
            (VMEM, exchange(last, "dp")),
            (VMEM, field),
        )
    )


def solution(mesh):
    return jax.shard_map(
        shards,
        mesh=mesh,
        in_specs=(
            P("dp", None, "atom"),
            P("dp", None, "atom"),
            P("dp", None, "atom"),
            P("dp", None, "atom"),
            P("dp", "atom"),
            P("dp"),
            P(),
            P(),
            P(),
            P(),
            P(),
            P("dp", None, "atom"),
        ),
        out_specs=(P("dp", None, "atom"), P("atom", None), P(), P()),
        check_vma=False,
    )
```

```python
import math

import jax
import jax.numpy as jnp
from jax import lax
from jax.experimental import pallas as pl
from jax.experimental.pallas import tpu as pltpu
from jax.sharding import PartitionSpec as P

F32 = jnp.float32
BF16 = jnp.bfloat16
I32 = jnp.int32

CH = 128
ROWS = 128
SLABS = 16
STRUCTS = 16
ATOMS = ROWS * SLABS
SLOTS = 32
EDGES = SLOTS * ROWS
GHOST = 32
KVEC = 2048
KSHARE = KVEC // SLABS
NB = 8
TOP = 6
SIDE = 2 * TOP + 1
PLANE = 128
HALF = (TOP + 1) * PLANE
WAVES = SIDE
BASIS = WAVES * 2 * PLANE
TILE = 256
MINE = CH // SLABS
QUARTER = CH // 4
FRAC_AT = CH
HALO = CH + 16
THIRD = HALO // 3
COT_AT, HID_AT, PAY = QUARTER, 2 * QUARTER, 2 * QUARTER + 16

VMEM = pl.BlockSpec(memory_space=pltpu.VMEM)
HBM = pl.BlockSpec(memory_space=pltpu.HBM)
SMEM = pl.BlockSpec(memory_space=pltpu.SMEM)

NN = (((1,), (0,)), ((), ()))
NT = (((1,), (1,)), ((), ()))
TN = (((0,), (0,)), ((), ()))


def dot(a, b, dims):
    return lax.dot_general(a, b, dims, preferred_element_type=F32)


def split(x):
    hi = x.astype(BF16)
    return hi, (x - hi.astype(F32)).astype(BF16)


def call(kernel, outs, scratch, mib, flops, *args):
    return pl.pallas_call(
        kernel,
        out_shape=[shape for _, shape in outs],
        in_specs=[spec for spec, _ in args],
        out_specs=[spec for spec, _ in outs],
        scratch_shapes=scratch,
        compiler_params=pltpu.CompilerParams(vmem_limit_bytes=mib * 2**20),
        cost_estimate=pl.CostEstimate(
            flops=flops, bytes_accessed=2**16, transcendentals=0
        ),
    )(*[arg for _, arg in args])


def pack_kernel(
    feats_hbm, cot_hbm, frac_hbm, weight_hbm, halo_hbm, first_hbm, second_hbm, payload_hbm, feats, cot, frac, weight, halo, first_end, second_end, payload, rows, sems
):
    pairs = (
        (frac_hbm, frac),
        (feats_hbm, feats),
        (weight_hbm, weight),
        (cot_hbm, cot),
    )
    copies = [
        pltpu.make_async_copy(src, dst, sems.at[n]) for n, (src, dst) in enumerate(pairs)
    ]
    for copy in copies:
        copy.start()
    copies[0].wait()
    rows[...] = jnp.zeros((16, ROWS), F32)
    for d in range(3):
        first = jnp.floor(frac[d] * 256.0) * (1.0 / 256.0)
        rows[d : d + 1, :] = first
        rows[d + 3 : d + 4, :] = frac[d] - first
    where = rows[...]
    halo[FRAC_AT:HALO] = where.astype(BF16)
    copies[1].wait()
    halo[0:CH] = feats[0]
    wide = jnp.concatenate([feats[0].astype(F32), where], axis=0)
    bands = [wide[n * THIRD : (n + 1) * THIRD] for n in range(3)]
    lane = lax.broadcasted_iota(I32, (THIRD, ROWS), 1)

    def dense(shift):
        turned = [pltpu.roll(b, shift + GHOST * n, 1) if shift + n else b for n, b in enumerate(bands)]
        return jnp.where(lane < GHOST, turned[0], jnp.where(lane < 2 * GHOST, turned[1], turned[2]))

    low, high = dense(0), dense(GHOST)
    even = (lax.axis_index("atom") & 1) == 0
    first_end[...] = jnp.where(even, high, low).astype(BF16)
    second_end[...] = jnp.where(even, low, high).astype(BF16)
    sent = [
        pltpu.make_async_copy(first_end, first_hbm, sems.at[8]),
        pltpu.make_async_copy(second_end, second_hbm, sems.at[9]),
        pltpu.make_async_copy(halo, halo_hbm, sems.at[5]),
    ]
    for copy in sent:
        copy.start()
    for a in range(SLABS):
        payload[a, 0:COT_AT] = feats[0, a % 4 * QUARTER : (a % 4 + 1) * QUARTER]
    copies[3].wait()
    for a in range(SLABS):
        payload[a, COT_AT:HID_AT] = cot[0, a // 4 * QUARTER : (a // 4 + 1) * QUARTER]
    parts = slice(0, HID_AT), slice(HID_AT, PAY)
    sent += [
        pltpu.make_async_copy(payload.at[:, part], payload_hbm.at[:, part], sems.at[6 + n])
        for n, part in enumerate(parts)
    ]
    sent[3].start()
    copies[2].wait()
    hidden = dot(weight[...], feats[0], TN)
    for a in range(SLABS):
        payload[a, HID_AT:PAY] = jnp.concatenate(
            [hidden[a * MINE : (a + 1) * MINE], where[0:8]], axis=0
        ).astype(BF16)
    sent[4].start()
    for copy in sent:
        copy.wait()


def joined_frac(rows):
    wide = rows.astype(F32)
    return [wide[d : d + 1] + wide[d + 3 : d + 4] for d in range(3)]


ROOT3, ROOT5, ROOT15 = math.sqrt(3.0), math.sqrt(5.0), math.sqrt(15.0)
STEP = 1.75 / (NB - 1)
BAND = 16
EDGE_COST = 10**10


def edge_kernel(
    atom_count,
    own,
    first_swap,
    second_swap,
    neighbours,
    images,
    count,
    in_weight,
    radial_weight,
    out_weight,
    cot,
    early,
    local,
    ext,
    hot,
    weights,
    basis,
    radial,
    moved,
    shape_w,
    length,
    feats9,
    up9,
    pulled,
    inv,
):
    slab = lax.axis_index("atom")
    first = slab * ROWS
    atoms = atom_count[0]
    live_here = atoms - first
    live_left = atoms - ((first - ROWS) & (ATOMS - 1))
    live_right = atoms - ((first + ROWS) & (ATOMS - 1))
    lane = lax.broadcasted_iota(I32, (CH, ROWS), 1)
    ext[:, 0:ROWS] = jnp.where(lane < live_here, own[0:CH].astype(F32), 0.0).astype(BF16)
    even = (slab & 1) == 0
    swaps = first_swap[...].astype(F32), second_swap[...].astype(F32)
    right = jnp.where(even, swaps[0], swaps[1])
    left = jnp.where(even, swaps[1], swaps[0])
    right = jnp.concatenate(
        [right] + [pltpu.roll(right, ROWS - GHOST * n, 1) for n in (1, 2)], axis=0
    )
    left = jnp.concatenate(
        [pltpu.roll(left, ROWS - GHOST * (n + 1), 1) for n in range(3)], axis=0
    )
    near_right = jnp.where(lane < live_right, right[0:CH], 0.0)
    near_left = jnp.where(lane < live_left, left[0:CH], 0.0)
    ext[:, ROWS : 2 * ROWS] = jnp.where(lane < GHOST, near_right, near_left).astype(BF16)
    hidden = dot(in_weight[...], ext[...], TN).astype(BF16)

    offset = (neighbours[0] - first) & (ATOMS - 1)
    column = jnp.where(offset < ROWS + GHOST, offset, offset - (ATOMS - 2 * ROWS))
    at = column & (ROWS - 1)
    in_slab = column < ROWS
    frac_own = joined_frac(own[FRAC_AT:HALO])
    frac_left = joined_frac(left[FRAC_AT:HALO])
    frac_right = joined_frac(right[FRAC_AT:HALO])
    lane1 = lax.broadcasted_iota(I32, (1, ROWS), 1)

    code = images[0]
    ninth = (code * 57) >> 9
    third = (code * 171) >> 9
    shifts = (ninth, third - 3 * ninth, code - 3 * third)
    vector = []
    for d in range(3):
        near = jnp.broadcast_to(frac_own[d], (SLOTS, ROWS))
        far = jnp.where(lane1 < GHOST, frac_right[d], frac_left[d])
        far = jnp.broadcast_to(far, (SLOTS, ROWS))
        other = jnp.where(
            in_slab,
            jnp.take_along_axis(near, at, axis=1),
            jnp.take_along_axis(far, at, axis=1),
        )
        vector.append(0.5 * (other - near + (shifts[d].astype(F32) - 1.0)))
    x, y, z = vector
    square = x * x + y * y + z * z
    slot = lax.broadcasted_iota(I32, (SLOTS, ROWS), 0)
    lane32 = lax.broadcasted_iota(I32, (SLOTS, ROWS), 1)
    used = (slot < count[...]) & (lane32 < live_here)
    column = jnp.where(used, column, -1)
    harmonics = (
        ROOT3 * x,
        ROOT3 * y,
        ROOT3 * z,
        ROOT15 * x * y,
        ROOT15 * y * z,
        0.5 * ROOT5 * (3.0 * z * z - square),
        ROOT15 * x * z,
        0.5 * ROOT15 * (x * x - y * y),
    )
    for m in range(8):
        shape_w[m] = harmonics[m]
    length[...] = jnp.sqrt(square)

    rows256 = lax.broadcasted_iota(I32, (2 * ROWS, ROWS), 0)
    centre = lax.broadcasted_iota(I32, (NB, ROWS), 0).astype(F32) * STEP
    basis[24:32, :] = jnp.zeros((8, EDGES), F32)
    for e in range(SLOTS):
        here = slice(e * ROWS, (e + 1) * ROWS)
        hot[:, here] = jnp.where(rows256 == column[e : e + 1], 1.0, 0.0).astype(BF16)
        gap = (length[e : e + 1, :] - centre) * (1.0 / STEP)
        gauss = jnp.exp(-(gap * gap))
        hi, lo = split(gauss)
        basis[0:8, here] = hi.astype(F32)
        basis[8:16, here] = lo.astype(F32)
        basis[16:24, here] = hi.astype(F32)
    weights[...] = jnp.zeros((32, 3 * CH), F32)
    for l in range(3):
        hi, lo = split(radial_weight[l] * SLOTS**-0.5)
        part = slice(l * CH, (l + 1) * CH)
        weights[0:8, part] = hi.astype(F32)
        weights[8:16, part] = hi.astype(F32)
        weights[16:24, part] = lo.astype(F32)
    radial[...] = dot(weights[...].astype(BF16), basis[...].astype(BF16), TN)
    moved[...] = dot(hidden, hot[...], NN)

    def forward(step, carry):
        top = pl.multiple_of(step * BAND, BAND)
        total = [jnp.zeros((BAND, ROWS), F32) for _ in range(9)]
        for e in range(SLOTS):
            here = slice(e * ROWS, (e + 1) * ROWS)
            value = moved[pl.ds(top, BAND), here]
            parts = [
                radial[pl.ds(pl.multiple_of(l * CH + top, BAND), BAND), here] * value
                for l in range(3)
            ]
            total[0] = total[0] + parts[0]
            for m in range(1, 9):
                l = 1 if m < 4 else 2
                total[m] = total[m] + shape_w[m - 1, e : e + 1, :] * parts[l]
        for m in range(9):
            feats9[m, pl.ds(top, BAND), :] = total[m]
        squares = [t * t for t in total]
        inv[pl.ds(top, BAND), :] = squares[0].astype(BF16)
        inv[pl.ds(pl.multiple_of(CH + top, BAND), BAND), :] = (
            squares[1] + squares[2] + squares[3]
        ).astype(BF16)
        inv[pl.ds(pl.multiple_of(2 * CH + top, BAND), BAND), :] = (
            squares[4] + squares[5] + squares[6] + squares[7] + squares[8]
        ).astype(BF16)
        return carry

    lax.fori_loop(0, CH // BAND, forward, 0)

    masked = jnp.where(lane < live_here, cot[0].astype(F32), 0.0).astype(BF16)
    local[...] = dot(out_weight[...], inv[...], TN)
    up9[...] = 2.0 * dot(out_weight[...], masked, NN)
    grad_out = dot(inv[...], masked, NT)
    for d in range(4, STRUCTS):
        to = d * SLOTS
        early[to : to + SLOTS, :] = grad_out[(d - 4) * SLOTS : (d - 3) * SLOTS]

    def backward(step, carry):
        top = pl.multiple_of(step * BAND, BAND)
        up = [
            up9[pl.ds(pl.multiple_of(l * CH + top, BAND), BAND), :] for l in range(3)
        ]
        upstream = []
        for m in range(9):
            l = 0 if m == 0 else (1 if m < 4 else 2)
            upstream.append(feats9[m, pl.ds(top, BAND), :] * up[l])
        for e in range(SLOTS):
            here = slice(e * ROWS, (e + 1) * ROWS)
            term = [upstream[0]] + [
                shape_w[m - 1, e : e + 1, :] * upstream[m] for m in range(1, 9)
            ]
            pull = (
                radial[pl.ds(top, BAND), here] * term[0]
                + radial[pl.ds(pl.multiple_of(CH + top, BAND), BAND), here]
                * (term[1] + term[2] + term[3])
                + radial[pl.ds(pl.multiple_of(2 * CH + top, BAND), BAND), here]
                * (term[4] + term[5] + term[6] + term[7] + term[8])
            )
            pulled[pl.ds(top, BAND), here] = pull.astype(BF16)
        return carry

    lax.fori_loop(0, CH // BAND, backward, 0)
    back = dot(pulled[...], hot[...], NT)
    grad_in = dot(ext[...], back.astype(BF16), NT)
    for d in range(4):
        to = d * SLOTS
        early[to : to + SLOTS, :] = grad_in[d * SLOTS : (d + 1) * SLOTS]


def half_point(miller):
    m0, m1, m2 = miller[0:1], miller[1:2], miller[2:3]
    sign = jnp.where(m0 < 0, -1, 1)
    m0, m1, m2 = sign * m0, sign * m1, sign * m2
    minus = m1 < 0
    turn = jnp.where(minus, -1, 1)
    plane = m0 + jnp.where(minus, TOP + 1, 0)
    return plane, turn * m1 * SIDE + (turn * m2 + TOP)


def one_hot(point):
    row = lax.broadcasted_iota(I32, (PLANE, KVEC), 0)
    return jnp.where(row == point, 1.0, 0.0).astype(BF16)


def turns(frac_row, first, count):
    width = frac_row.shape[1]
    m = (lax.broadcasted_iota(I32, (count, width), 0) + first).astype(F32)
    turn = m * frac_row
    turn = turn - jnp.floor(turn + 0.5)
    quarter = jnp.floor(turn * 4.0 + 0.5)
    arc = (turn - 0.25 * quarter) * (2.0 * math.pi)
    s2 = arc * arc
    sine = arc * (1.0 + s2 * (-1 / 6 + s2 * (1 / 120 + s2 * (-1 / 5040))))
    cosine = 1.0 + s2 * (-0.5 + s2 * (1 / 24 + s2 * (-1 / 720 + s2 * (1 / 40320))))
    odd = jnp.abs(quarter) == 1.0
    back = jnp.abs(quarter) == 2.0
    flip = jnp.where(quarter < 0.0, -1.0, 1.0)
    cos_out = jnp.where(odd, -flip * sine, jnp.where(back, -cosine, cosine))
    sin_out = jnp.where(odd, flip * cosine, jnp.where(back, -sine, sine))
    return cos_out, sin_out


def waves(frac, plane):
    width = plane.shape[1]
    c1, s1 = turns(frac[1], 0, 8)
    c2, s2 = turns(frac[2], -TOP, 16)
    for k in (0, PLANE):
        plane[k + 88 : k + PLANE, :] = jnp.zeros((PLANE - 88, width), F32)
    for m in range(TOP + 1):
        cm, sm = c1[m : m + 1], s1[m : m + 1]
        plane[m * SIDE : m * SIDE + 16, :] = cm * c2 - sm * s2
        plane[PLANE + m * SIDE : PLANE + m * SIDE + 16, :] = sm * c2 + cm * s2
    c0, s0 = turns(frac[0], 0, 8)
    return [c0[m : m + 1] for m in range(TOP + 1)] + [
        s0[m : m + 1] for m in range(1, TOP + 1)
    ]


def lattice_kernel(miller, filter_weight, folded, turned, wide):
    plane, point = half_point(miller[...])
    turned[...] = filter_weight[...].T * (1.0 / math.sqrt(KVEC * ATOMS))
    quarter = lax.axis_index("atom") >> 2
    mine = turned[pl.ds(pl.multiple_of(quarter * QUARTER, QUARTER), QUARTER), :]
    for b in range(2 * (TOP + 1)):
        here = slice(b * QUARTER, (b + 1) * QUARTER)
        wide[here, :] = jnp.where(plane == b, mine, 0.0).astype(BF16)
    sums = dot(wide[...], one_hot(point), NT)
    half = (TOP + 1) * QUARTER
    for m in range(TOP + 1):
        here = slice(m * QUARTER, (m + 1) * QUARTER)
        there = slice(half + m * QUARTER, half + (m + 1) * QUARTER)
        lanes = slice(m * PLANE, (m + 1) * PLANE)
        folded[0:QUARTER, lanes] = sums[here] + sums[there]
        folded[QUARTER : 2 * QUARTER, lanes] = sums[here] - sums[there]


def by_lane_group(pieces):
    group = lax.broadcasted_iota(I32, pieces[0].shape, 1) // 8
    for bit in (1, 2, 4, 8):
        low = group & bit == 0
        pieces = [
            jnp.where(low, piece, pltpu.roll(pieces[n + bit], 8 * bit, 1))
            if n & bit == 0
            else jnp.where(low, pltpu.roll(pieces[n - bit], CH - 8 * bit, 1), piece)
            for n, piece in enumerate(pieces)
        ]
    return pieces


def blocks(x, m):
    at = 2 * m * PLANE
    cc, cs = x[:, at : at + PLANE], x[:, at + PLANE : at + 2 * PLANE]
    if m == 0:
        return cc, None, None, cs
    at = 2 * (TOP + m) * PLANE
    sc, ss = x[:, at : at + PLANE], x[:, at + PLANE : at + 2 * PLANE]
    return cc, ss, sc, cs


def filtered(plus, minus, x):
    first, second = [], []
    for m in range(TOP + 1):
        here = slice(m * PLANE, (m + 1) * PLANE)
        p, d = plus[:, here], minus[:, here]
        cc, ss, sc, cs = blocks(x, m)
        if m == 0:
            first += [p * cc, p * cs]
        else:
            first += [p * cc - d * ss, p * cs + d * sc]
            second += [p * sc + d * cs, p * ss - d * cc]
    return first + second


def spectrum_kernel(
    atom_count, gathered, folded, miller, early, parts, ewald, factor, frac, values, plane, wide
):
    for p in range(SLABS):
        here = slice(p * ROWS, (p + 1) * ROWS)
        values[:, here] = gathered[p]
        tail = gathered[p, HID_AT:PAY].astype(F32)
        frac[0:3, here] = tail[MINE : MINE + 3] + tail[MINE + 3 : MINE + 6]
    along = waves([frac[d : d + 1, :] for d in range(3)], plane)
    live = lax.broadcasted_iota(I32, (1, ATOMS), 1) < atom_count[0]
    live = jnp.where(live, 1.0, 0.0)
    around = plane[...].astype(BF16)
    for low, high in ((0, TOP + 1), (TOP + 1, WAVES)):
        for f in range(low, high):
            wide[f * PAY : (f + 1) * PAY, :] = (
                values[...].astype(F32) * (along[f] * live)
            ).astype(BF16)
        both = dot(wide[low * PAY : high * PAY, :], around, NT)
        for f in range(low, high):
            here = slice(f * 2 * PLANE, (f + 1) * 2 * PLANE)
            factor[:, here] = both[(f - low) * PAY : (f - low + 1) * PAY]

    at = pl.multiple_of((lax.axis_index("atom") & 3) * MINE, MINE)
    s = factor[HID_AT : HID_AT + MINE, :]
    g = factor[pl.ds(pl.multiple_of(COT_AT + at, MINE), MINE), :]
    plus = folded[pl.ds(at, MINE), :]
    minus = folded[pl.ds(pl.multiple_of(QUARTER + at, MINE), MINE), :]
    pair_plus, pair_minus = [], []
    for m in range(TOP + 1):
        cc, ss, sc, cs = blocks(s, m)
        gcc, gss, gsc, gcs = blocks(g, m)
        even, odd = cc * gcc + cs * gcs, 0.0
        if m > 0:
            even = even + ss * gss + sc * gsc
            odd = sc * gcs + cs * gsc - cc * gss - ss * gcc
        pair_plus.append(even + odd)
        pair_minus.append(even - odd)
    pair = jnp.concatenate(pair_plus + pair_minus, axis=0)
    pair = split(pair * (1.0 / math.sqrt(KVEC * ATOMS)))
    around_plane, point = half_point(miller[...])
    found = dot(jnp.concatenate(pair, axis=0), one_hot(point), NN)
    planes = 2 * (TOP + 1)
    pair = jnp.zeros((MINE, KVEC), F32)
    for b in range(planes):
        value = found[b * MINE : (b + 1) * MINE] + found[(planes + b) * MINE : (planes + b + 1) * MINE]
        pair = jnp.where(around_plane == b, value, pair)
    pair = by_lane_group([pair[:, d * ROWS : (d + 1) * ROWS] for d in range(SLABS)])
    grad = filtered(
        folded[0:QUARTER, :],
        folded[QUARTER : 2 * QUARTER, :],
        factor[COT_AT:HID_AT, :],
    )
    grad = jnp.concatenate(split(jnp.concatenate(grad, axis=1)), axis=0)
    block = dot(grad, factor[0:QUARTER, :].astype(BF16), NT)
    block = block[0:QUARTER] + block[QUARTER : 2 * QUARTER]
    block = jnp.concatenate([block[8 * q : 8 * q + 8] for q in range(4)], axis=1)
    for d in range(STRUCTS):
        parts[d, 0:16, :] = jnp.concatenate(
            [pair[d], block], axis=0
        ).astype(BF16)
        parts[d, 16:48, :] = early[d * SLOTS : (d + 1) * SLOTS, :].astype(BF16)
    coef = filtered(plus, minus, s)
    coef = [
        jnp.concatenate([coef[2 * f], coef[2 * f + 1]], axis=1) for f in range(WAVES)
    ]
    field = dot(jnp.concatenate(coef, axis=0).astype(BF16), around, NN)
    total = field[0:MINE] * along[0]
    for f in range(1, WAVES):
        total = total + field[f * MINE : (f + 1) * MINE] * along[f]
    for p in range(SLABS):
        ewald[p] = total[:, p * ROWS : (p + 1) * ROWS]


SPECTRUM_SCRATCH = [
    pltpu.VMEM((PAY, BASIS), F32),
    pltpu.VMEM((8, ATOMS), F32),
    pltpu.VMEM((PAY, ATOMS), BF16),
    pltpu.VMEM((2 * PLANE, ATOMS), F32),
    pltpu.VMEM((WAVES * PAY, ATOMS), BF16),
]


def turn_kernel(sums, ewald, out):
    total = sums[0].astype(F32)
    for d in range(1, STRUCTS):
        total = total + sums[d].astype(F32)
    lane = lax.broadcasted_iota(I32, (MINE, CH), 1)
    share = pltpu.roll(total[8:16], (8 - 8 * lax.axis_index("dp")) & (CH - 1), 1)
    for p in range(SLABS):
        picked = pltpu.roll(total[0:8], (CH - 8 * p) % CH, 1)
        out[p] = jnp.concatenate(
            [total[16:48], jnp.where(lane < 8, picked, share), ewald[p]], axis=0
        ).astype(BF16)


def middle_kernel(atom_count, sums, own, local, last, field):
    row = lax.broadcasted_iota(I32, (8, CH), 0)
    lane = lax.broadcasted_iota(I32, (8, CH), 1)
    pick = jnp.where(lane == row, 1.0, 0.0).astype(BF16)
    blocks = [sums[p].astype(F32) for p in range(SLABS)]
    pairs = jnp.concatenate([block[32:40] for block in blocks], axis=0)
    picked = dot(pick, pairs.astype(BF16), NT)
    total, share = blocks[0][0:32], jnp.zeros((8, CH), F32)
    for block in blocks[1:]:
        total = total + block[0:32]
    for p, block in enumerate(blocks):
        turned = pltpu.roll(block[32:40], (8 * p - 8) % CH, 1)
        share = jnp.where(lane >> 3 == p, turned, share)
    out = jnp.concatenate([total, picked, share], axis=0).astype(BF16)
    for d in range(STRUCTS):
        last[d] = out
    ewald = jnp.concatenate([block[40:48] for block in blocks], axis=0)
    live = atom_count[0] - lax.axis_index("atom") * ROWS
    live = lax.broadcasted_iota(I32, (CH, ROWS), 1) < live
    field[...] = jnp.where(live, own[0:CH].astype(F32) + local[...] + ewald, 0.0)


def finish_kernel(sums, field, updated, grad_filter, grad_in, grad_out):
    updated[0] = field[...].astype(BF16)
    lane8 = lax.broadcasted_iota(I32, (8, CH), 1)
    heads = [sums[d, 32:48].astype(F32) for d in range(STRUCTS)]
    for d in range(STRUCTS):
        grad_filter[8 * d : 8 * d + 8, :] = heads[d][0:8]
    grads = []
    for c in range(0, CH, 8):
        g, q = c // QUARTER, c % QUARTER // 8
        eight = pltpu.roll(heads[4 * q][8:16], (0 - g) * QUARTER % CH, 1)
        for u in range(1, 4):
            turned = pltpu.roll(heads[4 * q + u][8:16], (u - g) * QUARTER % CH, 1)
            eight = jnp.where(lane8 < u * QUARTER, eight, turned)
        grads.append(eight)
    row = lax.broadcasted_iota(I32, (CH, CH), 0)
    lane = lax.broadcasted_iota(I32, (CH, CH), 1)
    channel = 32 * ((lane >> 3) & 3) + 8 * (lane >> 5) + (lane & 7)
    order = jnp.where(row == channel, 1.0, 0.0).astype(BF16)
    ewald_in = dot(order, jnp.concatenate(grads, axis=0).astype(BF16), NT)
    for d in range(4):
        here = slice(d * SLOTS, (d + 1) * SLOTS)
        grad_in[here, :] = ewald_in[here] + sums[d, 0:32].astype(F32)
    for d in range(4, STRUCTS):
        grad_out[(d - 4) * SLOTS : (d - 3) * SLOTS, :] = sums[d, 0:32].astype(F32)


def exchange(x, axis):
    return lax.all_to_all(x, axis, 0, 0)


def shards(
    node_feats,
    frac,
    neighbours,
    images,
    neighbour_count,
    atom_count,
    miller,
    in_weight,
    radial_weight,
    out_weight,
    filter_weight,
    cotangent,
):
    struct = jax.ShapeDtypeStruct

    halo, *ends, payload = call(
        pack_kernel,
        [
            (HBM, struct((HALO, ROWS), BF16)),
            (HBM, struct((THIRD, ROWS), BF16)),
            (HBM, struct((THIRD, ROWS), BF16)),
            (HBM, struct((SLABS, PAY, ROWS), BF16)),
        ],
        [
            pltpu.VMEM((1, CH, ROWS), BF16),
            pltpu.VMEM((1, CH, ROWS), BF16),
            pltpu.VMEM((3, 1, ROWS), F32),
            pltpu.VMEM((CH, CH), BF16),
            pltpu.VMEM((HALO, ROWS), BF16),
            pltpu.VMEM((THIRD, ROWS), BF16),
            pltpu.VMEM((THIRD, ROWS), BF16),
            pltpu.VMEM((SLABS, PAY, ROWS), BF16),
            pltpu.VMEM((16, ROWS), F32),
            pltpu.SemaphoreType.DMA((10,)),
        ],
        60,
        10**6,
        (HBM, node_feats),
        (HBM, cotangent),
        (HBM, frac.transpose(1, 0, 2)),
        (HBM, in_weight),
    )
    evens = range(0, SLABS, 2)
    pairs = [(n, n + 1) for n in evens], [(n + 1, (n + 2) % SLABS) for n in evens]
    first_swap, second_swap = (
        lax.ppermute(end, "atom", [*pair, *((j, i) for i, j in pair)])
        for end, pair in zip(ends, pairs)
    )
    gathered = exchange(payload, "atom")

    early, local = call(
        edge_kernel,
        [(VMEM, struct((4 * CH, CH), F32)), (VMEM, struct((CH, ROWS), F32))],
        [
            pltpu.VMEM((CH, 2 * ROWS), BF16),
            pltpu.VMEM((2 * ROWS, EDGES), BF16),
            pltpu.VMEM((32, 3 * CH), F32),
            pltpu.VMEM((32, EDGES), F32),
            pltpu.VMEM((3 * CH, EDGES), F32),
            pltpu.VMEM((CH, EDGES), F32),
            pltpu.VMEM((8, SLOTS, ROWS), F32),
            pltpu.VMEM((SLOTS, ROWS), F32),
            pltpu.VMEM((9, CH, ROWS), F32),
            pltpu.VMEM((3 * CH, ROWS), F32),
            pltpu.VMEM((CH, EDGES), BF16),
            pltpu.VMEM((3 * CH, ROWS), BF16),
        ],
        20,
        EDGE_COST,
        (SMEM, atom_count),
        (VMEM, halo),
        (VMEM, first_swap),
        (VMEM, second_swap),
        (VMEM, neighbours),
        (VMEM, images),
        (VMEM, neighbour_count),
        (VMEM, in_weight),
        (VMEM, radial_weight),
        (VMEM, out_weight),
        (VMEM, cotangent),
    )
    early, miller = lax.optimization_barrier((early, miller))
    (folded,) = call(
        lattice_kernel,
        [(VMEM, struct((2 * QUARTER, HALF), F32))],
        [
            pltpu.VMEM((CH, KVEC), F32),
            pltpu.VMEM((2 * (TOP + 1) * QUARTER, KVEC), BF16),
        ],
        12,
        10**8,
        (VMEM, miller),
        (VMEM, filter_weight),
    )
    parts, ewald = call(
        spectrum_kernel,
        [
            (VMEM, struct((STRUCTS, 48, CH), BF16)),
            (VMEM, struct((SLABS, MINE, ROWS), F32)),
        ],
        SPECTRUM_SCRATCH,
        20,
        10**10,
        (SMEM, atom_count),
        (VMEM, gathered),
        (VMEM, folded),
        (VMEM, miller),
        (VMEM, early),
    )
    (sums,) = call(
        turn_kernel,
        [(VMEM, struct((SLABS, 48, CH), BF16))],
        [],
        16,
        10**6,
        (VMEM, exchange(parts, "dp")),
        (VMEM, ewald),
    )
    last, field = call(
        middle_kernel,
        [
            (VMEM, struct((STRUCTS, 48, CH), BF16)),
            (VMEM, struct((CH, ROWS), F32)),
        ],
        [],
        16,
        10**6,
        (SMEM, atom_count),
        (VMEM, exchange(sums, "atom")),
        (VMEM, halo),
        (VMEM, local),
    )
    return tuple(
        call(
            finish_kernel,
            [
                (VMEM, struct((1, CH, ROWS), BF16)),
                (VMEM, struct((KSHARE, CH), F32)),
                (VMEM, struct((CH, CH), F32)),
                (VMEM, struct((3 * CH, CH), F32)),
            ],
            [],
            16,
            10**6,
            (VMEM, exchange(last, "dp")),
            (VMEM, field),
        )
    )


def solution(mesh):
    return jax.shard_map(
        shards,
        mesh=mesh,
        in_specs=(
            P("dp", None, "atom"),
            P("dp", None, "atom"),
            P("dp", None, "atom"),
            P("dp", None, "atom"),
            P("dp", "atom"),
            P("dp"),
            P(),
            P(),
            P(),
            P(),
            P(),
            P("dp", None, "atom"),
        ),
        out_specs=(P("dp", None, "atom"), P("atom", None), P(), P()),
        check_vma=False,
    )
```

```python
import math

import jax
import jax.numpy as jnp
from jax import lax
from jax.experimental import pallas as pl
from jax.experimental.pallas import tpu as pltpu
from jax.sharding import PartitionSpec as P

F32 = jnp.float32
BF16 = jnp.bfloat16
I32 = jnp.int32

CH = 128
ROWS = 128
SLABS = 16
STRUCTS = 16
ATOMS = ROWS * SLABS
SLOTS = 32
EDGES = SLOTS * ROWS
GHOST = 32
KVEC = 2048
KSHARE = KVEC // SLABS
NB = 8
TOP = 6
SIDE = 2 * TOP + 1
PLANE = 128
HALF = (TOP + 1) * PLANE
WAVES = SIDE
BASIS = WAVES * 2 * PLANE
TILE = 256
MINE = CH // SLABS
QUARTER = CH // 4
FRAC_AT = CH
HALO = CH + 16
COT_AT, HID_AT, PAY = QUARTER, 2 * QUARTER, 2 * QUARTER + 16

VMEM = pl.BlockSpec(memory_space=pltpu.VMEM)
HBM = pl.BlockSpec(memory_space=pltpu.HBM)

NN = (((1,), (0,)), ((), ()))
NT = (((1,), (1,)), ((), ()))
TN = (((0,), (0,)), ((), ()))


def dot(a, b, dims):
    return lax.dot_general(a, b, dims, preferred_element_type=F32)


def split(x):
    hi = x.astype(BF16)
    return hi, (x - hi.astype(F32)).astype(BF16)


def call(kernel, outs, scratch, mib, flops, *args):
    return pl.pallas_call(
        kernel,
        out_shape=[shape for _, shape in outs],
        in_specs=[spec for spec, _ in args],
        out_specs=[spec for spec, _ in outs],
        scratch_shapes=scratch,
        compiler_params=pltpu.CompilerParams(vmem_limit_bytes=mib * 2**20),
        cost_estimate=pl.CostEstimate(
            flops=flops, bytes_accessed=2**16, transcendentals=0
        ),
    )(*[arg for _, arg in args])


def pack_kernel(
    feats_hbm, cot_hbm, frac_hbm, weight_hbm, count_hbm, halo_hbm, payload_hbm, feats, cot, frac, weight, count, halo, payload, rows, sems
):
    pairs = (
        (frac_hbm, frac),
        (feats_hbm, feats),
        (weight_hbm, weight),
        (cot_hbm, cot),
        (count_hbm, count),
    )
    copies = [
        pltpu.make_async_copy(src, dst, sems.at[n]) for n, (src, dst) in enumerate(pairs)
    ]
    for copy in copies:
        copy.start()
    copies[0].wait()
    rows[...] = jnp.zeros((16, ROWS), F32)
    for d in range(3):
        first = jnp.floor(frac[d] * 256.0) * (1.0 / 256.0)
        rows[d : d + 1, :] = first
        rows[d + 3 : d + 4, :] = frac[d] - first
    copies[4].wait()
    rows[6:7, :] = jnp.broadcast_to((count[...] >> 4).astype(F32), (1, ROWS))
    rows[7:8, :] = jnp.broadcast_to((count[...] & 15).astype(F32), (1, ROWS))
    where = rows[...]
    halo[FRAC_AT:HALO] = where.astype(BF16)
    copies[1].wait()
    halo[0:CH] = feats[0]
    sent = [pltpu.make_async_copy(halo, halo_hbm, sems.at[5])]
    sent[0].start()
    for a in range(SLABS):
        payload[a, 0:COT_AT] = feats[0, a % 4 * QUARTER : (a % 4 + 1) * QUARTER]
    copies[3].wait()
    for a in range(SLABS):
        payload[a, COT_AT:HID_AT] = cot[0, a // 4 * QUARTER : (a // 4 + 1) * QUARTER]
    parts = slice(0, HID_AT), slice(HID_AT, PAY)
    sent += [
        pltpu.make_async_copy(payload.at[:, part], payload_hbm.at[:, part], sems.at[6 + n])
        for n, part in enumerate(parts)
    ]
    sent[1].start()
    copies[2].wait()
    hidden = dot(weight[...], feats[0], TN)
    for a in range(SLABS):
        payload[a, HID_AT:PAY] = jnp.concatenate(
            [hidden[a * MINE : (a + 1) * MINE], where[0:8]], axis=0
        ).astype(BF16)
    sent[2].start()
    for copy in sent:
        copy.wait()


def joined_count(rows):
    wide = rows.astype(F32)
    return 16.0 * wide[6:7] + wide[7:8]


def joined_frac(rows):
    wide = rows.astype(F32)
    return [wide[d : d + 1] + wide[d + 3 : d + 4] for d in range(3)]


ROOT3, ROOT5, ROOT15 = math.sqrt(3.0), math.sqrt(5.0), math.sqrt(15.0)
STEP = 1.75 / (NB - 1)
BAND = 16
EDGE_COST = 10**10


def edge_kernel(
    own,
    first_swap,
    second_swap,
    neighbours,
    images,
    count,
    in_weight,
    radial_weight,
    out_weight,
    cot,
    early,
    local,
    ext,
    hot,
    weights,
    basis,
    radial,
    moved,
    shape_w,
    length,
    feats9,
    up9,
    pulled,
    inv,
):
    slab = lax.axis_index("atom")
    first = slab * ROWS
    atoms = joined_count(own[FRAC_AT:HALO]).astype(I32)
    live_here = atoms - first
    live_left = atoms - ((first - ROWS) & (ATOMS - 1))
    live_right = atoms - ((first + ROWS) & (ATOMS - 1))
    lane = lax.broadcasted_iota(I32, (CH, ROWS), 1)
    ext[:, 0:ROWS] = jnp.where(lane < live_here, own[0:CH].astype(F32), 0.0).astype(BF16)
    even = (slab & 1) == 0
    swaps = first_swap[...].astype(F32), second_swap[...].astype(F32)
    right = jnp.where(even, swaps[0], swaps[1])
    left = jnp.where(even, swaps[1], swaps[0])
    near_right = jnp.where(lane < live_right, right[0:CH], 0.0)
    near_left = jnp.where(lane < live_left, left[0:CH], 0.0)
    ext[:, ROWS : 2 * ROWS] = jnp.where(lane < GHOST, near_right, near_left).astype(BF16)
    hidden = dot(in_weight[...], ext[...], TN).astype(BF16)

    offset = (neighbours[0] - first) & (ATOMS - 1)
    column = jnp.where(offset < ROWS + GHOST, offset, offset - (ATOMS - 2 * ROWS))
    at = column & (ROWS - 1)
    in_slab = column < ROWS
    frac_own = joined_frac(own[FRAC_AT:HALO])
    frac_left = joined_frac(left[FRAC_AT:HALO])
    frac_right = joined_frac(right[FRAC_AT:HALO])
    lane1 = lax.broadcasted_iota(I32, (1, ROWS), 1)

    code = images[0]
    ninth = (code * 57) >> 9
    third = (code * 171) >> 9
    shifts = (ninth, third - 3 * ninth, code - 3 * third)
    vector = []
    for d in range(3):
        near = jnp.broadcast_to(frac_own[d], (SLOTS, ROWS))
        far = jnp.where(lane1 < GHOST, frac_right[d], frac_left[d])
        far = jnp.broadcast_to(far, (SLOTS, ROWS))
        other = jnp.where(
            in_slab,
            jnp.take_along_axis(near, at, axis=1),
            jnp.take_along_axis(far, at, axis=1),
        )
        vector.append(0.5 * (other - near + (shifts[d].astype(F32) - 1.0)))
    x, y, z = vector
    square = x * x + y * y + z * z
    slot = lax.broadcasted_iota(I32, (SLOTS, ROWS), 0)
    lane32 = lax.broadcasted_iota(I32, (SLOTS, ROWS), 1)
    used = (slot < count[...]) & (lane32 < live_here)
    column = jnp.where(used, column, -1)
    harmonics = (
        ROOT3 * x,
        ROOT3 * y,
        ROOT3 * z,
        ROOT15 * x * y,
        ROOT15 * y * z,
        0.5 * ROOT5 * (3.0 * z * z - square),
        ROOT15 * x * z,
        0.5 * ROOT15 * (x * x - y * y),
    )
    for m in range(8):
        shape_w[m] = harmonics[m]
    length[...] = jnp.sqrt(square)

    rows256 = lax.broadcasted_iota(I32, (2 * ROWS, ROWS), 0)
    centre = lax.broadcasted_iota(I32, (NB, ROWS), 0).astype(F32) * STEP
    basis[24:32, :] = jnp.zeros((8, EDGES), F32)
    for e in range(SLOTS):
        here = slice(e * ROWS, (e + 1) * ROWS)
        hot[:, here] = jnp.where(rows256 == column[e : e + 1], 1.0, 0.0).astype(BF16)
        gap = (length[e : e + 1, :] - centre) * (1.0 / STEP)
        gauss = jnp.exp(-(gap * gap))
        hi, lo = split(gauss)
        basis[0:8, here] = hi.astype(F32)
        basis[8:16, here] = lo.astype(F32)
        basis[16:24, here] = hi.astype(F32)
    weights[...] = jnp.zeros((32, 3 * CH), F32)
    for l in range(3):
        hi, lo = split(radial_weight[l] * SLOTS**-0.5)
        part = slice(l * CH, (l + 1) * CH)
        weights[0:8, part] = hi.astype(F32)
        weights[8:16, part] = hi.astype(F32)
        weights[16:24, part] = lo.astype(F32)
    radial[...] = dot(weights[...].astype(BF16), basis[...].astype(BF16), TN)
    moved[...] = dot(hidden, hot[...], NN)

    def forward(step, carry):
        top = pl.multiple_of(step * BAND, BAND)
        total = [jnp.zeros((BAND, ROWS), F32) for _ in range(9)]
        for e in range(SLOTS):
            here = slice(e * ROWS, (e + 1) * ROWS)
            value = moved[pl.ds(top, BAND), here]
            parts = [
                radial[pl.ds(pl.multiple_of(l * CH + top, BAND), BAND), here] * value
                for l in range(3)
            ]
            total[0] = total[0] + parts[0]
            for m in range(1, 9):
                l = 1 if m < 4 else 2
                total[m] = total[m] + shape_w[m - 1, e : e + 1, :] * parts[l]
        for m in range(9):
            feats9[m, pl.ds(top, BAND), :] = total[m]
        squares = [t * t for t in total]
        inv[pl.ds(top, BAND), :] = squares[0].astype(BF16)
        inv[pl.ds(pl.multiple_of(CH + top, BAND), BAND), :] = (
            squares[1] + squares[2] + squares[3]
        ).astype(BF16)
        inv[pl.ds(pl.multiple_of(2 * CH + top, BAND), BAND), :] = (
            squares[4] + squares[5] + squares[6] + squares[7] + squares[8]
        ).astype(BF16)
        return carry

    lax.fori_loop(0, CH // BAND, forward, 0, unroll=2)

    masked = jnp.where(lane < live_here, cot[0].astype(F32), 0.0).astype(BF16)
    local[...] = dot(out_weight[...], inv[...], TN)
    up9[...] = 2.0 * dot(out_weight[...], masked, NN)
    grad_out = dot(inv[...], masked, NT)
    for d in range(4, STRUCTS):
        to = d * SLOTS
        early[to : to + SLOTS, :] = grad_out[(d - 4) * SLOTS : (d - 3) * SLOTS]

    def backward(step, carry):
        top = pl.multiple_of(step * BAND, BAND)
        up = [
            up9[pl.ds(pl.multiple_of(l * CH + top, BAND), BAND), :] for l in range(3)
        ]
        upstream = []
        for m in range(9):
            l = 0 if m == 0 else (1 if m < 4 else 2)
            upstream.append(feats9[m, pl.ds(top, BAND), :] * up[l])
        for e in range(SLOTS):
            here = slice(e * ROWS, (e + 1) * ROWS)
            term = [upstream[0]] + [
                shape_w[m - 1, e : e + 1, :] * upstream[m] for m in range(1, 9)
            ]
            pull = (
                radial[pl.ds(top, BAND), here] * term[0]
                + radial[pl.ds(pl.multiple_of(CH + top, BAND), BAND), here]
                * (term[1] + term[2] + term[3])
                + radial[pl.ds(pl.multiple_of(2 * CH + top, BAND), BAND), here]
                * (term[4] + term[5] + term[6] + term[7] + term[8])
            )
            pulled[pl.ds(top, BAND), here] = pull.astype(BF16)
        return carry

    lax.fori_loop(0, CH // BAND, backward, 0, unroll=2)
    back = dot(pulled[...], hot[...], NT)
    grad_in = dot(ext[...], back.astype(BF16), NT)
    for d in range(4):
        to = d * SLOTS
        early[to : to + SLOTS, :] = grad_in[d * SLOTS : (d + 1) * SLOTS]


def half_point(miller):
    m0, m1, m2 = miller[0:1], miller[1:2], miller[2:3]
    sign = jnp.where(m0 < 0, -1, 1)
    m0, m1, m2 = sign * m0, sign * m1, sign * m2
    minus = m1 < 0
    turn = jnp.where(minus, -1, 1)
    plane = m0 + jnp.where(minus, TOP + 1, 0)
    return plane, turn * m1 * SIDE + (turn * m2 + TOP)


def one_hot(point):
    row = lax.broadcasted_iota(I32, (PLANE, KVEC), 0)
    return jnp.where(row == point, 1.0, 0.0).astype(BF16)


def turns(frac_row, first, count):
    width = frac_row.shape[1]
    m = (lax.broadcasted_iota(I32, (count, width), 0) + first).astype(F32)
    turn = m * frac_row
    turn = turn - jnp.floor(turn + 0.5)
    quarter = jnp.floor(turn * 4.0 + 0.5)
    arc = (turn - 0.25 * quarter) * (2.0 * math.pi)
    s2 = arc * arc
    sine = arc * (1.0 + s2 * (-1 / 6 + s2 * (1 / 120 + s2 * (-1 / 5040))))
    cosine = 1.0 + s2 * (-0.5 + s2 * (1 / 24 + s2 * (-1 / 720 + s2 * (1 / 40320))))
    odd = jnp.abs(quarter) == 1.0
    back = jnp.abs(quarter) == 2.0
    flip = jnp.where(quarter < 0.0, -1.0, 1.0)
    cos_out = jnp.where(odd, -flip * sine, jnp.where(back, -cosine, cosine))
    sin_out = jnp.where(odd, flip * cosine, jnp.where(back, -sine, sine))
    return cos_out, sin_out


def waves(frac, plane):
    width = plane.shape[1]
    c1, s1 = turns(frac[1], 0, 8)
    c2, s2 = turns(frac[2], -TOP, 16)
    for k in (0, PLANE):
        plane[k + 88 : k + PLANE, :] = jnp.zeros((PLANE - 88, width), F32)
    for m in range(TOP + 1):
        cm, sm = c1[m : m + 1], s1[m : m + 1]
        plane[m * SIDE : m * SIDE + 16, :] = cm * c2 - sm * s2
        plane[PLANE + m * SIDE : PLANE + m * SIDE + 16, :] = sm * c2 + cm * s2
    c0, s0 = turns(frac[0], 0, 8)
    return [c0[m : m + 1] for m in range(TOP + 1)] + [
        s0[m : m + 1] for m in range(1, TOP + 1)
    ]


def lattice_kernel(miller, filter_weight, folded, turned, wide):
    plane, point = half_point(miller[...])
    turned[...] = filter_weight[...].T * (1.0 / math.sqrt(KVEC * ATOMS))
    quarter = lax.axis_index("atom") >> 2
    mine = turned[pl.ds(pl.multiple_of(quarter * QUARTER, QUARTER), QUARTER), :]
    for b in range(2 * (TOP + 1)):
        here = slice(b * QUARTER, (b + 1) * QUARTER)
        wide[here, :] = jnp.where(plane == b, mine, 0.0).astype(BF16)
    sums = dot(wide[...], one_hot(point), NT)
    half = (TOP + 1) * QUARTER
    for m in range(TOP + 1):
        here = slice(m * QUARTER, (m + 1) * QUARTER)
        there = slice(half + m * QUARTER, half + (m + 1) * QUARTER)
        lanes = slice(m * PLANE, (m + 1) * PLANE)
        folded[0:QUARTER, lanes] = sums[here] + sums[there]
        folded[QUARTER : 2 * QUARTER, lanes] = sums[here] - sums[there]


def by_lane_group(pieces):
    group = lax.broadcasted_iota(I32, pieces[0].shape, 1) // 8
    for bit in (1, 2, 4, 8):
        low = group & bit == 0
        pieces = [
            jnp.where(low, piece, pltpu.roll(pieces[n + bit], 8 * bit, 1))
            if n & bit == 0
            else jnp.where(low, pltpu.roll(pieces[n - bit], CH - 8 * bit, 1), piece)
            for n, piece in enumerate(pieces)
        ]
    return pieces


def blocks(x, m):
    at = 2 * m * PLANE
    cc, cs = x[:, at : at + PLANE], x[:, at + PLANE : at + 2 * PLANE]
    if m == 0:
        return cc, None, None, cs
    at = 2 * (TOP + m) * PLANE
    sc, ss = x[:, at : at + PLANE], x[:, at + PLANE : at + 2 * PLANE]
    return cc, ss, sc, cs


def filtered(plus, minus, x):
    first, second = [], []
    for m in range(TOP + 1):
        here = slice(m * PLANE, (m + 1) * PLANE)
        p, d = plus[:, here], minus[:, here]
        cc, ss, sc, cs = blocks(x, m)
        if m == 0:
            first += [p * cc, p * cs]
        else:
            first += [p * cc - d * ss, p * cs + d * sc]
            second += [p * sc + d * cs, p * ss - d * cc]
    return first + second


def spectrum_kernel(
    gathered, folded, miller, early, parts, ewald, factor, frac, values, plane, wide
):
    for p in range(SLABS):
        here = slice(p * ROWS, (p + 1) * ROWS)
        values[:, here] = gathered[p]
        tail = gathered[p, HID_AT:PAY].astype(F32)
        frac[0:3, here] = tail[MINE : MINE + 3] + tail[MINE + 3 : MINE + 6]
    along = waves([frac[d : d + 1, :] for d in range(3)], plane)
    atoms = joined_count(gathered[0, HID_AT:PAY].astype(F32)[MINE:16]).astype(I32)
    live = lax.broadcasted_iota(I32, (1, ATOMS), 1) < atoms[:, 0:1]
    live = jnp.where(live, 1.0, 0.0)
    around = plane[...].astype(BF16)
    for low, high in ((0, TOP + 1), (TOP + 1, WAVES)):
        for f in range(low, high):
            wide[f * PAY : (f + 1) * PAY, :] = (
                values[...].astype(F32) * (along[f] * live)
            ).astype(BF16)
        both = dot(wide[low * PAY : high * PAY, :], around, NT)
        for f in range(low, high):
            here = slice(f * 2 * PLANE, (f + 1) * 2 * PLANE)
            factor[:, here] = both[(f - low) * PAY : (f - low + 1) * PAY]

    at = pl.multiple_of((lax.axis_index("atom") & 3) * MINE, MINE)
    s = factor[HID_AT : HID_AT + MINE, :]
    g = factor[pl.ds(pl.multiple_of(COT_AT + at, MINE), MINE), :]
    plus = folded[pl.ds(at, MINE), :]
    minus = folded[pl.ds(pl.multiple_of(QUARTER + at, MINE), MINE), :]
    pair_plus, pair_minus = [], []
    for m in range(TOP + 1):
        cc, ss, sc, cs = blocks(s, m)
        gcc, gss, gsc, gcs = blocks(g, m)
        even, odd = cc * gcc + cs * gcs, 0.0
        if m > 0:
            even = even + ss * gss + sc * gsc
            odd = sc * gcs + cs * gsc - cc * gss - ss * gcc
        pair_plus.append(even + odd)
        pair_minus.append(even - odd)
    pair = jnp.concatenate(pair_plus + pair_minus, axis=0)
    pair = split(pair * (1.0 / math.sqrt(KVEC * ATOMS)))
    around_plane, point = half_point(miller[...])
    found = dot(jnp.concatenate(pair, axis=0), one_hot(point), NN)
    planes = 2 * (TOP + 1)
    pair = jnp.zeros((MINE, KVEC), F32)
    for b in range(planes):
        value = found[b * MINE : (b + 1) * MINE] + found[(planes + b) * MINE : (planes + b + 1) * MINE]
        pair = jnp.where(around_plane == b, value, pair)
    pair = by_lane_group([pair[:, d * ROWS : (d + 1) * ROWS] for d in range(SLABS)])
    grad = filtered(
        folded[0:QUARTER, :],
        folded[QUARTER : 2 * QUARTER, :],
        factor[COT_AT:HID_AT, :],
    )
    grad = jnp.concatenate(split(jnp.concatenate(grad, axis=1)), axis=0)
    block = dot(grad, factor[0:QUARTER, :].astype(BF16), NT)
    block = block[0:QUARTER] + block[QUARTER : 2 * QUARTER]
    block = jnp.concatenate([block[8 * q : 8 * q + 8] for q in range(4)], axis=1)
    for d in range(STRUCTS):
        parts[d, 0:16, :] = jnp.concatenate(
            [pair[d], block], axis=0
        ).astype(BF16)
        parts[d, 16:48, :] = early[d * SLOTS : (d + 1) * SLOTS, :].astype(BF16)
    coef = filtered(plus, minus, s)
    coef = [
        jnp.concatenate([coef[2 * f], coef[2 * f + 1]], axis=1) for f in range(WAVES)
    ]
    field = dot(jnp.concatenate(coef, axis=0).astype(BF16), around, NN)
    total = field[0:MINE] * along[0]
    for f in range(1, WAVES):
        total = total + field[f * MINE : (f + 1) * MINE] * along[f]
    for p in range(SLABS):
        ewald[p] = total[:, p * ROWS : (p + 1) * ROWS]


SPECTRUM_SCRATCH = [
    pltpu.VMEM((PAY, BASIS), F32),
    pltpu.VMEM((8, ATOMS), F32),
    pltpu.VMEM((PAY, ATOMS), BF16),
    pltpu.VMEM((2 * PLANE, ATOMS), F32),
    pltpu.VMEM((WAVES * PAY, ATOMS), BF16),
]


def turn_kernel(sums, ewald, out):
    total = sums[0].astype(F32)
    for d in range(1, STRUCTS):
        total = total + sums[d].astype(F32)
    lane = lax.broadcasted_iota(I32, (MINE, CH), 1)
    share = pltpu.roll(total[8:16], (8 - 8 * lax.axis_index("dp")) & (CH - 1), 1)
    for p in range(SLABS):
        picked = pltpu.roll(total[0:8], (CH - 8 * p) % CH, 1)
        out[p] = jnp.concatenate(
            [total[16:48], jnp.where(lane < 8, picked, share), ewald[p]], axis=0
        ).astype(BF16)


def middle_kernel(sums, own, local, last, field):
    row = lax.broadcasted_iota(I32, (8, CH), 0)
    lane = lax.broadcasted_iota(I32, (8, CH), 1)
    pick = jnp.where(lane == row, 1.0, 0.0).astype(BF16)
    blocks = [sums[p].astype(F32) for p in range(SLABS)]
    pairs = jnp.concatenate([block[32:40] for block in blocks], axis=0)
    picked = dot(pick, pairs.astype(BF16), NT)
    total, share = blocks[0][0:32], jnp.zeros((8, CH), F32)
    for block in blocks[1:]:
        total = total + block[0:32]
    for p, block in enumerate(blocks):
        turned = pltpu.roll(block[32:40], (8 * p - 8) % CH, 1)
        share = jnp.where(lane >> 3 == p, turned, share)
    out = jnp.concatenate([total, picked, share], axis=0).astype(BF16)
    for d in range(STRUCTS):
        last[d] = out
    ewald = jnp.concatenate([block[40:48] for block in blocks], axis=0)
    live = joined_count(own[FRAC_AT:HALO]).astype(I32) - lax.axis_index("atom") * ROWS
    live = lax.broadcasted_iota(I32, (CH, ROWS), 1) < live
    field[...] = jnp.where(live, own[0:CH].astype(F32) + local[...] + ewald, 0.0)


def finish_kernel(sums, field, updated, grad_filter, grad_in, grad_out):
    updated[0] = field[...].astype(BF16)
    lane8 = lax.broadcasted_iota(I32, (8, CH), 1)
    heads = [sums[d, 32:48].astype(F32) for d in range(STRUCTS)]
    for d in range(STRUCTS):
        grad_filter[8 * d : 8 * d + 8, :] = heads[d][0:8]
    grads = []
    for c in range(0, CH, 8):
        g, q = c // QUARTER, c % QUARTER // 8
        eight = pltpu.roll(heads[4 * q][8:16], (0 - g) * QUARTER % CH, 1)
        for u in range(1, 4):
            turned = pltpu.roll(heads[4 * q + u][8:16], (u - g) * QUARTER % CH, 1)
            eight = jnp.where(lane8 < u * QUARTER, eight, turned)
        grads.append(eight)
    row = lax.broadcasted_iota(I32, (CH, CH), 0)
    lane = lax.broadcasted_iota(I32, (CH, CH), 1)
    channel = 32 * ((lane >> 3) & 3) + 8 * (lane >> 5) + (lane & 7)
    order = jnp.where(row == channel, 1.0, 0.0).astype(BF16)
    ewald_in = dot(order, jnp.concatenate(grads, axis=0).astype(BF16), NT)
    for d in range(4):
        here = slice(d * SLOTS, (d + 1) * SLOTS)
        grad_in[here, :] = ewald_in[here] + sums[d, 0:32].astype(F32)
    for d in range(4, STRUCTS):
        grad_out[(d - 4) * SLOTS : (d - 3) * SLOTS, :] = sums[d, 0:32].astype(F32)


def exchange(x, axis):
    return lax.all_to_all(x, axis, 0, 0)


def shards(
    node_feats,
    frac,
    neighbours,
    images,
    neighbour_count,
    atom_count,
    miller,
    in_weight,
    radial_weight,
    out_weight,
    filter_weight,
    cotangent,
):
    struct = jax.ShapeDtypeStruct

    halo, payload = call(
        pack_kernel,
        [
            (HBM, struct((HALO, ROWS), BF16)),
            (HBM, struct((SLABS, PAY, ROWS), BF16)),
        ],
        [
            pltpu.VMEM((1, CH, ROWS), BF16),
            pltpu.VMEM((1, CH, ROWS), BF16),
            pltpu.VMEM((3, 1, ROWS), F32),
            pltpu.VMEM((CH, CH), BF16),
            pltpu.VMEM((1, 1), I32),
            pltpu.VMEM((HALO, ROWS), BF16),
            pltpu.VMEM((SLABS, PAY, ROWS), BF16),
            pltpu.VMEM((16, ROWS), F32),
            pltpu.SemaphoreType.DMA((8,)),
        ],
        60,
        10**6,
        (HBM, node_feats),
        (HBM, cotangent),
        (HBM, frac.transpose(1, 0, 2)),
        (HBM, in_weight),
        (HBM, atom_count.reshape(1, 1)),
    )
    evens = range(0, SLABS, 2)
    pairs = [(n, n + 1) for n in evens], [(n + 1, (n + 2) % SLABS) for n in evens]
    first_swap, second_swap = (
        lax.ppermute(halo, "atom", [*pair, *((j, i) for i, j in pair)]) for pair in pairs
    )
    gathered = exchange(payload, "atom")

    early, local = call(
        edge_kernel,
        [(VMEM, struct((4 * CH, CH), F32)), (VMEM, struct((CH, ROWS), F32))],
        [
            pltpu.VMEM((CH, 2 * ROWS), BF16),
            pltpu.VMEM((2 * ROWS, EDGES), BF16),
            pltpu.VMEM((32, 3 * CH), F32),
            pltpu.VMEM((32, EDGES), F32),
            pltpu.VMEM((3 * CH, EDGES), F32),
            pltpu.VMEM((CH, EDGES), F32),
            pltpu.VMEM((8, SLOTS, ROWS), F32),
            pltpu.VMEM((SLOTS, ROWS), F32),
            pltpu.VMEM((9, CH, ROWS), F32),
            pltpu.VMEM((3 * CH, ROWS), F32),
            pltpu.VMEM((CH, EDGES), BF16),
            pltpu.VMEM((3 * CH, ROWS), BF16),
        ],
        20,
        EDGE_COST,
        (VMEM, halo),
        (VMEM, first_swap),
        (VMEM, second_swap),
        (VMEM, neighbours),
        (VMEM, images),
        (VMEM, neighbour_count),
        (VMEM, in_weight),
        (VMEM, radial_weight),
        (VMEM, out_weight),
        (VMEM, cotangent),
    )
    early, miller = lax.optimization_barrier((early, miller))
    (folded,) = call(
        lattice_kernel,
        [(VMEM, struct((2 * QUARTER, HALF), F32))],
        [
            pltpu.VMEM((CH, KVEC), F32),
            pltpu.VMEM((2 * (TOP + 1) * QUARTER, KVEC), BF16),
        ],
        12,
        10**8,
        (VMEM, miller),
        (VMEM, filter_weight),
    )
    parts, ewald = call(
        spectrum_kernel,
        [
            (VMEM, struct((STRUCTS, 48, CH), BF16)),
            (VMEM, struct((SLABS, MINE, ROWS), F32)),
        ],
        SPECTRUM_SCRATCH,
        20,
        10**10,
        (VMEM, gathered),
        (VMEM, folded),
        (VMEM, miller),
        (VMEM, early),
    )
    (sums,) = call(
        turn_kernel,
        [(VMEM, struct((SLABS, 48, CH), BF16))],
        [],
        16,
        10**6,
        (VMEM, exchange(parts, "dp")),
        (VMEM, ewald),
    )
    last, field = call(
        middle_kernel,
        [
            (VMEM, struct((STRUCTS, 48, CH), BF16)),
            (VMEM, struct((CH, ROWS), F32)),
        ],
        [],
        16,
        10**6,
        (VMEM, exchange(sums, "atom")),
        (VMEM, halo),
        (VMEM, local),
    )
    return tuple(
        call(
            finish_kernel,
            [
                (VMEM, struct((1, CH, ROWS), BF16)),
                (VMEM, struct((KSHARE, CH), F32)),
                (VMEM, struct((CH, CH), F32)),
                (VMEM, struct((3 * CH, CH), F32)),
            ],
            [],
            16,
            10**6,
            (VMEM, exchange(last, "dp")),
            (VMEM, field),
        )
    )


def solution(mesh):
    return jax.shard_map(
        shards,
        mesh=mesh,
        in_specs=(
            P("dp", None, "atom"),
            P("dp", None, "atom"),
            P("dp", None, "atom"),
            P("dp", None, "atom"),
            P("dp", "atom"),
            P("dp"),
            P(),
            P(),
            P(),
            P(),
            P(),
            P("dp", None, "atom"),
        ),
        out_specs=(P("dp", None, "atom"), P("atom", None), P(), P()),
        check_vma=False,
    )
```
